256 devices in a mesh: ctx: 16 (over x, y), exp: 16 (over z, core).
Axes of the slice: x: 4, y: 4, z: 8, core: 2. Of those that a mesh axis runs over, the one named last changes fastest.
Arguments:
- u_in: bfloat16 [4096, 8192], P('ctx', 'exp'), may hold values from -6 to 6
- z_gate: bfloat16 [4096, 8192], P('ctx', 'exp'), may hold values from -6 to 6
- delta: float32 [4096, 8192], P('ctx', 'exp'), may hold values from 0.125 to 8, as said below
- b_in: float32 [4096, 16], P('ctx'), may hold values from -1.5 to 1.5
- c_in: float32 [4096, 16], P('ctx'), may hold values from -1.5 to 1.5
- rate: float32 [16, 8192], P(None, 'exp'), may hold values from 0.00024414062 to 0.05
- skip: float32 [8192], P('exp'), may hold values from 0.5 to 1.5
- w_out: bfloat16 [8192, 2048], P('exp'), may hold values from -0.015625 to 0.015625
- resid: bfloat16 [4096, 2048], P(('ctx', 'exp')), may hold values from -6 to 6
- gain: float32 [2048], replicated, may hold values from 0.5 to 1.5
- expert_ids: int32 [4096, 2], P(('ctx', 'exp')), may hold values from 0 to 15, all different within a row; in each aligned block of 16 rows (0 to 15, 16 to 31, ...) at most 4 rows name the same one
- route_weights: float32 [4096, 2], P(('ctx', 'exp')), may hold values from 0.2 to 1
- w_gate: bfloat16 [16, 2048, 8192], P('exp', None, 'ctx'), may hold values from -0.125 to 0.125
- w_up: bfloat16 [16, 2048, 8192], P('exp', None, 'ctx'), may hold values from -0.125 to 0.125
- w_down: bfloat16 [16, 8192, 2048], P('exp', 'ctx'), may hold values from -0.0625 to 0.0625
- d_out: bfloat16 [4096, 2048], P(('ctx', 'exp')), may hold values from -6 to 6
Outputs:
- final: bfloat16 [4096, 2048], P(('ctx', 'exp'))
- grad_resid: bfloat16 [4096, 2048], P(('ctx', 'exp'))
- grad_u: bfloat16 [4096, 8192], P('ctx', 'exp')
The draws below stay inside these ranges and needn't reach their ends.
Inputs may be any that keep to these rules, and one draw needn't show every extreme that they name: `expert_ids`: in each aligned block of 16 rows (the rows of one device) no expert is named by more than 4 rows, a bound that some block reaches; the two ids of a row differ. `delta`: positive step sizes.
All inputs are finite; a program needn't handle non-finite values.
Results may differ from the reference program's by a relative error of at most 0.025.
Values may be sent and summed in bfloat16 or wider, within the bound.
A program may use at most 128 MiB of HBM per device.

```python
import math
import jax
import jax.numpy as jnp
import numpy as np
from jax import lax

D = 2048
FF = 8192
DI = 8192
STATE = 16
MR = 16
SEG = 256
L = 4096
EXPERTS = 16
CAP = 4
FFB = 512
N_CTX = 16


def draw_delta(key, part):
    key = jax.random.fold_in(key, 7)
    segment_key, channel_key, order_key, element_key = jax.random.split(key, 4)
    segment_count = L // SEG
    segment_multiplier = jnp.exp(jax.random.uniform(segment_key, (segment_count, 1, 1), jnp.float32, math.log(0.25), math.log(4.0)))
    channel_multiplier = jnp.exp(jax.random.uniform(channel_key, (segment_count, 1, DI), jnp.float32, math.log(0.5), math.log(2.0)))
    sort_permutation = jax.random.randint(order_key, (segment_count, 1, DI), 0, 2)
    latter_portion = (jnp.arange(SEG, dtype=jnp.int32)[None, :, None] >= SEG // 2).astype(jnp.int32)
    spike_amount = jnp.where(latter_portion == sort_permutation, 2.0, 0.5).astype(jnp.float32)
    element_multiplier = jnp.exp(jax.random.uniform(element_key, (segment_count, SEG, DI), jnp.float32, math.log(0.7), math.log(1.4)))
    value_entry = jnp.clip(segment_multiplier * channel_multiplier * spike_amount * element_multiplier, 0.125, 8.0)
    return value_entry.reshape(L, DI).astype(jnp.float32)


def block_scale(stream_key, dims, cuts, low, high):
    level = 1.0
    for dim, parts in cuts:
        heights = jax.random.uniform(jax.random.fold_in(jax.random.fold_in(stream_key, 6), dim), (parts,), jnp.float32, low / len(cuts), high / len(cuts))
        level = level * jnp.repeat(jnp.exp(heights), dims[dim] // parts).reshape((-1,) + (1,) * (len(dims) - 1 - dim))
    return level


def shared_out(rng, own, number, rows, amount, top, bound, lean):
    sequence = jax.random.permutation(rng, amount)
    heavy_load, common = load_shares(amount, rows * top, bound, lean, True), load_shares(amount, rows * top, bound, lean, False)
    places = jnp.arange(amount)

    def named(lengths, offset_by):
        used = int((lengths > 0).sum())
        fixed = max(1, used // 4)
        passed = fixed + (places - fixed + offset_by * (used - fixed)) % max(1, amount - fixed)
        return jnp.zeros((amount,), jnp.int32).at[sequence[jnp.where(places < fixed, places, passed)]].set(jnp.asarray(lengths, jnp.int32))

    lengths = jnp.where(number % 4 == 0, named(heavy_load, number // 4), named(common, number - number // 4 - 1))
    mixed = jax.random.permutation(jax.random.fold_in(own, 3), amount)
    donor, receiver = mixed[0:amount // 2 * 2:2], mixed[1:amount // 2 * 2:2]
    margin = jnp.minimum(lengths[donor] - 1, bound - lengths[receiver]) // 2
    margin = jnp.where((donor == sequence[0]) | (receiver == sequence[0]) | (lengths[receiver] == 0), 0, jnp.maximum(margin, 0))
    passed = jax.random.randint(jax.random.fold_in(own, 4), (amount // 2,), 0, 1 << 20) % (margin + 1)
    lengths = lengths.at[donor].add(-passed).at[receiver].add(passed)
    members = jnp.searchsorted(jnp.cumsum(lengths), jnp.arange(rows * top), side="right").astype(jnp.int32)
    grid = members.reshape(top, rows).T
    grid = grid[jax.random.permutation(jax.random.fold_in(own, 1), rows)]
    offset_by = jax.random.randint(jax.random.fold_in(own, 2), (rows, 1), 0, top)
    return jnp.take_along_axis(grid, (jnp.arange(top)[None, :] + offset_by) % top, axis=1)


def load_shares(number_of, total, most, skew, full):
    weights = [(1 << 20) // math.isqrt(grade ** skew) + 1 for grade in range(1, number_of + 1)]
    largest = most if full else min(most, max(-(-total // number_of), total * weights[0] // sum(weights)))
    least = 1 if total - largest >= number_of - 1 else 0
    holding, spare = [largest] + [least] * (number_of - 1), total - largest - least * (number_of - 1)
    while spare > 0:
        candidates = [i for i in range(1, number_of) if holding[i] < largest] or [i for i in range(1, number_of) if holding[i] < most]
        mass, left = sum([weights[i] for i in candidates]), spare
        for i in candidates:
            extra = min(most - holding[i], max(1, left * weights[i] // mass), spare)
            holding[i] = holding[i] + extra
            spare = spare - extra
    return np.array(holding)


def scatter_about(stream_key, extent, spread, reach, cuts=(), kind=jnp.bfloat16):
    entries = jax.random.normal(stream_key, extent, jnp.float32) * spread
    if len(cuts) > 0:
        entries = block_scale(stream_key, extent, cuts, -0.22, 0.18) * entries
    return jnp.clip(entries, min=-reach, max=reach).astype(kind)


def setup_inputs(seed: int = 0) -> dict:
    keys = jax.random.split(jax.random.key(seed), 17)
    u_in = scatter_about(keys[0], (L, DI), 1.0, 6.0, ((0, 16), (1, 16)))
    z_gate = scatter_about(keys[1], (L, DI), 1.0, 6.0, ((0, 16), (1, 16)))
    delta = draw_delta(jax.random.fold_in(keys[16], 71), 0)
    b_in = scatter_about(keys[3], (L, STATE), 0.25, 1.5, ((0, 16),), jnp.float32)
    c_in = scatter_about(keys[4], (L, STATE), 0.25, 1.5, ((0, 16),), jnp.float32)
    rate = jnp.clip(jnp.exp(math.log(0.05) - 5.322034 * jax.random.uniform(keys[5], (STATE, DI), jnp.float32) ** block_scale(keys[5], (STATE, DI), ((1, 16),), -0.2, 0.2)), 0.00024414062, 0.05)
    skip = jnp.clip(0.5 + 1.0 * jax.random.uniform(keys[6], (DI,), jnp.float32) ** block_scale(keys[6], (DI,), ((0, 16),), -0.2, 0.2), 0.5, 1.5)
    w_out = scatter_about(keys[7], (DI, D), (16 * DI) ** -0.5, 0.015625, ((0, 16),))
    resid = scatter_about(keys[8], (L, D), 1.0, 6.0, ((0, 256),))
    gain = jnp.clip(1.0 + 0.1 * jax.random.normal(keys[9], (D,), jnp.float32), 0.5, 1.5)
    expert_ids_keys = jax.random.split(jax.random.fold_in(keys[10], 1), L // MR)
    expert_ids_turns = jax.random.permutation(jax.random.fold_in(keys[10], 3), L // MR)
    expert_ids = jax.vmap(lambda own, number: shared_out(jax.random.fold_in(keys[10], 2), own, number, MR, EXPERTS, 2, CAP, 2))(expert_ids_keys, expert_ids_turns).reshape((L, 2))
    route_weights = jnp.clip(0.2 + 0.8 * jax.random.uniform(keys[11], (L, 2), jnp.float32) ** block_scale(keys[11], (L, 2), ((0, 256),), -0.2, 0.2), 0.2, 1.0)
    w_gate = scatter_about(keys[12], (EXPERTS, D, FF), D ** -0.5, 0.125, ((0, 16), (2, 16)))
    w_up = scatter_about(keys[13], (EXPERTS, D, FF), D ** -0.5, 0.125, ((0, 16), (2, 16)))
    w_down = scatter_about(keys[14], (EXPERTS, FF, D), FF ** -0.5, 0.0625, ((0, 16), (1, 16)))
    d_out = scatter_about(keys[15], (L, D), 1.0, 6.0, ((0, 256),))
    return dict(u_in=u_in, z_gate=z_gate, delta=delta, b_in=b_in, c_in=c_in, rate=rate, skip=skip, w_out=w_out, resid=resid, gain=gain, expert_ids=expert_ids, route_weights=route_weights, w_gate=w_gate, w_up=w_up, w_down=w_down, d_out=d_out)


def reference(u_in, z_gate, delta, b_in, c_in, rate, skip, w_out, resid, gain, expert_ids, route_weights, w_gate, w_up, w_down, d_out):
    length = u_in.shape[0]
    u_float = u_in.astype(jnp.float32)
    z_float = z_gate.astype(jnp.float32)
    start_state = jnp.zeros(rate.shape, jnp.float32)

    def forward_step(carried, inputs):
        step_size, value_entry, b_row, c_row = inputs
        decay = jnp.exp(-step_size[None, :] * rate)
        carried = decay * carried + b_row[:, None] * (step_size * value_entry)[None, :]
        return (carried, lax.optimization_barrier(jnp.sum(c_row[:, None] * carried, axis=0)))
    _, scanned = lax.scan(forward_step, start_state, (delta, u_float, b_in, c_in))
    scanned = scanned + skip[None, :] * u_float
    z_act = jax.nn.silu(z_float)
    gated = (scanned * z_act).astype(jnp.bfloat16)
    stream = resid.astype(jnp.float32) + jnp.dot(gated, w_out, preferred_element_type=jnp.float32)
    inverse = lax.rsqrt(lax.optimization_barrier(jnp.mean(stream * stream, axis=-1, keepdims=True)) + 1e-05)
    normed = (stream * inverse * gain[None, :]).astype(jnp.bfloat16)
    blocks = length // MR
    owners = expert_ids.reshape(blocks, 2 * MR)
    onehot = (owners[:, :, None] == jnp.arange(EXPERTS, dtype=jnp.int32)[None, None, :]).astype(jnp.int32)
    before = jnp.cumsum(onehot, axis=1) - onehot
    slots = lax.optimization_barrier(jnp.sum(before * onehot, axis=2))
    position = (jnp.arange(blocks, dtype=jnp.int32)[:, None] * CAP + slots).reshape(-1)
    owners = owners.reshape(-1)
    total_slots = blocks * CAP
    table = jnp.zeros((EXPERTS, total_slots), jnp.int32).at[owners, position].set(jnp.arange(2 * length, dtype=jnp.int32))
    filled = jnp.zeros((EXPERTS, total_slots), jnp.float32).at[owners, position].set(1.0)
    paired = jnp.repeat(normed, 2, axis=0)
    weights_flat = route_weights.reshape(-1)
    cotangent = (weights_flat[:, None] * jnp.repeat(d_out.astype(jnp.float32), 2, axis=0)).astype(jnp.bfloat16)

    def expert(inputs):
        index, live, gate_mat, up_mat, down_mat = inputs
        live_cast = live[:, None].astype(jnp.bfloat16)
        inputs_rows = paired[index] * live_cast
        grads_rows = cotangent[index] * live_cast
        gate_pre = jnp.dot(inputs_rows, gate_mat, preferred_element_type=jnp.float32)
        up_pre = jnp.dot(inputs_rows, up_mat, preferred_element_type=jnp.float32)
        sigma = jax.nn.sigmoid(gate_pre)
        active = gate_pre * sigma
        hidden_act = (active * up_pre).astype(jnp.bfloat16)
        rows_count = hidden_act.shape[0]
        hidden_blocks = hidden_act.astype(jnp.float32).reshape(rows_count, N_CTX, FFB)
        down_blocks = down_mat.astype(jnp.float32).reshape(N_CTX, FFB, D)
        down_part = jnp.einsum('rcf,cfd->crd', hidden_blocks, down_blocks).astype(jnp.bfloat16)
        out_rows = lax.optimization_barrier(jnp.sum(down_part.astype(jnp.float32), axis=0)).astype(jnp.bfloat16)
        hidden_grad = jnp.dot(grads_rows, down_mat.T, preferred_element_type=jnp.float32)
        gate_grad = (hidden_grad * up_pre * sigma * (1.0 + gate_pre * (1.0 - sigma))).astype(jnp.bfloat16)
        up_grad = (hidden_grad * active).astype(jnp.bfloat16)
        gate_blocks = gate_grad.astype(jnp.float32).reshape(rows_count, N_CTX, FFB)
        up_blocks = up_grad.astype(jnp.float32).reshape(rows_count, N_CTX, FFB)
        gate_w = gate_mat.astype(jnp.float32).reshape(D, N_CTX, FFB)
        up_w = up_mat.astype(jnp.float32).reshape(D, N_CTX, FFB)
        row_part = (jnp.einsum('rcf,dcf->crd', gate_blocks, gate_w) + jnp.einsum('rcf,dcf->crd', up_blocks, up_w)).astype(jnp.bfloat16)
        row_grad = lax.optimization_barrier(jnp.sum(row_part.astype(jnp.float32), axis=0)).astype(jnp.bfloat16)
        return (out_rows, row_grad)
    out_rows, grad_rows = lax.map(expert, (table, filled, w_gate, w_up, w_down))
    flat_index = table.reshape(-1)
    live_flat = filled.reshape(-1)[:, None]
    expert_out = jnp.zeros((2 * length, D), jnp.float32).at[flat_index].add(out_rows.reshape(-1, D).astype(jnp.float32) * live_flat)
    row_grad = jnp.zeros((2 * length, D), jnp.float32).at[flat_index].add(grad_rows.reshape(-1, D).astype(jnp.float32) * live_flat)
    expert_out = expert_out.reshape(length, 2, D)
    row_grad = row_grad.reshape(length, 2, D)
    final = (stream + route_weights[:, 0:1] * expert_out[:, 0] + route_weights[:, 1:2] * expert_out[:, 1]).astype(jnp.bfloat16)
    normed_grad = row_grad[:, 0] + row_grad[:, 1]
    scaled = normed_grad * gain[None, :]
    project_mean = lax.optimization_barrier(jnp.mean(scaled * stream, axis=-1, keepdims=True))
    stream_grad = inverse * (scaled - stream * inverse * inverse * project_mean)
    grad_resid = (d_out.astype(jnp.float32) + stream_grad).astype(jnp.bfloat16)
    out_grad = jnp.dot(grad_resid, w_out.T, preferred_element_type=jnp.float32) * z_act

    def backward_step(carried, inputs):
        step_size, grad_value, b_row, c_row = inputs
        adjoint = c_row[:, None] * grad_value[None, :] + carried
        decay = jnp.exp(-step_size[None, :] * rate)
        return (decay * adjoint, lax.optimization_barrier(jnp.sum(b_row[:, None] * adjoint, axis=0)) * step_size)
    _, back_terms = lax.scan(backward_step, start_state, (delta, out_grad, b_in, c_in), reverse=True)
    grad_u = (back_terms + skip[None, :] * out_grad).astype(jnp.bfloat16)
    return (final, grad_resid, grad_u)
```

```python
import functools
import math

import jax
import jax.numpy as jnp
from jax import lax
from jax.experimental import pallas as pl
from jax.experimental.pallas import tpu as pltpu
from jax.sharding import PartitionSpec as P

LANES = 128
VMEM = pl.BlockSpec(memory_space=pltpu.VMEM)
PARAMS = pltpu.CompilerParams(vmem_limit_bytes=48 * 1024 * 1024)


def contract_last(left, right):
    return lax.dot_general(
        left, right, (((1,), (1,)), ((), ())), preferred_element_type=jnp.float32
    )


def silu(v):
    return v * (1.0 / (1.0 + jnp.exp(-v)))


def tiles_of(channels):
    return [slice(i * LANES, (i + 1) * LANES) for i in range(channels // LANES)]


GROUP = 8


def scan_tokens(rows, channels, planes, step, initial, out_ref=None, backward=False):
    tiles = tiles_of(channels)
    row_index = lax.broadcasted_iota(jnp.int32, (GROUP, LANES), 0)

    def group(i, carried):
        base = rows - GROUP - i * GROUP if backward else i * GROUP
        base = pl.multiple_of(base, GROUP)
        blocks = [[plane[pl.ds(base, GROUP), tile] for plane in planes] for tile in tiles]
        made = [jnp.zeros((GROUP, LANES), jnp.float32) for _ in tiles]
        carried = list(carried)
        for j in reversed(range(GROUP)) if backward else range(GROUP):
            for k, tile in enumerate(tiles):
                line = [b[j : j + 1] for b in blocks[k]]
                carried[k], row = step(base + j, tile, line, carried[k])
                if out_ref is not None:
                    made[k] = jnp.where(row_index == j, row, made[k])
        if out_ref is not None:
            for k, tile in enumerate(tiles):
                out_ref[pl.ds(base, GROUP), tile] = made[k]
        return tuple(carried)

    return lax.fori_loop(0, rows // GROUP, group, tuple(initial))


def zero_state(rate_ref):
    states, channels = rate_ref.shape
    return [jnp.zeros((states, LANES), jnp.float32) for _ in tiles_of(channels)]


def put_state(ref, done):
    for tile, held in zip(tiles_of(ref.shape[-1]), done):
        ref[:, tile] = held


def take_state(ref):
    return [ref[:, tile] for tile in tiles_of(ref.shape[-1])]


def forward_end(delta_ref, u_ref, brep_ref, rate_ref, end_ref, sum_ref, drive_ref):
    rows, channels = delta_ref.shape
    drive_ref[...] = delta_ref[...] * u_ref[...].astype(jnp.float32)
    sum_ref[...] = jnp.sum(delta_ref[...], axis=0, keepdims=True)

    def step(t, tile, line, held):
        decay = jnp.exp2(line[0] * rate_ref[:, tile])
        return decay * held + brep_ref[t] * line[1], None

    put_state(
        end_ref, scan_tokens(rows, channels, (delta_ref, drive_ref), step, zero_state(rate_ref))
    )


def forward_out(
    delta_ref, u_ref, brep_ref, crep_ref, rate_ref, start_ref, skip_ref, z_ref, gated_ref, drive_ref, y_ref
):
    rows, channels = delta_ref.shape
    drive_ref[...] = delta_ref[...] * u_ref[...].astype(jnp.float32)

    def step(t, tile, line, held):
        decay = jnp.exp2(line[0] * rate_ref[:, tile])
        new = decay * held + brep_ref[t] * line[1]
        return new, jnp.sum(crep_ref[t] * new, axis=0, keepdims=True)

    scan_tokens(rows, channels, (delta_ref, drive_ref), step, take_state(start_ref), y_ref)
    z = z_ref[...].astype(jnp.float32)
    scanned = y_ref[...] + skip_ref[...] * u_ref[...].astype(jnp.float32)
    gated_ref[...] = (scanned * silu(z)).astype(gated_ref.dtype)


def backward_end(delta_ref, grad_ref, crep_ref, rate_ref, end_ref):
    rows, channels = delta_ref.shape

    def step(t, tile, line, held):
        decay = jnp.exp2(line[0] * rate_ref[:, tile])
        return decay * (held + crep_ref[t] * line[1]), None

    put_state(
        end_ref,
        scan_tokens(
            rows, channels, (delta_ref, grad_ref), step, zero_state(rate_ref), backward=True
        ),
    )


def backward_out(
    delta_ref, grad_ref, brep_ref, crep_ref, rate_ref, start_ref, skip_ref, out_ref, y_ref
):
    rows, channels = delta_ref.shape

    def step(t, tile, line, held):
        decay = jnp.exp2(line[0] * rate_ref[:, tile])
        new = held + crep_ref[t] * line[1]
        return decay * new, jnp.sum(brep_ref[t] * new, axis=0, keepdims=True)

    scan_tokens(
        rows, channels, (delta_ref, grad_ref), step, take_state(start_ref), y_ref, backward=True
    )
    out_ref[...] = (delta_ref[...] * y_ref[...] + skip_ref[...] * grad_ref[...]).astype(
        out_ref.dtype
    )


def local_call(body, outs, scratch, args):
    return pl.pallas_call(
        body,
        out_shape=outs,
        in_specs=[VMEM] * len(args),
        out_specs=[VMEM] * len(outs),
        scratch_shapes=scratch,
        compiler_params=PARAMS,
    )(*args)


SIDE = 4
TO_RIGHT, TO_LEFT, ON_RIGHT, ON_LEFT = 0, 1, 2, 3


class Ring:
    def __init__(self, along_x):
        c = lax.axis_index("ctx")
        x, y = c // SIDE, c % SIDE
        self.place = x if along_x else y
        up, down = (self.place + 1) % SIDE, (self.place + SIDE - 1) % SIDE
        self.after, self.before, self.across = up, down, (self.place + 2) % SIDE
        self.right = {"ctx": up * SIDE + y if along_x else x * SIDE + up}
        self.left = {"ctx": down * SIDE + y if along_x else x * SIDE + down}


def halves(ref):
    n = ref.shape[0] // 2
    return ref.at[pl.ds(0, n)], ref.at[pl.ds(n, n)]


class Gather:
    def __init__(self, ring, block, send, recv):
        self.ring, self.block, self.send, self.recv = ring, block, send, recv

    def copy(self, ref, way):
        target = self.ring.right if way in (TO_RIGHT, ON_RIGHT) else self.ring.left
        return pltpu.make_async_remote_copy(
            src_ref=ref,
            dst_ref=ref,
            send_sem=self.send.at[way],
            recv_sem=self.recv.at[way],
            device_id=target,
            device_id_type=pl.DeviceIdType.MESH,
        )

    def start(self):
        own = self.block(self.ring.place)
        self.copy(own, TO_RIGHT).start()
        self.copy(own, TO_LEFT).start()

    def before(self):
        came = self.block(self.ring.before)
        self.copy(came, TO_RIGHT).wait_recv()
        self.copy(halves(came)[0], ON_RIGHT).start()

    def after(self):
        came = self.block(self.ring.after)
        self.copy(came, TO_LEFT).wait_recv()
        self.copy(halves(came)[1], ON_LEFT).start()

    def across(self):
        first, second = halves(self.block(self.ring.across))
        self.copy(first, ON_RIGHT).wait_recv()
        self.copy(second, ON_LEFT).wait_recv()

    def finish(self):
        own = self.block(self.ring.place)
        self.copy(own, TO_RIGHT).wait_send()
        self.copy(own, TO_LEFT).wait_send()
        self.copy(halves(self.block(self.ring.before))[0], ON_RIGHT).wait_send()
        self.copy(halves(self.block(self.ring.after))[1], ON_LEFT).wait_send()


def add_into(total, term):
    total[...] = (total[...].astype(jnp.float32) + term[...].astype(jnp.float32)).astype(
        total.dtype
    )


class Reduce:
    def __init__(self, ring, part, far, near, send, recv):
        self.ring, self.part, self.far, self.near = ring, part, far, near
        self.send, self.recv = send, recv

    def copy(self, way):
        ring = self.ring
        source = {
            TO_RIGHT: lambda: halves(self.part(ring.across))[0],
            TO_LEFT: lambda: halves(self.part(ring.across))[1],
            ON_RIGHT: lambda: self.part(ring.after),
            ON_LEFT: lambda: self.part(ring.before),
        }[way]()
        target = {
            TO_RIGHT: self.far.at[0],
            TO_LEFT: self.far.at[1],
            ON_RIGHT: self.near.at[0],
            ON_LEFT: self.near.at[1],
        }[way]
        return pltpu.make_async_remote_copy(
            src_ref=source,
            dst_ref=target,
            send_sem=self.send.at[way],
            recv_sem=self.recv.at[way],
            device_id=ring.right if way in (TO_RIGHT, ON_RIGHT) else ring.left,
            device_id_type=pl.DeviceIdType.MESH,
        )

    def start(self):
        self.copy(TO_RIGHT).start()
        self.copy(TO_LEFT).start()

    def middle(self):
        self.copy(TO_RIGHT).wait_recv()
        add_into(halves(self.part(self.ring.after))[0], self.far.at[0])
        self.copy(ON_RIGHT).start()
        self.copy(TO_LEFT).wait_recv()
        add_into(halves(self.part(self.ring.before))[1], self.far.at[1])
        self.copy(ON_LEFT).start()

    def total(self):
        self.copy(ON_RIGHT).wait_recv()
        self.copy(ON_LEFT).wait_recv()
        f32 = jnp.float32
        own = self.part(self.ring.place)
        return (
            own[...].astype(f32) + self.near[0].astype(f32) + self.near[1].astype(f32)
        ).astype(own.dtype)

    def finish(self):
        for way in range(4):
            self.copy(way).wait_send()


def greet(targets):
    barrier = pltpu.get_barrier_semaphore()
    for target in targets:
        pl.semaphore_signal(
            barrier, inc=1, device_id=target, device_id_type=pl.DeviceIdType.MESH
        )
    pl.semaphore_wait(barrier, len(targets))


def experts_kernel(
    rows_ref,
    cots_ref,
    wg_ref,
    wu_ref,
    wd_ref,
    out_ref,
    grad_ref,
    held,
    parts,
    far,
    near,
    own2,
    far2,
    near2,
    send,
    recv,
):
    f32 = jnp.float32
    bf16 = jnp.bfloat16
    ring_x, ring_y = Ring(True), Ring(False)
    first = (ring_x, ring_y)
    second = (ring_y, ring_x)
    rows, width = held.shape[-2], held.shape[-1]
    greet((ring_x.right, ring_x.left, ring_y.right, ring_y.left))

    def gathers(phase):
        out = []
        for array in (1, 0):
            for half in (0, 1):
                if phase == 0:
                    block = functools.partial(
                        lambda a, h, i: held.at[a, h, second[h].place, i], array, half
                    )
                    ring = first[half]
                else:
                    block = functools.partial(lambda a, h, i: held.at[a, h, i], array, half)
                    ring = second[half]
                out.append(
                    Gather(ring, block, send.at[array, half, phase], recv.at[array, half, phase])
                )
        return out

    for array, ref in ((1, cots_ref), (0, rows_ref)):
        for half in (0, 1):
            held[array, half, second[half].place, first[half].place] = ref[
                half * rows : (half + 1) * rows, :
            ]
    near_gathers, far_gathers = gathers(0), gathers(1)
    for g in near_gathers:
        g.start()
    for g in near_gathers:
        g.before()
        g.after()
    for g, h in zip(near_gathers, far_gathers):
        g.across()
        h.start()

    def reduces(array, phase):
        out = []
        for half in (0, 1):
            if phase == 0:
                part = functools.partial(lambda h, i: parts.at[array, h, i], half)
                ring, boxes = second[half], (far.at[array, half], near.at[array, half])
            else:
                part = functools.partial(lambda h, i: own2.at[array, h, i], half)
                ring, boxes = first[half], (far2.at[array, half], near2.at[array, half])
            out.append(
                Reduce(
                    ring,
                    part,
                    *boxes,
                    send.at[array, half, 2 + phase],
                    recv.at[array, half, 2 + phase],
                )
            )
        return out

    both = SIDE * rows

    def group(k, carried):
        @pl.when(k == 1)
        def _():
            for g in far_gathers:
                g.before()

        @pl.when(k == 2)
        def _():
            for g in far_gathers:
                g.after()

        @pl.when(k == 3)
        def _():
            for g in far_gathers:
                g.across()

        shift = jnp.where(k == 0, 0, jnp.where(k == 1, SIDE - 1, jnp.where(k == 2, 1, 2)))
        places = [(second[h].place + shift) % SIDE for h in (0, 1)]

        def taken(array):
            return jnp.concatenate(
                [held[array, h, places[h]].reshape(both, width) for h in (0, 1)], axis=0
            )

        def put(array, tile, value):
            value = value.astype(bf16)
            for h in (0, 1):
                parts[array, h, places[h], :, :, tile] = value[
                    h * both : (h + 1) * both
                ].reshape(SIDE, rows, -1)

        x = taken(0)
        gate = jnp.dot(x, wg_ref[...], preferred_element_type=f32)
        up = jnp.dot(x, wu_ref[...], preferred_element_type=f32)
        hidden_grad = contract_last(taken(1), wd_ref[...])
        sigma = 1.0 / (1.0 + jnp.exp(-gate))
        active = gate * sigma
        hidden = (active * up).astype(bf16)
        gate_grad = (hidden_grad * up * sigma * (1.0 + gate * (1.0 - sigma))).astype(bf16)
        up_grad = (hidden_grad * active).astype(bf16)
        step = 512
        for n in range(width // step):
            tile = slice(n * step, (n + 1) * step)
            put(
                1,
                tile,
                contract_last(gate_grad, wg_ref[tile, :]) + contract_last(up_grad, wu_ref[tile, :]),
            )

        @pl.when(k == 3)
        def _():
            for r in reduces(1, 0):
                r.start()

        for n in range(width // step):
            tile = slice(n * step, (n + 1) * step)
            put(0, tile, jnp.dot(hidden, wd_ref[:, tile], preferred_element_type=f32))
        return carried

    lax.fori_loop(0, SIDE, group, 0)
    grads, outs = reduces(1, 0), reduces(0, 0)
    grads2, outs2 = reduces(1, 1), reduces(0, 1)
    for r in grads:
        r.middle()
    for r in outs:
        r.start()
    for half in (0, 1):
        own2[1, half] = grads[half].total()
        grads2[half].start()
    for r in outs:
        r.middle()
    for r in grads2:
        r.middle()
    for half in (0, 1):
        grad_ref[half * rows : (half + 1) * rows, :] = grads2[half].total()
    for half in (0, 1):
        own2[0, half] = outs[half].total()
        outs2[half].start()
    for r in outs2:
        r.middle()
    for half in (0, 1):
        out_ref[half * rows : (half + 1) * rows, :] = outs2[half].total()
    for g in near_gathers + far_gathers:
        g.finish()
    for r in grads + outs + grads2 + outs2:
        r.finish()


def experts(rows, cots, w_gate, w_up, w_down):
    count, width = rows.shape
    half = count // 2
    bf16 = jnp.bfloat16
    full = pltpu.VMEM((2, 2, SIDE, SIDE, half, width), bf16)
    return pl.pallas_call(
        experts_kernel,
        out_shape=[jax.ShapeDtypeStruct((count, width), bf16)] * 2,
        in_specs=[VMEM] * 5,
        out_specs=[VMEM] * 2,
        scratch_shapes=[
            full,
            full,
            pltpu.VMEM((2, 2, 2, SIDE // 2, half, width), bf16),
            pltpu.VMEM((2, 2, 2, SIDE, half, width), bf16),
            pltpu.VMEM((2, 2, SIDE, half, width), bf16),
            pltpu.VMEM((2, 2, 2, half // 2, width), bf16),
            pltpu.VMEM((2, 2, 2, half, width), bf16),
            pltpu.SemaphoreType.DMA((2, 2, 4, 4)),
            pltpu.SemaphoreType.DMA((2, 2, 4, 4)),
        ],
        compiler_params=pltpu.CompilerParams(
            vmem_limit_bytes=58 * 1024 * 1024, collective_id=1, has_side_effects=True
        ),
    )(rows, cots, w_gate, w_up, w_down)


def entering(ends, sums, rate2, backward):
    count = sums.shape[0]
    place = lax.axis_index("ctx")
    index = jnp.arange(count)
    if backward:
        between = (index[None, :] > place) & (index[None, :] < index[:, None])
        live = index > place
    else:
        between = (index[None, :] < place) & (index[None, :] > index[:, None])
        live = index < place
    gap = jnp.sum(jnp.where(between[:, :, None], sums[None], 0.0), axis=1)
    terms = jnp.exp2(gap[:, None, :] * rate2[None]) * ends.astype(jnp.float32)
    return jnp.sum(jnp.where(live[:, None, None], terms, 0.0), axis=0)


def local(
    u_in,
    z_gate,
    delta,
    b_in,
    c_in,
    rate,
    skip,
    w_out,
    resid,
    gain,
    expert_ids,
    route_weights,
    w_gate,
    w_up,
    w_down,
    d_out,
):
    seg_rows, channels = u_in.shape
    states = rate.shape[0]
    my_rows, width = resid.shape
    experts_count = lax.axis_size("exp")
    capacity = 4 * my_rows // experts_count
    f32 = jnp.float32
    shape = jax.ShapeDtypeStruct
    plane = pltpu.VMEM((seg_rows, channels), f32)
    rate2 = rate * (-math.log2(math.e))
    skip_row = skip[None, :]
    brep = jnp.broadcast_to(b_in[:, :, None], (seg_rows, states, LANES))
    crep = jnp.broadcast_to(c_in[:, :, None], (seg_rows, states, LANES))
    z_act = jax.nn.silu(z_gate.astype(f32))
    state_end, last_sum = local_call(
        forward_end,
        [shape((states, channels), f32), shape((1, channels), f32)],
        [plane],
        (delta, u_in, brep, rate2),
    )
    sums = lax.all_gather(last_sum[0], "ctx")
    ends = lax.all_gather(state_end.astype(jnp.bfloat16), "ctx")
    state_in = entering(ends, sums, rate2, False)
    (gated,) = local_call(
        forward_out,
        [shape((seg_rows, channels), jnp.bfloat16)],
        [plane, plane],
        (delta, u_in, brep, crep, rate2, state_in, skip_row, z_gate),
    )
    mixed = lax.psum_scatter(
        jnp.dot(gated, w_out, preferred_element_type=jnp.float32).astype(jnp.bfloat16),
        "exp",
        scatter_dimension=0,
        tiled=True,
    ).astype(jnp.float32)
    stream = resid.astype(jnp.float32) + mixed
    inverse = lax.rsqrt(jnp.mean(stream * stream, axis=-1, keepdims=True) + 1e-05)
    normed = (stream * inverse * gain[None, :]).astype(jnp.bfloat16)
    owners = expert_ids.reshape(-1)
    assign_count = owners.shape[0]
    onehot = (owners[:, None] == jnp.arange(experts_count, dtype=jnp.int32)[None, :]).astype(
        jnp.float32
    )
    assign_index = jnp.arange(assign_count)
    strict = (assign_index[:, None] > assign_index[None, :]).astype(jnp.float32)
    before = jnp.dot(strict, onehot, precision=lax.Precision.HIGHEST)
    slots = jnp.sum(before * onehot, axis=1).astype(jnp.int32)
    target = owners * capacity + slots
    placing = (
        jnp.arange(experts_count * capacity, dtype=jnp.int32)[:, None] == target[None, :]
    ).astype(jnp.bfloat16)
    paired = jnp.repeat(normed, 2, axis=0)
    outgoing = (
        jnp.dot(placing, paired, preferred_element_type=jnp.float32)
        .astype(jnp.bfloat16)
        .reshape(experts_count, capacity, width)
    )
    cotangent = (
        route_weights.reshape(-1)[:, None] * jnp.repeat(d_out.astype(jnp.float32), 2, axis=0)
    ).astype(jnp.bfloat16)
    grad_outgoing = (
        jnp.dot(placing, cotangent, preferred_element_type=jnp.float32)
        .astype(jnp.bfloat16)
        .reshape(experts_count, capacity, width)
    )
    arrived = lax.all_to_all(outgoing, "exp", split_axis=0, concat_axis=0, tiled=True)
    grad_arrived = lax.all_to_all(grad_outgoing, "exp", split_axis=0, concat_axis=0, tiled=True)
    summed, row_sums = experts(
        arrived.reshape(-1, width), grad_arrived.reshape(-1, width), w_gate[0], w_up[0], w_down[0]
    )
    row_sums = row_sums.reshape(arrived.shape)
    summed = summed.reshape(arrived.shape)
    returned = lax.all_to_all(summed, "exp", split_axis=0, concat_axis=0, tiled=True)
    expert_out = lax.dot_general(
        placing,
        returned.reshape(-1, width),
        (((0,), (0,)), ((), ())),
        preferred_element_type=jnp.float32,
    )
    expert_out = expert_out.reshape(my_rows, 2, width)
    final = (
        stream + route_weights[:, 0:1] * expert_out[:, 0] + route_weights[:, 1:2] * expert_out[:, 1]
    ).astype(jnp.bfloat16)
    grad_back = lax.all_to_all(row_sums, "exp", split_axis=0, concat_axis=0, tiled=True)
    normed_grad = lax.dot_general(
        placing,
        grad_back.reshape(-1, width),
        (((0,), (0,)), ((), ())),
        preferred_element_type=jnp.float32,
    )
    normed_grad = normed_grad.reshape(my_rows, 2, width)
    normed_grad = normed_grad[:, 0] + normed_grad[:, 1]
    scaled = normed_grad * gain[None, :]
    project_mean = jnp.mean(scaled * stream, axis=-1, keepdims=True)
    stream_grad = inverse * (scaled - stream * inverse * inverse * project_mean)
    grad_resid = (d_out.astype(jnp.float32) + stream_grad).astype(jnp.bfloat16)
    segment_grad = lax.all_gather(grad_resid, "exp", axis=0, tiled=True)
    out_grad = contract_last(segment_grad, w_out) * z_act
    (back_end,) = local_call(
        backward_end,
        [shape((states, channels), f32)],
        [],
        (delta, out_grad, crep, rate2),
    )
    back_ends = lax.all_gather(back_end.astype(jnp.bfloat16), "ctx")
    grad_in = entering(back_ends, sums, rate2, True)
    (grad_u,) = local_call(
        backward_out,
        [shape((seg_rows, channels), jnp.bfloat16)],
        [plane],
        (delta, out_grad, brep, crep, rate2, grad_in, skip_row),
    )
    return (final, grad_resid, grad_u)


def solution(mesh):
    return jax.shard_map(
        local,
        mesh=mesh,
        in_specs=(
            P("ctx", "exp"),
            P("ctx", "exp"),
            P("ctx", "exp"),
            P("ctx", None),
            P("ctx", None),
            P(None, "exp"),
            P("exp"),
            P("exp", None),
            P(("ctx", "exp"), None),
            P(),
            P(("ctx", "exp"), None),
            P(("ctx", "exp"), None),
            P("exp", None, "ctx"),
            P("exp", None, "ctx"),
            P("exp", "ctx", None),
            P(("ctx", "exp"), None),
        ),
        out_specs=(P(("ctx", "exp"), None), P(("ctx", "exp"), None), P("ctx", "exp")),
        check_vma=False,
    )
```

```python
import functools
import math

import jax
import jax.numpy as jnp
from jax import lax
from jax.experimental import pallas as pl
from jax.experimental.pallas import tpu as pltpu
from jax.sharding import PartitionSpec as P

LANES = 128
VMEM = pl.BlockSpec(memory_space=pltpu.VMEM)


def contract_last(left, right):
    return lax.dot_general(
        left, right, (((1,), (1,)), ((), ())), preferred_element_type=jnp.float32
    )


def silu(v):
    return v * (1.0 / (1.0 + jnp.exp(-v)))


def tiles_of(channels):
    return [slice(i * LANES, (i + 1) * LANES) for i in range(channels // LANES)]


GROUP = 8


def scan_tokens(rows, channels, planes, step, initial, out_ref=None, backward=False):
    tiles = tiles_of(channels)
    row_index = lax.broadcasted_iota(jnp.int32, (GROUP, LANES), 0)

    def group(i, carried):
        base = rows - GROUP - i * GROUP if backward else i * GROUP
        base = pl.multiple_of(base, GROUP)
        blocks = [[plane[pl.ds(base, GROUP), tile] for plane in planes] for tile in tiles]
        made = [jnp.zeros((GROUP, LANES), jnp.float32) for _ in tiles]
        carried = list(carried)
        for j in reversed(range(GROUP)) if backward else range(GROUP):
            for k, tile in enumerate(tiles):
                line = [b[j : j + 1] for b in blocks[k]]
                carried[k], row = step(base + j, tile, line, carried[k])
                if out_ref is not None:
                    made[k] = jnp.where(row_index == j, row, made[k])
        if out_ref is not None:
            for k, tile in enumerate(tiles):
                out_ref[pl.ds(base, GROUP), tile] = made[k]
        return tuple(carried)

    return lax.fori_loop(0, rows // GROUP, group, tuple(initial))


def zero_state(rate_ref):
    states, channels = rate_ref.shape
    return [jnp.zeros((states, LANES), jnp.float32) for _ in tiles_of(channels)]


SIDE = 4
TO_RIGHT, TO_LEFT, ON_RIGHT, ON_LEFT = 0, 1, 2, 3


class Ring:
    def __init__(self, along_x):
        c = lax.axis_index("ctx")
        x, y = c // SIDE, c % SIDE
        self.place = x if along_x else y
        up, down = (self.place + 1) % SIDE, (self.place + SIDE - 1) % SIDE
        self.after, self.before, self.across = up, down, (self.place + 2) % SIDE
        self.right = {"ctx": up * SIDE + y if along_x else x * SIDE + up}
        self.left = {"ctx": down * SIDE + y if along_x else x * SIDE + down}


def halves(ref):
    n = ref.shape[0] // 2
    return ref.at[pl.ds(0, n)], ref.at[pl.ds(n, n)]


class Gather:
    def __init__(self, ring, block, send, recv):
        self.ring, self.block, self.send, self.recv = ring, block, send, recv

    def copy(self, ref, way):
        target = self.ring.right if way in (TO_RIGHT, ON_RIGHT) else self.ring.left
        return pltpu.make_async_remote_copy(
            src_ref=ref,
            dst_ref=ref,
            send_sem=self.send.at[way],
            recv_sem=self.recv.at[way],
            device_id=target,
            device_id_type=pl.DeviceIdType.MESH,
        )

    def start(self):
        own = self.block(self.ring.place)
        self.copy(own, TO_RIGHT).start()
        self.copy(own, TO_LEFT).start()

    def before(self):
        came = self.block(self.ring.before)
        self.copy(came, TO_RIGHT).wait_recv()
        self.copy(halves(came)[0], ON_RIGHT).start()

    def after(self):
        came = self.block(self.ring.after)
        self.copy(came, TO_LEFT).wait_recv()
        self.copy(halves(came)[1], ON_LEFT).start()

    def across(self):
        first, second = halves(self.block(self.ring.across))
        self.copy(first, ON_RIGHT).wait_recv()
        self.copy(second, ON_LEFT).wait_recv()

    def finish(self):
        own = self.block(self.ring.place)
        self.copy(own, TO_RIGHT).wait_send()
        self.copy(own, TO_LEFT).wait_send()
        self.copy(halves(self.block(self.ring.before))[0], ON_RIGHT).wait_send()
        self.copy(halves(self.block(self.ring.after))[1], ON_LEFT).wait_send()


def add_into(total, term):
    total[...] = (total[...].astype(jnp.float32) + term[...].astype(jnp.float32)).astype(
        total.dtype
    )


class Reduce:
    def __init__(self, ring, part, far, near, send, recv):
        self.ring, self.part, self.far, self.near = ring, part, far, near
        self.send, self.recv = send, recv

    def copy(self, way):
        ring = self.ring
        source = {
            TO_RIGHT: lambda: halves(self.part(ring.across))[0],
            TO_LEFT: lambda: halves(self.part(ring.across))[1],
            ON_RIGHT: lambda: self.part(ring.after),
            ON_LEFT: lambda: self.part(ring.before),
        }[way]()
        target = {
            TO_RIGHT: self.far.at[0],
            TO_LEFT: self.far.at[1],
            ON_RIGHT: self.near.at[0],
            ON_LEFT: self.near.at[1],
        }[way]
        return pltpu.make_async_remote_copy(
            src_ref=source,
            dst_ref=target,
            send_sem=self.send.at[way],
            recv_sem=self.recv.at[way],
            device_id=ring.right if way in (TO_RIGHT, ON_RIGHT) else ring.left,
            device_id_type=pl.DeviceIdType.MESH,
        )

    def start(self):
        self.copy(TO_RIGHT).start()
        self.copy(TO_LEFT).start()

    def middle(self):
        self.copy(TO_RIGHT).wait_recv()
        add_into(halves(self.part(self.ring.after))[0], self.far.at[0])
        self.copy(ON_RIGHT).start()
        self.copy(TO_LEFT).wait_recv()
        add_into(halves(self.part(self.ring.before))[1], self.far.at[1])
        self.copy(ON_LEFT).start()

    def total(self):
        self.copy(ON_RIGHT).wait_recv()
        self.copy(ON_LEFT).wait_recv()
        f32 = jnp.float32
        own = self.part(self.ring.place)
        return (
            own[...].astype(f32) + self.near[0].astype(f32) + self.near[1].astype(f32)
        ).astype(own.dtype)

    def finish(self):
        for way in range(4):
            self.copy(way).wait_send()


def barrier_with(axes):
    barrier = pltpu.get_barrier_semaphore()
    total = 0
    for axis in axes:
        count = lax.axis_size(axis)
        me = lax.axis_index(axis)

        def signal(d, carried):
            pl.semaphore_signal(
                barrier,
                inc=1,
                device_id={axis: (me + d) % count},
                device_id_type=pl.DeviceIdType.MESH,
            )
            return carried

        lax.fori_loop(1, count, signal, 0)
        total += count - 1
    pl.semaphore_wait(barrier, total)


def remote(source, target, send, recv, device):
    return pltpu.make_async_remote_copy(
        src_ref=source,
        dst_ref=target,
        send_sem=send,
        recv_sem=recv,
        device_id=device,
        device_id_type=pl.DeviceIdType.MESH,
    )


def each(low, high, body):
    def step(i, carried):
        body(i)
        return carried

    lax.fori_loop(low, high, step, 0)


class Exchange:
    def __init__(self, source, box, send, recv):
        self.source, self.box, self.send, self.recv = source, box, send, recv
        self.me, self.count = lax.axis_index("exp"), lax.axis_size("exp")

    def copy(self, other, slot):
        return remote(
            self.source.at[other],
            self.box.at[slot],
            self.send.at[other],
            self.recv.at[slot],
            {"exp": other},
        )

    def start(self):
        self.box[self.me] = self.source[self.me]
        each(1, self.count, lambda d: self.copy((self.me + d) % self.count, self.me).start())

    def wait(self):
        def one(d):
            other = (self.me + d) % self.count
            self.copy(other, other).wait_recv()

        each(1, self.count, one)

    def finish(self):
        each(1, self.count, lambda d: self.copy((self.me + d) % self.count, self.me).wait_send())


class Spread:
    def __init__(self, source, box, send, recv):
        self.source, self.box, self.send, self.recv = source, box, send, recv
        self.me = lax.axis_index("ctx")

    def copy(self, other, slot):
        return remote(
            self.source,
            self.box.at[slot],
            self.send.at[other],
            self.recv.at[slot],
            {"ctx": other},
        )

    def start(self, low, high):
        each(low, high, lambda other: self.copy(other, self.me).start())

    def wait_one(self, other):
        self.copy(other, other).wait_recv()

    def finish(self, low, high):
        each(low, high, lambda other: self.copy(other, self.me).wait_send())


def regroup(quarter, rows, slots, transposed):
    size = (rows * 4, rows) if transposed else (rows, rows * 4)
    row = lax.broadcasted_iota(jnp.int32, size, 1 if transposed else 0)
    slab = lax.broadcasted_iota(jnp.int32, size, 0 if transposed else 1)
    place = (row // slots) * (4 * slots) + quarter * slots + row % slots
    return jnp.where(slab == place, 1.0, 0.0).astype(jnp.bfloat16)


def quarters(value):
    step = value.shape[-1] // 4
    return jnp.concatenate([value[:, q * step : (q + 1) * step] for q in range(4)], axis=0)


def whole(value):
    step = value.shape[0] // 4
    return jnp.concatenate([value[q * step : (q + 1) * step] for q in range(4)], axis=1)


def layer_kernel(
    delta_ref,
    u_ref,
    z_ref,
    brep_ref,
    crep_ref,
    rate_ref,
    skip_ref,
    wout_ref,
    resid_ref,
    gain_ref,
    weight_ref,
    place_ref,
    placet_ref,
    wg_ref,
    wu_ref,
    wd_ref,
    dout_ref,
    final_ref,
    gresid_ref,
    gradu_ref,
    drive,
    y,
    gated,
    end16,
    back16,
    sums,
    end_box,
    sum_box,
    back_box,
    state_send,
    state_recv,
    mixed,
    pair_box,
    mix_box,
    mix_send,
    mix_recv,
    slabs,
    boxes,
    slab_send,
    slab_recv,
    stream,
    segment,
    seg_send,
    seg_recv,
    held,
    parts,
    far,
    near,
    own2,
    far2,
    near2,
    send,
    recv,
):
    f32 = jnp.float32
    bf16 = jnp.bfloat16
    ring_x, ring_y = Ring(True), Ring(False)
    first = (ring_x, ring_y)
    second = (ring_y, ring_x)
    rows, width = held.shape[-2], held.shape[-1]
    seg_rows, channels = delta_ref.shape
    ctx, ctx_count = lax.axis_index("ctx"), lax.axis_size("ctx")
    exp, exp_count = lax.axis_index("exp"), lax.axis_size("exp")
    z, core = exp // 2, exp % 2
    z_count = exp_count // 2
    sibling = {"exp": z * 2 + 1 - core}
    slots = 2 * rows // exp_count
    my_rows = resid_ref.shape[0]
    slab_rows = slabs.shape[2]
    slab_width = slabs.shape[3]
    COT, ROW, GRAD, OUT = range(4)
    moves = [Exchange(slabs.at[i], boxes.at[i], slab_send.at[i], slab_recv.at[i]) for i in range(4)]
    ends = Spread(end16, end_box, state_send.at[0], state_recv.at[0])
    totals = Spread(sums, sum_box, state_send.at[1], state_recv.at[1])
    backs = Spread(back16, back_box, state_send.at[2], state_recv.at[2])

    def to_slabs(kind, value):
        slabs[kind] = value.astype(bf16).reshape(exp_count, slab_rows, slab_width)

    def dispatched(kind):
        flat = boxes[kind].reshape(exp_count * slab_rows, slab_width)
        return [
            jnp.dot(
                regroup(q, 2 * rows, slots, False), flat, preferred_element_type=f32
            ).astype(bf16)
            for q in range(4)
        ]

    def give_back(kind, read):
        total = None
        for q in range(4):
            tile = slice(q * slab_width, (q + 1) * slab_width)
            term = jnp.dot(
                regroup(q, 2 * rows, slots, True), read(tile), preferred_element_type=f32
            )
            total = term if total is None else total + term
        to_slabs(kind, total)

    def gather(array, half, phase):
        if phase == 0:
            block = lambda i: held.at[array, half, second[half].place, i]
            ring = first[half]
        else:
            block = lambda i: held.at[array, half, i]
            ring = second[half]
        return Gather(ring, block, send.at[array, half, phase], recv.at[array, half, phase])

    near_gathers = [[gather(a, h, 0) for h in (0, 1)] for a in (0, 1)]
    far_gathers = [[gather(a, h, 1) for h in (0, 1)] for a in (0, 1)]

    def take_in(array, kind):
        for q, value in enumerate(dispatched(kind)):
            tile = slice(q * slab_width, (q + 1) * slab_width)
            for half in (0, 1):
                held[array, half, second[half].place, first[half].place, :, tile] = value[
                    half * rows : (half + 1) * rows
                ]
        for g in near_gathers[array]:
            g.start()

    def spread_out(array):
        for g in near_gathers[array]:
            g.before()
            g.after()
        for g, h in zip(near_gathers[array], far_gathers[array]):
            g.across()
            h.start()

    def reduces(array, phase):
        out = []
        for half in (0, 1):
            if phase == 0:
                part = functools.partial(lambda h, i: parts.at[array, h, i], half)
                ring, inbox = second[half], (far.at[array, half], near.at[array, half])
            else:
                part = functools.partial(lambda h, i: own2.at[array, h, i], half)
                ring, inbox = first[half], (far2.at[array, half], near2.at[array, half])
            out.append(
                Reduce(
                    ring,
                    part,
                    *inbox,
                    send.at[array, half, 2 + phase],
                    recv.at[array, half, 2 + phase],
                )
            )
        return out

    def decay_of(line, tile):
        return jnp.exp2(line[0] * rate_ref[:, tile])

    states = rate_ref.shape[0]

    def joined(box, low_first):
        tiles = tiles_of(channels)

        def one(i, carried):
            gap, held_state = carried
            other = ctx - 1 - i if low_first else ctx + 1 + i
            (ends if low_first else backs).wait_one(other)
            totals.wait_one(other)
            made = tuple(
                h
                + jnp.exp2(gap[:, tile] * rate_ref[:, tile]) * box[other, :, tile].astype(f32)
                for tile, h in zip(tiles, held_state)
            )
            return gap + sum_box[other], made

        count = ctx if low_first else ctx_count - 1 - ctx
        zero = tuple(jnp.zeros((states, LANES), f32) for _ in tiles)
        return lax.fori_loop(0, count, one, (jnp.zeros((1, channels), f32), zero))[1]

    sums[...] = jnp.sum(delta_ref[...], axis=0, keepdims=True)
    d_out = dout_ref[...].astype(f32)
    to_slabs(
        COT,
        sum(
            jnp.dot(
                place_ref[k],
                quarters((weight_ref[:, k : k + 1] * d_out).astype(bf16)),
                preferred_element_type=f32,
            )
            for k in (0, 1)
        ),
    )
    barrier_with(("ctx", "exp"))
    totals.start(0, ctx)
    totals.start(ctx + 1, ctx_count)
    moves[COT].start()
    drive[...] = delta_ref[...] * u_ref[...].astype(f32)

    def end_step(t, tile, line, h):
        return decay_of(line, tile) * h + brep_ref[t] * line[1], None

    done = scan_tokens(seg_rows, channels, (delta_ref, drive), end_step, zero_state(rate_ref))
    for tile, h in zip(tiles_of(channels), done):
        end16[:, tile] = h.astype(bf16)
    ends.start(ctx + 1, ctx_count)
    moves[COT].wait()
    take_in(1, COT)

    def out_step(t, tile, line, h):
        new = decay_of(line, tile) * h + brep_ref[t] * line[1]
        return new, jnp.sum(crep_ref[t] * new, axis=0, keepdims=True)

    scan_tokens(seg_rows, channels, (delta_ref, drive), out_step, joined(end_box, True), y)
    gated[...] = (
        (y[...] + skip_ref[...] * u_ref[...].astype(f32)) * silu(z_ref[...].astype(f32))
    ).astype(bf16)
    step = 512
    for n in range(width // step):
        tile = slice(n * step, (n + 1) * step)
        value = (
            jnp.dot(gated[...], wout_ref[:, tile], preferred_element_type=f32)
            .astype(bf16)
            .reshape(z_count, 2, my_rows, step)
        )
        for k in (0, 1):
            mixed[k, :, :, tile] = value[:, k]
    pair = remote(
        mixed.at[1 - core], pair_box, mix_send.at[z], mix_recv.at[z], sibling
    )
    pair.start()
    spread_out(1)
    pair.wait_recv()

    def mix(other, slot):
        return remote(
            mixed.at[core, other],
            mix_box.at[slot],
            mix_send.at[other],
            mix_recv.at[slot],
            {"exp": other * 2 + core},
        )

    def mix_start(d):
        other = (z + d) % z_count
        add_into(mixed.at[core, other], pair_box.at[other])
        mix(other, z).start()

    each(1, z_count, mix_start)
    stream[...] = (
        resid_ref[...].astype(f32) + mixed[core, z].astype(f32) + pair_box[z].astype(f32)
    )

    def mix_take(d):
        other = (z + d) % z_count
        mix(other, other).wait_recv()
        stream[...] += mix_box[other].astype(f32)

    each(1, z_count, mix_take)
    flow = stream[...]
    inverse = lax.rsqrt(jnp.mean(flow * flow, axis=-1, keepdims=True) + 1e-05)
    normed = (flow * inverse * gain_ref[...]).astype(bf16)
    spread = place_ref[0] + place_ref[1]
    to_slabs(ROW, jnp.dot(spread, quarters(normed), preferred_element_type=f32))
    moves[ROW].start()
    for g in far_gathers[1]:
        g.before()
        g.after()
    moves[ROW].wait()
    take_in(0, ROW)
    spread_out(0)

    both = SIDE * rows

    def group(k, carried):
        @pl.when(k == 0)
        def _():
            for g in far_gathers[1]:
                g.across()

        @pl.when(k == 1)
        def _():
            for g in far_gathers[0]:
                g.before()

        @pl.when(k == 2)
        def _():
            for g in far_gathers[0]:
                g.after()

        @pl.when(k == 3)
        def _():
            for g in far_gathers[0]:
                g.across()

        shift = jnp.where(k == 0, 0, jnp.where(k == 1, SIDE - 1, jnp.where(k == 2, 1, 2)))
        places = [(second[h].place + shift) % SIDE for h in (0, 1)]

        def taken(array):
            return jnp.concatenate(
                [held[array, h, places[h]].reshape(both, width) for h in (0, 1)], axis=0
            )

        def put(array, tile, value):
            value = value.astype(bf16)
            for h in (0, 1):
                parts[array, h, places[h], :, :, tile] = value[
                    h * both : (h + 1) * both
                ].reshape(SIDE, rows, -1)

        x = taken(0)
        gate = jnp.dot(x, wg_ref[...], preferred_element_type=f32)
        up = jnp.dot(x, wu_ref[...], preferred_element_type=f32)
        hidden_grad = contract_last(taken(1), wd_ref[...])
        sigma = 1.0 / (1.0 + jnp.exp(-gate))
        active = gate * sigma
        hidden = (active * up).astype(bf16)
        gate_grad = (hidden_grad * up * sigma * (1.0 + gate * (1.0 - sigma))).astype(bf16)
        up_grad = (hidden_grad * active).astype(bf16)
        for n in range(width // step):
            tile = slice(n * step, (n + 1) * step)
            put(
                1,
                tile,
                contract_last(gate_grad, wg_ref[tile, :]) + contract_last(up_grad, wu_ref[tile, :]),
            )

        @pl.when(k == 3)
        def _():
            for r in reduces(1, 0):
                r.start()

        for n in range(width // step):
            tile = slice(n * step, (n + 1) * step)
            put(0, tile, jnp.dot(hidden, wd_ref[:, tile], preferred_element_type=f32))
        return carried

    lax.fori_loop(0, SIDE, group, 0)
    grads, outs = reduces(1, 0), reduces(0, 0)
    grads2, outs2 = reduces(1, 1), reduces(0, 1)
    for r in grads:
        r.middle()
    for half in (0, 1):
        own2[1, half] = grads[half].total()
        grads2[half].start()
    for r in outs:
        r.start()
    for r in grads2:
        r.middle()
    sent = [r.total() for r in grads2]
    give_back(GRAD, lambda tile: jnp.concatenate([v[:, tile] for v in sent], axis=0))
    moves[GRAD].start()
    moves[GRAD].wait()

    def combined(kind, matrix):
        flat = boxes[kind].reshape(exp_count * slab_rows, slab_width)
        return whole(jnp.dot(matrix, flat, preferred_element_type=f32))

    scaled = combined(GRAD, placet_ref[0] + placet_ref[1]) * gain_ref[...]
    flow = stream[...]
    inverse = lax.rsqrt(jnp.mean(flow * flow, axis=-1, keepdims=True) + 1e-05)
    project = jnp.mean(scaled * flow, axis=-1, keepdims=True)
    grad_rows = (
        dout_ref[...].astype(f32) + inverse * (scaled - flow * inverse * inverse * project)
    ).astype(bf16)
    gresid_ref[...] = grad_rows
    segment[exp] = grad_rows

    def seg(target, slot):
        return remote(
            segment.at[exp],
            segment.at[slot],
            seg_send.at[0, target],
            seg_recv.at[0, slot // 2],
            {"exp": target * 2 + core},
        )

    def seg_pair(slot):
        return remote(
            segment.at[slot],
            segment.at[slot],
            seg_send.at[1, slot // 2],
            seg_recv.at[1, slot // 2],
            sibling,
        )

    each(1, z_count, lambda d: seg((z + d) % z_count, exp).start())
    seg_pair(exp).start()
    for r in outs:
        r.middle()

    def seg_take(d):
        other = ((z + d) % z_count) * 2 + core
        seg((z + d) % z_count, other).wait_recv()
        seg_pair(other).start()

    each(1, z_count, seg_take)
    for half in (0, 1):
        own2[0, half] = outs[half].total()
        outs2[half].start()
    each(0, z_count, lambda i: seg_pair(i * 2 + 1 - core).wait_recv())
    grad = drive
    grad[...] = contract_last(
        segment[...].reshape(seg_rows, width), wout_ref[...]
    ) * silu(z_ref[...].astype(f32))

    def back_end_step(t, tile, line, h):
        return decay_of(line, tile) * (h + crep_ref[t] * line[1]), None

    done = scan_tokens(
        seg_rows, channels, (delta_ref, grad), back_end_step, zero_state(rate_ref), backward=True
    )
    for tile, h in zip(tiles_of(channels), done):
        back16[:, tile] = h.astype(bf16)
    backs.start(0, ctx)
    for r in outs2:
        r.middle()
    sent = [r.total() for r in outs2]
    give_back(OUT, lambda tile: jnp.concatenate([v[:, tile] for v in sent], axis=0))
    moves[OUT].start()

    def back_step(t, tile, line, h):
        new = h + crep_ref[t] * line[1]
        return decay_of(line, tile) * new, jnp.sum(brep_ref[t] * new, axis=0, keepdims=True)

    scan_tokens(
        seg_rows,
        channels,
        (delta_ref, grad),
        back_step,
        joined(back_box, False),
        y,
        backward=True,
    )
    gradu_ref[...] = (delta_ref[...] * y[...] + skip_ref[...] * grad[...]).astype(bf16)
    moves[OUT].wait()
    final_ref[...] = (
        stream[...]
        + weight_ref[:, 0:1] * combined(OUT, placet_ref[0])
        + weight_ref[:, 1:2] * combined(OUT, placet_ref[1])
    ).astype(bf16)

    for array in (0, 1):
        for g in near_gathers[array] + far_gathers[array]:
            g.finish()
    for r in grads + outs + grads2 + outs2:
        r.finish()
    for m in moves:
        m.finish()
    pair.wait_send()
    totals.finish(0, ctx)
    totals.finish(ctx + 1, ctx_count)
    ends.finish(ctx + 1, ctx_count)
    backs.finish(0, ctx)
    each(1, z_count, lambda d: mix((z + d) % z_count, z).wait_send())
    each(1, z_count, lambda d: seg((z + d) % z_count, exp).wait_send())
    each(0, z_count, lambda i: seg_pair(i * 2 + core).wait_send())


def layer(args, exp_count, ctx_count):
    delta, rate, resid = args[0], args[5], args[8]
    seg_rows, channels = delta.shape
    states = rate.shape[0]
    my_rows, width = resid.shape
    bf16, f32 = jnp.bfloat16, jnp.float32
    slots = 4 * my_rows // exp_count
    half = exp_count * slots // 2
    vm, dma = pltpu.VMEM, pltpu.SemaphoreType.DMA
    full = vm((2, 2, SIDE, SIDE, half, width), bf16)
    plane = vm((seg_rows, channels), f32)
    slab = vm((4, exp_count, 4 * slots, width // 4), bf16)
    state_box = vm((ctx_count, states, channels), bf16)
    shape = jax.ShapeDtypeStruct
    return pl.pallas_call(
        layer_kernel,
        out_shape=[
            shape((my_rows, width), bf16),
            shape((my_rows, width), bf16),
            shape((seg_rows, channels), bf16),
        ],
        in_specs=[VMEM] * len(args),
        out_specs=[VMEM] * 3,
        scratch_shapes=[
            plane,
            plane,
            vm((seg_rows, channels), bf16),
            vm((states, channels), bf16),
            vm((states, channels), bf16),
            vm((1, channels), f32),
            state_box,
            vm((ctx_count, 1, channels), f32),
            state_box,
            dma((3, ctx_count)),
            dma((3, ctx_count)),
            vm((2, exp_count // 2, my_rows, width), bf16),
            vm((exp_count // 2, my_rows, width), bf16),
            vm((exp_count // 2, my_rows, width), bf16),
            dma((exp_count // 2,)),
            dma((exp_count // 2,)),
            slab,
            slab,
            dma((4, exp_count)),
            dma((4, exp_count)),
            vm((my_rows, width), f32),
            vm((exp_count, my_rows, width), bf16),
            dma((2, exp_count // 2)),
            dma((2, exp_count // 2)),
            full,
            full,
            vm((2, 2, 2, SIDE // 2, half, width), bf16),
            vm((2, 2, 2, SIDE, half, width), bf16),
            vm((2, 2, SIDE, half, width), bf16),
            vm((2, 2, 2, half // 2, width), bf16),
            vm((2, 2, 2, half, width), bf16),
            dma((2, 2, 4, 4)),
            dma((2, 2, 4, 4)),
        ],
        compiler_params=pltpu.CompilerParams(
            vmem_limit_bytes=60 * 1024 * 1024, collective_id=1, has_side_effects=True
        ),
    )(*args)


def local(
    u_in,
    z_gate,
    delta,
    b_in,
    c_in,
    rate,
    skip,
    w_out,
    resid,
    gain,
    expert_ids,
    route_weights,
    w_gate,
    w_up,
    w_down,
    d_out,
):
    seg_rows, channels = u_in.shape
    states = rate.shape[0]
    my_rows, width = resid.shape
    experts_count = lax.axis_size("exp")
    capacity = 4 * my_rows // experts_count
    f32 = jnp.float32
    rate2 = rate * (-math.log2(math.e))
    brep = jnp.broadcast_to(b_in[:, :, None], (seg_rows, states, LANES))
    crep = jnp.broadcast_to(c_in[:, :, None], (seg_rows, states, LANES))
    owners = expert_ids.reshape(-1)
    assign_count = owners.shape[0]
    onehot = (owners[:, None] == jnp.arange(experts_count, dtype=jnp.int32)[None, :]).astype(
        jnp.float32
    )
    assign_index = jnp.arange(assign_count)
    strict = (assign_index[:, None] > assign_index[None, :]).astype(jnp.float32)
    before = jnp.dot(strict, onehot, precision=lax.Precision.HIGHEST)
    slots = jnp.sum(before * onehot, axis=1).astype(jnp.int32)
    target = owners * capacity + slots
    row = jnp.arange(4 * experts_count * capacity, dtype=jnp.int32)[:, None]
    column = jnp.arange(4 * my_rows, dtype=jnp.int32)[None, :]
    slab = 4 * capacity
    code = (row // slab) * capacity + row % capacity
    same = (row % slab) // capacity == column // my_rows
    targets = target.reshape(my_rows, 2)
    place = jnp.stack(
        [same & (code == jnp.tile(targets[:, k], 4)[None, :]) for k in (0, 1)]
    ).astype(jnp.bfloat16)
    return tuple(
        layer(
            (
                delta,
                u_in,
                z_gate,
                brep,
                crep,
                rate2,
                skip[None, :],
                w_out,
                resid,
                gain[None, :],
                route_weights,
                place,
                jnp.swapaxes(place, 1, 2),
                w_gate[0],
                w_up[0],
                w_down[0],
                d_out,
            ),
            experts_count,
            lax.axis_size("ctx"),
        )
    )


def solution(mesh):
    return jax.shard_map(
        local,
        mesh=mesh,
        in_specs=(
            P("ctx", "exp"),
            P("ctx", "exp"),
            P("ctx", "exp"),
            P("ctx", None),
            P("ctx", None),
            P(None, "exp"),
            P("exp"),
            P("exp", None),
            P(("ctx", "exp"), None),
            P(),
            P(("ctx", "exp"), None),
            P(("ctx", "exp"), None),
            P("exp", None, "ctx"),
            P("exp", None, "ctx"),
            P("exp", "ctx", None),
            P(("ctx", "exp"), None),
        ),
        out_specs=(P(("ctx", "exp"), None), P(("ctx", "exp"), None), P("ctx", "exp")),
        check_vma=False,
    )
```

```python
import functools
import math

import jax
import jax.numpy as jnp
from jax import lax
from jax.experimental import pallas as pl
from jax.experimental.pallas import tpu as pltpu
from jax.sharding import PartitionSpec as P

LANES = 128
VMEM = pl.BlockSpec(memory_space=pltpu.VMEM)


def contract_last(left, right):
    return lax.dot_general(
        left, right, (((1,), (1,)), ((), ())), preferred_element_type=jnp.float32
    )


def silu(v):
    return v * (1.0 / (1.0 + jnp.exp(-v)))


def tiles_of(channels):
    return [slice(i * LANES, (i + 1) * LANES) for i in range(channels // LANES)]


GROUP = 8


def scan_tokens(rows, channels, planes, step, initial, out_ref=None, backward=False):
    tiles = tiles_of(channels)
    row_index = lax.broadcasted_iota(jnp.int32, (GROUP, LANES), 0)

    def group(i, carried):
        base = rows - GROUP - i * GROUP if backward else i * GROUP
        base = pl.multiple_of(base, GROUP)
        blocks = [[plane[pl.ds(base, GROUP), tile] for plane in planes] for tile in tiles]
        made = [jnp.zeros((GROUP, LANES), jnp.float32) for _ in tiles]
        carried = list(carried)
        for j in reversed(range(GROUP)) if backward else range(GROUP):
            for k, tile in enumerate(tiles):
                line = [b[j : j + 1] for b in blocks[k]]
                carried[k], row = step(base + j, tile, line, carried[k])
                if out_ref is not None:
                    made[k] = jnp.where(row_index == j, row, made[k])
        if out_ref is not None:
            for k, tile in enumerate(tiles):
                out_ref[pl.ds(base, GROUP), tile] = made[k]
        return tuple(carried)

    return lax.fori_loop(0, rows // GROUP, group, tuple(initial))


def zero_state(rate_ref):
    states, channels = rate_ref.shape
    return [jnp.zeros((states, LANES), jnp.float32) for _ in tiles_of(channels)]


SIDE = 4
TO_RIGHT, TO_LEFT, ON_RIGHT, ON_LEFT = 0, 1, 2, 3


class Ring:
    def __init__(self, along_x):
        c = lax.axis_index("ctx")
        x, y = c // SIDE, c % SIDE
        self.place = x if along_x else y
        up, down = (self.place + 1) % SIDE, (self.place + SIDE - 1) % SIDE
        self.after, self.before, self.across = up, down, (self.place + 2) % SIDE
        self.right = {"ctx": up * SIDE + y if along_x else x * SIDE + up}
        self.left = {"ctx": down * SIDE + y if along_x else x * SIDE + down}


def halves(ref):
    n = ref.shape[0] // 2
    return ref.at[pl.ds(0, n)], ref.at[pl.ds(n, n)]


class Gather:
    def __init__(self, ring, block, send, recv):
        self.ring, self.block, self.send, self.recv = ring, block, send, recv

    def copy(self, ref, way):
        target = self.ring.right if way in (TO_RIGHT, ON_RIGHT) else self.ring.left
        return pltpu.make_async_remote_copy(
            src_ref=ref,
            dst_ref=ref,
            send_sem=self.send.at[way],
            recv_sem=self.recv.at[way],
            device_id=target,
            device_id_type=pl.DeviceIdType.MESH,
        )

    def start(self):
        own = self.block(self.ring.place)
        self.copy(own, TO_RIGHT).start()
        self.copy(own, TO_LEFT).start()

    def before(self):
        came = self.block(self.ring.before)
        self.copy(came, TO_RIGHT).wait_recv()
        self.copy(halves(came)[0], ON_RIGHT).start()

    def after(self):
        came = self.block(self.ring.after)
        self.copy(came, TO_LEFT).wait_recv()
        self.copy(halves(came)[1], ON_LEFT).start()

    def across(self):
        first, second = halves(self.block(self.ring.across))
        self.copy(first, ON_RIGHT).wait_recv()
        self.copy(second, ON_LEFT).wait_recv()

    def finish(self):
        own = self.block(self.ring.place)
        self.copy(own, TO_RIGHT).wait_send()
        self.copy(own, TO_LEFT).wait_send()
        self.copy(halves(self.block(self.ring.before))[0], ON_RIGHT).wait_send()
        self.copy(halves(self.block(self.ring.after))[1], ON_LEFT).wait_send()


def add_into(total, term):
    total[...] = (total[...].astype(jnp.float32) + term[...].astype(jnp.float32)).astype(
        total.dtype
    )


class Reduce:
    def __init__(self, ring, part, far, near, send, recv):
        self.ring, self.part, self.far, self.near = ring, part, far, near
        self.send, self.recv = send, recv

    def copy(self, way):
        ring = self.ring
        source = {
            TO_RIGHT: lambda: halves(self.part(ring.across))[0],
            TO_LEFT: lambda: halves(self.part(ring.across))[1],
            ON_RIGHT: lambda: self.part(ring.after),
            ON_LEFT: lambda: self.part(ring.before),
        }[way]()
        target = {
            TO_RIGHT: self.far.at[0],
            TO_LEFT: self.far.at[1],
            ON_RIGHT: self.near.at[0],
            ON_LEFT: self.near.at[1],
        }[way]
        return pltpu.make_async_remote_copy(
            src_ref=source,
            dst_ref=target,
            send_sem=self.send.at[way],
            recv_sem=self.recv.at[way],
            device_id=ring.right if way in (TO_RIGHT, ON_RIGHT) else ring.left,
            device_id_type=pl.DeviceIdType.MESH,
        )

    def start(self):
        self.copy(TO_RIGHT).start()
        self.copy(TO_LEFT).start()

    def middle(self):
        self.copy(TO_RIGHT).wait_recv()
        add_into(halves(self.part(self.ring.after))[0], self.far.at[0])
        self.copy(ON_RIGHT).start()
        self.copy(TO_LEFT).wait_recv()
        add_into(halves(self.part(self.ring.before))[1], self.far.at[1])
        self.copy(ON_LEFT).start()

    def total(self):
        self.copy(ON_RIGHT).wait_recv()
        self.copy(ON_LEFT).wait_recv()
        f32 = jnp.float32
        own = self.part(self.ring.place)
        return (
            own[...].astype(f32) + self.near[0].astype(f32) + self.near[1].astype(f32)
        ).astype(own.dtype)

    def finish(self):
        for way in range(4):
            self.copy(way).wait_send()


def barrier_with(axes):
    barrier = pltpu.get_barrier_semaphore()
    total = 0
    for axis in axes:
        count = lax.axis_size(axis)
        me = lax.axis_index(axis)

        def signal(d, carried):
            pl.semaphore_signal(
                barrier,
                inc=1,
                device_id={axis: (me + d) % count},
                device_id_type=pl.DeviceIdType.MESH,
            )
            return carried

        lax.fori_loop(1, count, signal, 0)
        total += count - 1
    pl.semaphore_wait(barrier, total)


def remote(source, target, send, recv, device):
    return pltpu.make_async_remote_copy(
        src_ref=source,
        dst_ref=target,
        send_sem=send,
        recv_sem=recv,
        device_id=device,
        device_id_type=pl.DeviceIdType.MESH,
    )


def each(low, high, body):
    def step(i, carried):
        body(i)
        return carried

    lax.fori_loop(low, high, step, 0)


class Exchange:
    def __init__(self, source, box, send, recv):
        self.source, self.box, self.send, self.recv = source, box, send, recv
        self.me, self.count = lax.axis_index("exp"), lax.axis_size("exp")

    def copy(self, other, slot):
        return remote(
            self.source.at[other],
            self.box.at[slot],
            self.send.at[other],
            self.recv.at[slot],
            {"exp": other},
        )

    def start(self):
        self.box[self.me] = self.source[self.me]
        each(1, self.count, lambda d: self.copy((self.me + d) % self.count, self.me).start())

    def wait(self):
        def one(d):
            other = (self.me + d) % self.count
            self.copy(other, other).wait_recv()

        each(1, self.count, one)

    def finish(self):
        each(1, self.count, lambda d: self.copy((self.me + d) % self.count, self.me).wait_send())


class Spread:
    def __init__(self, source, box, send, recv):
        self.source, self.box, self.send, self.recv = source, box, send, recv
        self.me = lax.axis_index("ctx")

    def copy(self, other, slot):
        return remote(
            self.source,
            self.box.at[slot],
            self.send.at[other],
            self.recv.at[slot],
            {"ctx": other},
        )

    def start(self, low, high):
        each(low, high, lambda other: self.copy(other, self.me).start())

    def wait_one(self, other):
        self.copy(other, other).wait_recv()

    def finish(self, low, high):
        each(low, high, lambda other: self.copy(other, self.me).wait_send())


def regroup(quarter, rows, slots, transposed):
    size = (rows * 4, rows) if transposed else (rows, rows * 4)
    row = lax.broadcasted_iota(jnp.int32, size, 1 if transposed else 0)
    slab = lax.broadcasted_iota(jnp.int32, size, 0 if transposed else 1)
    place = (row // slots) * (4 * slots) + quarter * slots + row % slots
    return jnp.where(slab == place, 1.0, 0.0).astype(jnp.bfloat16)


def quarters(value):
    step = value.shape[-1] // 4
    return jnp.concatenate([value[:, q * step : (q + 1) * step] for q in range(4)], axis=0)


def whole(value):
    step = value.shape[0] // 4
    return jnp.concatenate([value[q * step : (q + 1) * step] for q in range(4)], axis=1)


def as_column(row):
    count = row.shape[1]
    line = lax.broadcasted_iota(jnp.int32, (count, count), 0)
    column = lax.broadcasted_iota(jnp.int32, (count, count), 1)
    return jnp.sum(jnp.where(line == column, row, 0.0), axis=1, keepdims=True)


def make_places(ids_ref, place_ref, placet_ref, experts, slots, tokens):
    f32, i32 = jnp.float32, jnp.int32
    iota = lax.broadcasted_iota
    ids = [as_column(ids_ref[k : k + 1, :].astype(f32)) for k in (0, 1)]
    names = iota(i32, (tokens, experts), 1).astype(f32)
    onehot = [jnp.where(names == c, 1.0, 0.0) for c in ids]
    earlier = iota(i32, (tokens, tokens), 0) > iota(i32, (tokens, tokens), 1)
    before = jnp.dot(
        jnp.where(earlier, 1.0, 0.0).astype(jnp.bfloat16),
        (onehot[0] + onehot[1]).astype(jnp.bfloat16),
        preferred_element_type=f32,
    )
    slab = 4 * slots

    def codes(size, axis):
        row = iota(i32, size, axis)
        return ((row // slab) * slots + row % slots).astype(f32), (row % slab) // slots

    wide = 4 * experts * slots
    for k in (0, 1):
        target = ids[k] * slots + jnp.sum(before * onehot[k], axis=1, keepdims=True)
        place = iota(i32, (tokens, 4 * tokens), 1) % tokens
        own = place == iota(i32, (tokens, 4 * tokens), 0)
        target_row = jnp.sum(jnp.where(own, target, 0.0), axis=0, keepdims=True)
        code, quarter = codes((wide, 4 * tokens), 0)
        same = quarter == iota(i32, (wide, 4 * tokens), 1) // tokens
        place_ref[k] = jnp.where(
            jnp.logical_and(same, code == target_row), 1.0, 0.0
        ).astype(place_ref.dtype)
        code, quarter = codes((4 * tokens, wide), 1)
        same = quarter == iota(i32, (4 * tokens, wide), 0) // tokens
        target_column = jnp.concatenate([target] * 4, axis=0)
        placet_ref[k] = jnp.where(
            jnp.logical_and(same, code == target_column), 1.0, 0.0
        ).astype(placet_ref.dtype)


def spread_lanes(source_ref, target_ref):
    states, count = source_ref.shape

    def some(i, carried):
        for part in range(count // LANES):
            lanes = source_ref[:, part * LANES : (part + 1) * LANES]
            turned = pltpu.roll(lanes, (LANES - i * GROUP) % LANES, 1)
            for j in range(GROUP):
                target_ref[part * LANES + i * GROUP + j] = jnp.broadcast_to(
                    turned[:, j : j + 1], (states, LANES)
                )
        return carried

    lax.fori_loop(0, LANES // GROUP, some, 0)


def layer_kernel(
    delta_ref,
    u_ref,
    z_ref,
    b_ref,
    c_ref,
    plain_rate_ref,
    skip_ref,
    wout_hbm,
    resid_ref,
    gain_ref,
    ids_ref,
    weight_ref,
    wg_hbm,
    wu_hbm,
    wd_hbm,
    dout_ref,
    final_ref,
    gresid_ref,
    gradu_ref,
    brep_ref,
    crep_ref,
    rate_ref,
    wout_ref,
    wg_ref,
    wu_ref,
    wd_ref,
    weight_sem,
    place_ref,
    placet_ref,
    drive,
    y,
    gated,
    end16,
    back16,
    sums,
    end_box,
    sum_box,
    back_box,
    state_send,
    state_recv,
    mixed,
    pair_box,
    pair_send,
    pair_recv,
    mix_box,
    mix_send,
    mix_recv,
    slabs,
    boxes,
    slab_send,
    slab_recv,
    stream,
    segment,
    seg_send,
    seg_recv,
    twin_send,
    twin_recv,
    held,
    parts,
    far,
    near,
    own2,
    far2,
    near2,
    send,
    recv,
):
    f32 = jnp.float32
    bf16 = jnp.bfloat16
    ring_x, ring_y = Ring(True), Ring(False)
    first = (ring_x, ring_y)
    second = (ring_y, ring_x)
    rows, width = held.shape[-2], held.shape[-1]
    seg_rows, channels = delta_ref.shape
    ctx, ctx_count = lax.axis_index("ctx"), lax.axis_size("ctx")
    exp, exp_count = lax.axis_index("exp"), lax.axis_size("exp")
    z, core = exp // 2, exp % 2
    z_count = exp_count // 2
    sibling = {"exp": z * 2 + 1 - core}
    slots = 2 * rows // exp_count
    my_rows = resid_ref.shape[0]
    slab_rows = slabs.shape[2]
    slab_width = slabs.shape[3]
    COT, ROW, GRAD, OUT = range(4)
    moves = [Exchange(slabs.at[i], boxes.at[i], slab_send.at[i], slab_recv.at[i]) for i in range(4)]
    ends = Spread(end16, end_box, state_send.at[0], state_recv.at[0])
    totals = Spread(sums, sum_box, state_send.at[1], state_recv.at[1])
    backs = Spread(back16, back_box, state_send.at[2], state_recv.at[2])

    def to_slabs(kind, value):
        slabs[kind] = value.astype(bf16).reshape(exp_count, slab_rows, slab_width)

    def dispatched(kind):
        flat = boxes[kind].reshape(exp_count * slab_rows, slab_width)
        return [
            jnp.dot(
                regroup(q, 2 * rows, slots, False), flat, preferred_element_type=f32
            ).astype(bf16)
            for q in range(4)
        ]

    def give_back(kind, read):
        total = None
        for q in range(4):
            tile = slice(q * slab_width, (q + 1) * slab_width)
            term = jnp.dot(
                regroup(q, 2 * rows, slots, True), read(tile), preferred_element_type=f32
            )
            total = term if total is None else total + term
        to_slabs(kind, total)

    def gather(array, half, phase):
        if phase == 0:
            block = lambda i: held.at[array, half, second[half].place, i]
            ring = first[half]
        else:
            block = lambda i: held.at[array, half, i]
            ring = second[half]
        return Gather(ring, block, send.at[array, half, phase], recv.at[array, half, phase])

    near_gathers = [[gather(a, h, 0) for h in (0, 1)] for a in (0, 1)]
    far_gathers = [[gather(a, h, 1) for h in (0, 1)] for a in (0, 1)]

    def take_in(array, kind):
        for q, value in enumerate(dispatched(kind)):
            tile = slice(q * slab_width, (q + 1) * slab_width)
            for half in (0, 1):
                held[array, half, second[half].place, first[half].place, :, tile] = value[
                    half * rows : (half + 1) * rows
                ]
        for g in near_gathers[array]:
            g.start()

    def spread_out(array):
        for g in near_gathers[array]:
            g.before()
            g.after()
        for g, h in zip(near_gathers[array], far_gathers[array]):
            g.across()
            h.start()

    def reduces(array, phase):
        out = []
        for half in (0, 1):
            if phase == 0:
                part = functools.partial(lambda h, i: parts.at[array, h, i], half)
                ring, inbox = second[half], (far.at[array, half], near.at[array, half])
            else:
                part = functools.partial(lambda h, i: own2.at[array, h, i], half)
                ring, inbox = first[half], (far2.at[array, half], near2.at[array, half])
            out.append(
                Reduce(
                    ring,
                    part,
                    *inbox,
                    send.at[array, half, 2 + phase],
                    recv.at[array, half, 2 + phase],
                )
            )
        return out

    def decay_of(line, tile):
        return jnp.exp2(line[0] * rate_ref[:, tile])

    states = rate_ref.shape[0]

    def joined(box, low_first):
        tiles = tiles_of(channels)

        def one(i, carried):
            gap, held_state = carried
            other = ctx - 1 - i if low_first else ctx + 1 + i
            (ends if low_first else backs).wait_one(other)
            totals.wait_one(other)
            made = tuple(
                h
                + jnp.exp2(gap[:, tile] * rate_ref[:, tile]) * box[other, :, tile].astype(f32)
                for tile, h in zip(tiles, held_state)
            )
            return gap + sum_box[other], made

        count = ctx if low_first else ctx_count - 1 - ctx
        zero = tuple(jnp.zeros((states, LANES), f32) for _ in tiles)
        return lax.fori_loop(0, count, one, (jnp.zeros((1, channels), f32), zero))[1]

    fetches = [
        pltpu.make_async_copy(source, target, weight_sem.at[i])
        for i, (source, target) in enumerate(
            ((wout_hbm, wout_ref), (wd_hbm, wd_ref), (wg_hbm, wg_ref), (wu_hbm, wu_ref))
        )
    ]
    for f in fetches:
        f.start()
    sums[...] = jnp.sum(delta_ref[...], axis=0, keepdims=True)
    rate_ref[...] = plain_rate_ref[...] * (-math.log2(math.e))
    make_places(ids_ref, place_ref, placet_ref, exp_count, slots, my_rows)
    columns = [as_column(weight_ref[k : k + 1, :]) for k in (0, 1)]
    d_out = dout_ref[...].astype(f32)
    to_slabs(
        COT,
        sum(
            jnp.dot(
                place_ref[k],
                quarters((columns[k] * d_out).astype(bf16)),
                preferred_element_type=f32,
            )
            for k in (0, 1)
        ),
    )
    barrier_with(("ctx", "exp"))
    totals.start(0, ctx)
    totals.start(ctx + 1, ctx_count)
    moves[COT].start()
    spread_lanes(b_ref, brep_ref)
    drive[...] = delta_ref[...] * u_ref[...].astype(f32)

    def end_step(t, tile, line, h):
        return decay_of(line, tile) * h + brep_ref[t] * line[1], None

    done = scan_tokens(seg_rows, channels, (delta_ref, drive), end_step, zero_state(rate_ref))
    for tile, h in zip(tiles_of(channels), done):
        end16[:, tile] = h.astype(bf16)
    ends.start(ctx + 1, ctx_count)
    spread_lanes(c_ref, crep_ref)
    moves[COT].wait()
    take_in(1, COT)

    def out_step(t, tile, line, h):
        new = decay_of(line, tile) * h + brep_ref[t] * line[1]
        return new, jnp.sum(crep_ref[t] * new, axis=0, keepdims=True)

    scan_tokens(seg_rows, channels, (delta_ref, drive), out_step, joined(end_box, True), y)
    gated[...] = (
        (y[...] + skip_ref[...] * u_ref[...].astype(f32)) * silu(z_ref[...].astype(f32))
    ).astype(bf16)
    step = 512
    fetches[0].wait()
    for n in range(width // step):
        tile = slice(n * step, (n + 1) * step)
        value = (
            jnp.dot(gated[...], wout_ref[:, tile], preferred_element_type=f32)
            .astype(bf16)
            .reshape(z_count, 2, my_rows, step)
        )
        for k in (0, 1):
            mixed[k, :, :, tile] = value[:, k]
    pair = remote(mixed.at[1 - core], pair_box, pair_send.at[0], pair_recv.at[0], sibling)
    pair.start()
    spread_out(1)
    pair.wait_recv()

    RIGHT, LEFT = 0, 1
    hops = z_count // 2
    middle = width // 2
    beside = [
        {"exp": ((z + 1) % z_count) * 2 + core},
        {"exp": ((z + z_count - 1) % z_count) * 2 + core},
    ]

    def at_distance(way, far_by):
        return (z + far_by) % z_count if way == RIGHT else (z + z_count - far_by) % z_count

    def side(ref, way, halved):
        return ref.at[:, pl.ds(way * middle, middle)] if halved else ref

    def mix(way, hop):
        return remote(
            side(mixed.at[core, at_distance(way, hops - hop)], way, hop == 0),
            side(mix_box.at[way, hop], way, hop == 0),
            mix_send.at[way, hop],
            mix_recv.at[way, hop],
            beside[way],
        )

    add_into(mixed.at[core, at_distance(RIGHT, hops)], pair_box.at[at_distance(RIGHT, hops)])
    for way in (RIGHT, LEFT):
        mix(way, 0).start()

    def add_pair(d):
        other = (z + d) % z_count
        add_into(mixed.at[core, other], pair_box.at[other])

    each(hops + 1, z_count + hops, add_pair)
    for hop in range(1, hops):
        for way in (RIGHT, LEFT):
            mix(way, hop - 1).wait_recv()
            add_into(
                side(mixed.at[core, at_distance(way, hops - hop)], way, hop == 1),
                side(mix_box.at[way, hop - 1], way, hop == 1),
            )
            mix(way, hop).start()
    for way in (RIGHT, LEFT):
        mix(way, hops - 1).wait_recv()
    stream[...] = (
        resid_ref[...].astype(f32)
        + mixed[core, z].astype(f32)
        + mix_box[RIGHT, hops - 1].astype(f32)
        + mix_box[LEFT, hops - 1].astype(f32)
    )
    flow = stream[...]
    inverse = lax.rsqrt(jnp.mean(flow * flow, axis=-1, keepdims=True) + 1e-05)
    normed = (flow * inverse * gain_ref[...]).astype(bf16)
    spread = place_ref[0] + place_ref[1]
    to_slabs(ROW, jnp.dot(spread, quarters(normed), preferred_element_type=f32))
    moves[ROW].start()
    for g in far_gathers[1]:
        g.before()
        g.after()
    moves[ROW].wait()
    take_in(0, ROW)
    spread_out(0)

    for f in fetches[1:]:
        f.wait()
    both = SIDE * rows

    def group(k, carried):
        @pl.when(k == 0)
        def _():
            for g in far_gathers[1]:
                g.across()

        @pl.when(k == 1)
        def _():
            for g in far_gathers[0]:
                g.before()

        @pl.when(k == 2)
        def _():
            for g in far_gathers[0]:
                g.after()

        @pl.when(k == 3)
        def _():
            for g in far_gathers[0]:
                g.across()

        shift = jnp.where(k == 0, 0, jnp.where(k == 1, SIDE - 1, jnp.where(k == 2, 1, 2)))
        places = [(second[h].place + shift) % SIDE for h in (0, 1)]

        def taken(array):
            return jnp.concatenate(
                [held[array, h, places[h]].reshape(both, width) for h in (0, 1)], axis=0
            )

        def put(array, tile, value):
            value = value.astype(bf16)
            for h in (0, 1):
                parts[array, h, places[h], :, :, tile] = value[
                    h * both : (h + 1) * both
                ].reshape(SIDE, rows, -1)

        x = taken(0)
        gate = jnp.dot(x, wg_ref[...], preferred_element_type=f32)
        up = jnp.dot(x, wu_ref[...], preferred_element_type=f32)
        hidden_grad = contract_last(taken(1), wd_ref[...])
        sigma = 1.0 / (1.0 + jnp.exp(-gate))
        active = gate * sigma
        hidden = (active * up).astype(bf16)
        gate_grad = (hidden_grad * up * sigma * (1.0 + gate * (1.0 - sigma))).astype(bf16)
        up_grad = (hidden_grad * active).astype(bf16)
        for n in range(width // step):
            tile = slice(n * step, (n + 1) * step)
            put(
                1,
                tile,
                contract_last(gate_grad, wg_ref[tile, :]) + contract_last(up_grad, wu_ref[tile, :]),
            )

        @pl.when(k == 3)
        def _():
            for r in reduces(1, 0):
                r.start()

        for n in range(width // step):
            tile = slice(n * step, (n + 1) * step)
            put(0, tile, jnp.dot(hidden, wd_ref[:, tile], preferred_element_type=f32))
        return carried

    lax.fori_loop(0, SIDE, group, 0)
    grads, outs = reduces(1, 0), reduces(0, 0)
    grads2, outs2 = reduces(1, 1), reduces(0, 1)
    for r in grads:
        r.middle()
    for half in (0, 1):
        own2[1, half] = grads[half].total()
        grads2[half].start()
    for r in outs:
        r.start()
    for r in grads2:
        r.middle()
    sent = [r.total() for r in grads2]
    give_back(GRAD, lambda tile: jnp.concatenate([v[:, tile] for v in sent], axis=0))
    moves[GRAD].start()
    for r in outs:
        r.middle()
    moves[GRAD].wait()

    def combined(kind, matrix):
        flat = boxes[kind].reshape(exp_count * slab_rows, slab_width)
        return whole(jnp.dot(matrix, flat, preferred_element_type=f32))

    scaled = combined(GRAD, placet_ref[0] + placet_ref[1]) * gain_ref[...]
    flow = stream[...]
    inverse = lax.rsqrt(jnp.mean(flow * flow, axis=-1, keepdims=True) + 1e-05)
    project = jnp.mean(scaled * flow, axis=-1, keepdims=True)
    grad_rows = (
        dout_ref[...].astype(f32) + inverse * (scaled - flow * inverse * inverse * project)
    ).astype(bf16)
    gresid_ref[...] = grad_rows
    segment[exp] = grad_rows

    def seg(way, hop, came=False):
        block = segment.at[at_distance(1 - way, hop + (1 if came else 0)) * 2 + core]
        block = side(block, way, hop == hops - 1)
        return remote(block, block, seg_send.at[way, hop], seg_recv.at[way, hop], beside[way])

    def twin(slot):
        return remote(
            segment.at[slot],
            segment.at[slot],
            twin_send.at[slot // 2],
            twin_recv.at[slot // 2],
            sibling,
        )

    for way in (RIGHT, LEFT):
        seg(way, 0).start()
    twin(exp).start()
    for hop in range(1, hops):
        for way in (RIGHT, LEFT):
            seg(way, hop - 1, True).wait_recv()
            seg(way, hop).start()
            twin(at_distance(1 - way, hop) * 2 + core).start()
    for way in (RIGHT, LEFT):
        seg(way, hops - 1, True).wait_recv()
    twin(at_distance(RIGHT, hops) * 2 + core).start()
    for half in (0, 1):
        own2[0, half] = outs[half].total()
        outs2[half].start()
    each(0, z_count, lambda i: twin(i * 2 + 1 - core).wait_recv())
    grad = drive
    grad[...] = contract_last(
        segment[...].reshape(seg_rows, width), wout_ref[...]
    ) * silu(z_ref[...].astype(f32))

    for r in outs2:
        r.middle()

    def back_end_step(t, tile, line, h):
        return decay_of(line, tile) * (h + crep_ref[t] * line[1]), None

    done = scan_tokens(
        seg_rows, channels, (delta_ref, grad), back_end_step, zero_state(rate_ref), backward=True
    )
    for tile, h in zip(tiles_of(channels), done):
        back16[:, tile] = h.astype(bf16)
    backs.start(0, ctx)
    sent = [r.total() for r in outs2]
    give_back(OUT, lambda tile: jnp.concatenate([v[:, tile] for v in sent], axis=0))
    moves[OUT].start()

    def back_step(t, tile, line, h):
        new = h + crep_ref[t] * line[1]
        return decay_of(line, tile) * new, jnp.sum(brep_ref[t] * new, axis=0, keepdims=True)

    scan_tokens(
        seg_rows,
        channels,
        (delta_ref, grad),
        back_step,
        joined(back_box, False),
        y,
        backward=True,
    )
    gradu_ref[...] = (delta_ref[...] * y[...] + skip_ref[...] * grad[...]).astype(bf16)
    moves[OUT].wait()
    final_ref[...] = (
        stream[...]
        + columns[0] * combined(OUT, placet_ref[0])
        + columns[1] * combined(OUT, placet_ref[1])
    ).astype(bf16)

    for array in (0, 1):
        for g in near_gathers[array] + far_gathers[array]:
            g.finish()
    for r in grads + outs + grads2 + outs2:
        r.finish()
    for m in moves:
        m.finish()
    pair.wait_send()
    totals.finish(0, ctx)
    totals.finish(ctx + 1, ctx_count)
    ends.finish(ctx + 1, ctx_count)
    backs.finish(0, ctx)
    for way in (RIGHT, LEFT):
        for hop in range(hops):
            mix(way, hop).wait_send()
            seg(way, hop).wait_send()
    each(0, z_count, lambda i: twin(i * 2 + core).wait_send())


def settle_kernel(*refs):
    half = len(refs) // 2
    for source, target in zip(refs[:half], refs[half:]):
        target[...] = source[...]


def settle(values):
    return pl.pallas_call(
        settle_kernel,
        out_shape=[jax.ShapeDtypeStruct(v.shape, v.dtype) for v in values],
        in_specs=[VMEM] * len(values),
        out_specs=[VMEM] * len(values),
    )(*values)


def layer(args, exp_count, ctx_count):
    delta, rate, resid = args[0], args[5], args[8]
    seg_rows, channels = delta.shape
    states = rate.shape[0]
    my_rows, width = resid.shape
    bf16, f32 = jnp.bfloat16, jnp.float32
    slots = 4 * my_rows // exp_count
    half = exp_count * slots // 2
    vm, dma = pltpu.VMEM, pltpu.SemaphoreType.DMA
    full = vm((2, 2, SIDE, SIDE, half, width), bf16)
    plane = vm((seg_rows, channels), f32)
    slab = vm((4, exp_count, 4 * slots, width // 4), bf16)
    state_box = vm((ctx_count, states, channels), bf16)
    shape = jax.ShapeDtypeStruct
    return pl.pallas_call(
        layer_kernel,
        out_shape=[
            shape((my_rows, width), bf16),
            shape((my_rows, width), bf16),
            shape((seg_rows, channels), bf16),
        ],
        in_specs=[
            pl.BlockSpec(memory_space=pl.ANY) if i in (7, 12, 13, 14) else VMEM
            for i in range(len(args))
        ],
        out_specs=[VMEM] * 3,
        scratch_shapes=[
            vm((seg_rows, states, LANES), f32),
            vm((seg_rows, states, LANES), f32),
            vm((states, channels), f32),
            *[vm(args[i].shape, bf16) for i in (7, 12, 13, 14)],
            dma((4,)),
            vm((2, 4 * exp_count * slots, 4 * my_rows), bf16),
            vm((2, 4 * my_rows, 4 * exp_count * slots), bf16),
            plane,
            plane,
            vm((seg_rows, channels), bf16),
            vm((states, channels), bf16),
            vm((states, channels), bf16),
            vm((1, channels), f32),
            state_box,
            vm((ctx_count, 1, channels), f32),
            state_box,
            dma((3, ctx_count)),
            dma((3, ctx_count)),
            vm((2, exp_count // 2, my_rows, width), bf16),
            vm((exp_count // 2, my_rows, width), bf16),
            dma((1,)),
            dma((1,)),
            vm((2, exp_count // 4, my_rows, width), bf16),
            dma((2, exp_count // 4)),
            dma((2, exp_count // 4)),
            slab,
            slab,
            dma((4, exp_count)),
            dma((4, exp_count)),
            vm((my_rows, width), f32),
            vm((exp_count, my_rows, width), bf16),
            dma((2, exp_count // 4)),
            dma((2, exp_count // 4)),
            dma((exp_count // 2,)),
            dma((exp_count // 2,)),
            full,
            full,
            vm((2, 2, 2, SIDE // 2, half, width), bf16),
            vm((2, 2, 2, SIDE, half, width), bf16),
            vm((2, 2, SIDE, half, width), bf16),
            vm((2, 2, 2, half // 2, width), bf16),
            vm((2, 2, 2, half, width), bf16),
            dma((2, 2, 4, 4)),
            dma((2, 2, 4, 4)),
        ],
        compiler_params=pltpu.CompilerParams(
            vmem_limit_bytes=60 * 1024 * 1024, collective_id=1, has_side_effects=True
        ),
    )(*args)


def local(
    u_in,
    z_gate,
    delta,
    b_in,
    c_in,
    rate,
    skip,
    w_out,
    resid,
    gain,
    expert_ids,
    route_weights,
    w_gate,
    w_up,
    w_down,
    d_out,
):
    return tuple(
        settle(
            layer(
                (
                    delta,
                    u_in,
                    z_gate,
                    b_in.T,
                    c_in.T,
                    rate,
                    skip[None, :],
                    w_out,
                    resid,
                    gain[None, :],
                    expert_ids.T,
                    route_weights.T,
                    w_gate[0],
                    w_up[0],
                    w_down[0],
                    d_out,
                ),
                lax.axis_size("exp"),
                lax.axis_size("ctx"),
            )
        )
    )


def solution(mesh):
    return jax.shard_map(
        local,
        mesh=mesh,
        in_specs=(
            P("ctx", "exp"),
            P("ctx", "exp"),
            P("ctx", "exp"),
            P("ctx", None),
            P("ctx", None),
            P(None, "exp"),
            P("exp"),
            P("exp", None),
            P(("ctx", "exp"), None),
            P(),
            P(("ctx", "exp"), None),
            P(("ctx", "exp"), None),
            P("exp", None, "ctx"),
            P("exp", None, "ctx"),
            P("exp", "ctx", None),
            P(("ctx", "exp"), None),
        ),
        out_specs=(P(("ctx", "exp"), None), P(("ctx", "exp"), None), P("ctx", "exp")),
        check_vma=False,
    )
```

```python
import functools
import math

import jax
import jax.numpy as jnp
from jax import lax
from jax.experimental import pallas as pl
from jax.experimental.pallas import tpu as pltpu
from jax.sharding import PartitionSpec as P

LANES = 128
VMEM = pl.BlockSpec(memory_space=pltpu.VMEM)


def contract_last(left, right):
    return lax.dot_general(
        left, right, (((1,), (1,)), ((), ())), preferred_element_type=jnp.float32
    )


def silu(v):
    return v * (1.0 / (1.0 + jnp.exp(-v)))


def tiles_of(channels):
    return [slice(i * LANES, (i + 1) * LANES) for i in range(channels // LANES)]


GROUP = 8


def scan_tokens(rows, channels, planes, step, initial, out_ref=None, backward=False):
    tiles = tiles_of(channels)
    row_index = lax.broadcasted_iota(jnp.int32, (GROUP, LANES), 0)

    def group(i, carried):
        base = rows - GROUP - i * GROUP if backward else i * GROUP
        base = pl.multiple_of(base, GROUP)
        blocks = [[plane[pl.ds(base, GROUP), tile] for plane in planes] for tile in tiles]
        made = [jnp.zeros((GROUP, LANES), jnp.float32) for _ in tiles]
        carried = list(carried)
        for j in reversed(range(GROUP)) if backward else range(GROUP):
            for k, tile in enumerate(tiles):
                line = [b[j : j + 1] for b in blocks[k]]
                carried[k], row = step(base + j, tile, line, carried[k])
                if out_ref is not None:
                    made[k] = jnp.where(row_index == j, row, made[k])
        if out_ref is not None:
            for k, tile in enumerate(tiles):
                out_ref[pl.ds(base, GROUP), tile] = made[k]
        return tuple(carried)

    return lax.fori_loop(0, rows // GROUP, group, tuple(initial))


def zero_state(rate_ref):
    states, channels = rate_ref.shape
    return [jnp.zeros((states, LANES), jnp.float32) for _ in tiles_of(channels)]


SIDE = 4
class Ring:
    def __init__(self, along_x):
        c = lax.axis_index("ctx")
        x, y = c // SIDE, c % SIDE
        self.place = x if along_x else y
        up, down = (self.place + 1) % SIDE, (self.place + SIDE - 1) % SIDE
        self.after, self.before, self.across = up, down, (self.place + 2) % SIDE
        self.right = {"ctx": up * SIDE + y if along_x else x * SIDE + up}
        self.left = {"ctx": down * SIDE + y if along_x else x * SIDE + down}


def halves(ref):
    n = ref.shape[0] // 2
    return ref.at[pl.ds(0, n)], ref.at[pl.ds(n, n)]


class Gather:
    def __init__(self, ring, block, pieces, send, recv):
        self.ring, self.block, self.pieces, self.send, self.recv = ring, block, pieces, send, recv

    def copy(self, ref, rightward, sem):
        return pltpu.make_async_remote_copy(
            src_ref=ref,
            dst_ref=ref,
            send_sem=self.send.at[sem],
            recv_sem=self.recv.at[sem],
            device_id=self.ring.right if rightward else self.ring.left,
            device_id_type=pl.DeviceIdType.MESH,
        )

    def piece(self, place, rightward, i):
        ref = self.block(place)
        ref = ref if self.pieces == 1 else ref.at[i]
        return self.copy(ref, rightward, 2 + i if rightward else 2 + self.pieces + i)

    def on(self, place, rightward):
        return self.copy(halves(self.block(place))[0 if rightward else 1], rightward, 0 if rightward else 1)

    def start(self, i=0):
        for rightward in (True, False):
            self.piece(self.ring.place, rightward, i).start()

    def before(self):
        for i in range(self.pieces):
            self.piece(self.ring.before, True, i).wait_recv()
        self.on(self.ring.before, True).start()

    def after(self):
        for i in range(self.pieces):
            self.piece(self.ring.after, False, i).wait_recv()
        self.on(self.ring.after, False).start()

    def across(self):
        for rightward in (True, False):
            self.on(self.ring.across, rightward).wait_recv()

    def finish(self):
        for rightward in (True, False):
            for i in range(self.pieces):
                self.piece(self.ring.place, rightward, i).wait_send()
        self.on(self.ring.before, True).wait_send()
        self.on(self.ring.after, False).wait_send()


def add_into(total, term):
    total[...] = (total[...].astype(jnp.float32) + term[...].astype(jnp.float32)).astype(
        total.dtype
    )


FAR_RIGHT, FAR_LEFT, ON_RIGHT, ON_LEFT, DIRECT_RIGHT, DIRECT_LEFT = range(6)


class Reduce:
    def __init__(self, ring, part, far, near, send, recv):
        self.ring, self.part, self.far, self.near = ring, part, far, near
        self.send, self.recv = send, recv

    def copy(self, way):
        ring = self.ring
        source, target = {
            FAR_RIGHT: lambda: (halves(self.part(ring.across))[0], self.far.at[0]),
            FAR_LEFT: lambda: (halves(self.part(ring.across))[1], self.far.at[1]),
            ON_RIGHT: lambda: (halves(self.part(ring.after))[0], halves(self.near.at[0])[0]),
            ON_LEFT: lambda: (halves(self.part(ring.before))[1], halves(self.near.at[1])[1]),
            DIRECT_RIGHT: lambda: (halves(self.part(ring.after))[1], halves(self.near.at[0])[1]),
            DIRECT_LEFT: lambda: (halves(self.part(ring.before))[0], halves(self.near.at[1])[0]),
        }[way]()
        rightward = way in (FAR_RIGHT, ON_RIGHT, DIRECT_RIGHT)
        return pltpu.make_async_remote_copy(
            src_ref=source,
            dst_ref=target,
            send_sem=self.send.at[way],
            recv_sem=self.recv.at[way],
            device_id=ring.right if rightward else ring.left,
            device_id_type=pl.DeviceIdType.MESH,
        )

    def start(self):
        self.copy(FAR_RIGHT).start()
        self.copy(FAR_LEFT).start()

    def direct(self):
        self.copy(DIRECT_RIGHT).start()
        self.copy(DIRECT_LEFT).start()

    def middle(self):
        self.copy(FAR_RIGHT).wait_recv()
        add_into(halves(self.part(self.ring.after))[0], self.far.at[0])
        self.copy(ON_RIGHT).start()
        self.copy(FAR_LEFT).wait_recv()
        add_into(halves(self.part(self.ring.before))[1], self.far.at[1])
        self.copy(ON_LEFT).start()

    def total(self):
        for way in (ON_RIGHT, ON_LEFT, DIRECT_RIGHT, DIRECT_LEFT):
            self.copy(way).wait_recv()
        f32 = jnp.float32
        own = self.part(self.ring.place)
        return (
            own[...].astype(f32) + self.near[0].astype(f32) + self.near[1].astype(f32)
        ).astype(own.dtype)

    def finish(self):
        for way in range(6):
            self.copy(way).wait_send()


def barrier_with(axes):
    barrier = pltpu.get_barrier_semaphore()
    total = 0
    for axis in axes:
        count = lax.axis_size(axis)
        me = lax.axis_index(axis)

        def signal(d, carried):
            pl.semaphore_signal(
                barrier,
                inc=1,
                device_id={axis: (me + d) % count},
                device_id_type=pl.DeviceIdType.MESH,
            )
            return carried

        lax.fori_loop(1, count, signal, 0)
        total += count - 1
    pl.semaphore_wait(barrier, total)


def remote(source, target, send, recv, device):
    return pltpu.make_async_remote_copy(
        src_ref=source,
        dst_ref=target,
        send_sem=send,
        recv_sem=recv,
        device_id=device,
        device_id_type=pl.DeviceIdType.MESH,
    )


def each(low, high, body):
    def step(i, carried):
        body(i)
        return carried

    lax.fori_loop(low, high, step, 0)


class Exchange:
    def __init__(self, source, box, send, recv):
        self.source, self.box, self.send, self.recv = source, box, send, recv
        self.me, self.count = lax.axis_index("exp"), lax.axis_size("exp")

    def copy(self, other, slot):
        return remote(
            self.source.at[other],
            self.box.at[slot],
            self.send.at[other],
            self.recv.at[slot],
            {"exp": other},
        )

    def start(self):
        self.box[self.me] = self.source[self.me]
        each(1, self.count, lambda d: self.copy((self.me + d) % self.count, self.me).start())

    def wait(self):
        def one(d):
            other = (self.me + d) % self.count
            self.copy(other, other).wait_recv()

        each(1, self.count, one)

    def finish(self):
        each(1, self.count, lambda d: self.copy((self.me + d) % self.count, self.me).wait_send())


class Spread:
    def __init__(self, source, box, send, recv):
        self.source, self.box, self.send, self.recv = source, box, send, recv
        self.me = lax.axis_index("ctx")

    def copy(self, other, slot):
        return remote(
            self.source,
            self.box.at[slot],
            self.send.at[other],
            self.recv.at[slot],
            {"ctx": other},
        )

    def start(self, low, high):
        each(low, high, lambda other: self.copy(other, self.me).start())

    def wait_one(self, other):
        self.copy(other, other).wait_recv()

    def finish(self, low, high):
        each(low, high, lambda other: self.copy(other, self.me).wait_send())


def regroup(quarter, rows, slots, transposed):
    size = (rows * 4, rows) if transposed else (rows, rows * 4)
    row = lax.broadcasted_iota(jnp.int32, size, 1 if transposed else 0)
    slab = lax.broadcasted_iota(jnp.int32, size, 0 if transposed else 1)
    place = (row // slots) * (4 * slots) + quarter * slots + row % slots
    return jnp.where(slab == place, 1.0, 0.0).astype(jnp.bfloat16)


def quarters(value):
    step = value.shape[-1] // 4
    return jnp.concatenate([value[:, q * step : (q + 1) * step] for q in range(4)], axis=0)


def whole(value):
    step = value.shape[0] // 4
    return jnp.concatenate([value[q * step : (q + 1) * step] for q in range(4)], axis=1)


def as_column(row):
    count = row.shape[1]
    line = lax.broadcasted_iota(jnp.int32, (count, count), 0)
    column = lax.broadcasted_iota(jnp.int32, (count, count), 1)
    return jnp.sum(jnp.where(line == column, row, 0.0), axis=1, keepdims=True)


def make_places(ids_ref, place_ref, placet_ref, experts, slots, tokens):
    f32, i32 = jnp.float32, jnp.int32
    iota = lax.broadcasted_iota
    ids = [as_column(ids_ref[k : k + 1, :].astype(f32)) for k in (0, 1)]
    names = iota(i32, (tokens, experts), 1).astype(f32)
    onehot = [jnp.where(names == c, 1.0, 0.0) for c in ids]
    earlier = iota(i32, (tokens, tokens), 0) > iota(i32, (tokens, tokens), 1)
    before = jnp.dot(
        jnp.where(earlier, 1.0, 0.0).astype(jnp.bfloat16),
        (onehot[0] + onehot[1]).astype(jnp.bfloat16),
        preferred_element_type=f32,
    )
    slab = 4 * slots

    def codes(size, axis):
        row = iota(i32, size, axis)
        return ((row // slab) * slots + row % slots).astype(f32), (row % slab) // slots

    wide = 4 * experts * slots
    for k in (0, 1):
        target = ids[k] * slots + jnp.sum(before * onehot[k], axis=1, keepdims=True)
        place = iota(i32, (tokens, 4 * tokens), 1) % tokens
        own = place == iota(i32, (tokens, 4 * tokens), 0)
        target_row = jnp.sum(jnp.where(own, target, 0.0), axis=0, keepdims=True)
        code, quarter = codes((wide, 4 * tokens), 0)
        same = quarter == iota(i32, (wide, 4 * tokens), 1) // tokens
        place_ref[k] = jnp.where(
            jnp.logical_and(same, code == target_row), 1.0, 0.0
        ).astype(place_ref.dtype)
        code, quarter = codes((4 * tokens, wide), 1)
        same = quarter == iota(i32, (4 * tokens, wide), 0) // tokens
        target_column = jnp.concatenate([target] * 4, axis=0)
        placet_ref[k] = jnp.where(
            jnp.logical_and(same, code == target_column), 1.0, 0.0
        ).astype(placet_ref.dtype)


def spread_lanes(source_ref, target_ref):
    states, count = source_ref.shape

    def some(i, carried):
        for part in range(count // LANES):
            lanes = source_ref[:, part * LANES : (part + 1) * LANES]
            turned = pltpu.roll(lanes, (LANES - i * GROUP) % LANES, 1)
            for j in range(GROUP):
                target_ref[part * LANES + i * GROUP + j] = jnp.broadcast_to(
                    turned[:, j : j + 1], (states, LANES)
                )
        return carried

    lax.fori_loop(0, LANES // GROUP, some, 0)


def layer_kernel(
    delta_ref,
    u_ref,
    z_ref,
    b_ref,
    c_ref,
    plain_rate_ref,
    skip_ref,
    wout_hbm,
    resid_ref,
    gain_ref,
    ids_ref,
    weight_ref,
    wg_hbm,
    wu_hbm,
    wd_hbm,
    dout_ref,
    final_ref,
    gresid_ref,
    gradu_ref,
    brep_ref,
    crep_ref,
    rate_ref,
    wout_ref,
    wg_ref,
    wu_ref,
    wd_ref,
    weight_sem,
    place_ref,
    placet_ref,
    drive,
    y,
    gated,
    end16,
    back16,
    sums,
    end_box,
    sum_box,
    back_box,
    state_send,
    state_recv,
    mixed,
    pair_box,
    pair_send,
    pair_recv,
    mix_box,
    mix_send,
    mix_recv,
    slabs,
    boxes,
    slab_send,
    slab_recv,
    stream,
    segment,
    seg_send,
    seg_recv,
    twin_send,
    twin_recv,
    held,
    parts,
    far,
    near,
    own2,
    far2,
    near2,
    send,
    recv,
):
    f32 = jnp.float32
    bf16 = jnp.bfloat16
    ring_x, ring_y = Ring(True), Ring(False)
    first = (ring_x, ring_y)
    second = (ring_y, ring_x)
    rows, width = held.shape[-2], held.shape[-1]
    seg_rows, channels = delta_ref.shape
    ctx, ctx_count = lax.axis_index("ctx"), lax.axis_size("ctx")
    exp, exp_count = lax.axis_index("exp"), lax.axis_size("exp")
    z, core = exp // 2, exp % 2
    z_count = exp_count // 2
    sibling = {"exp": z * 2 + 1 - core}
    slots = 2 * rows // exp_count
    my_rows = resid_ref.shape[0]
    slab_rows = slabs.shape[2]
    slab_width = slabs.shape[3]
    COT, ROW, GRAD, OUT = range(4)
    moves = [Exchange(slabs.at[i], boxes.at[i], slab_send.at[i], slab_recv.at[i]) for i in range(4)]
    ends = Spread(end16, end_box, state_send.at[0], state_recv.at[0])
    totals = Spread(sums, sum_box, state_send.at[1], state_recv.at[1])
    backs = Spread(back16, back_box, state_send.at[2], state_recv.at[2])

    def to_slabs(kind, value):
        slabs[kind] = value.astype(bf16).reshape(exp_count, slab_rows, slab_width)

    def dispatched(kind):
        flat = boxes[kind].reshape(exp_count * slab_rows, slab_width)
        return [
            jnp.dot(
                regroup(q, 2 * rows, slots, False), flat, preferred_element_type=f32
            ).astype(bf16)
            for q in range(4)
        ]

    def give_back(kind, read):
        total = None
        for q in range(4):
            tile = slice(q * slab_width, (q + 1) * slab_width)
            term = jnp.dot(
                regroup(q, 2 * rows, slots, True), read(tile), preferred_element_type=f32
            )
            total = term if total is None else total + term
        to_slabs(kind, total)

    def gather(array, half, phase):
        if phase == 0:
            block = lambda i: held.at[array, half, second[half].place, i]
            ring, pieces = first[half], 1
        else:
            block = lambda i: held.at[array, half, i]
            ring, pieces = second[half], SIDE
        return Gather(ring, block, pieces, send.at[array, half, phase], recv.at[array, half, phase])

    near_gathers = [[gather(a, h, 0) for h in (0, 1)] for a in (0, 1)]
    far_gathers = [[gather(a, h, 1) for h in (0, 1)] for a in (0, 1)]

    def take_in(array, kind):
        for q, value in enumerate(dispatched(kind)):
            tile = slice(q * slab_width, (q + 1) * slab_width)
            for half in (0, 1):
                held[array, half, second[half].place, first[half].place, :, tile] = value[
                    half * rows : (half + 1) * rows
                ]
        for g in near_gathers[array]:
            g.start()
        for half in (0, 1):
            far_gathers[array][half].start(first[half].place)

    def spread_out(array):
        pairs = list(zip(near_gathers[array], far_gathers[array]))
        for g, h in pairs:
            g.before()
            g.after()
        for g, h in pairs:
            h.start(g.ring.before)
            h.start(g.ring.after)
        for g, h in pairs:
            g.across()
            h.start(g.ring.across)

    def reduces(array, phase):
        out = []
        for half in (0, 1):
            if phase == 0:
                part = functools.partial(lambda h, i: parts.at[array, h, i], half)
                ring, inbox = second[half], (far.at[array, half], near.at[array, half])
            else:
                part = functools.partial(lambda h, i: own2.at[array, h, i], half)
                ring, inbox = first[half], (far2.at[array, half], near2.at[array, half])
            out.append(
                Reduce(
                    ring,
                    part,
                    *inbox,
                    send.at[array, half, 2 + phase],
                    recv.at[array, half, 2 + phase],
                )
            )
        return out

    def decay_of(line, tile):
        return jnp.exp2(line[0] * rate_ref[:, tile])

    states = rate_ref.shape[0]

    def joined(box, low_first):
        tiles = tiles_of(channels)

        def one(i, carried):
            gap, held_state = carried
            other = ctx - 1 - i if low_first else ctx + 1 + i
            (ends if low_first else backs).wait_one(other)
            totals.wait_one(other)
            made = tuple(
                h
                + jnp.exp2(gap[:, tile] * rate_ref[:, tile]) * box[other, :, tile].astype(f32)
                for tile, h in zip(tiles, held_state)
            )
            return gap + sum_box[other], made

        count = ctx if low_first else ctx_count - 1 - ctx
        zero = tuple(jnp.zeros((states, LANES), f32) for _ in tiles)
        return lax.fori_loop(0, count, one, (jnp.zeros((1, channels), f32), zero))[1]

    fetches = [
        pltpu.make_async_copy(source, target, weight_sem.at[i])
        for i, (source, target) in enumerate(
            ((wout_hbm, wout_ref), (wd_hbm, wd_ref), (wg_hbm, wg_ref), (wu_hbm, wu_ref))
        )
    ]
    for f in fetches:
        f.start()
    sums[...] = jnp.sum(delta_ref[...], axis=0, keepdims=True)
    rate_ref[...] = plain_rate_ref[...] * (-math.log2(math.e))
    make_places(ids_ref, place_ref, placet_ref, exp_count, slots, my_rows)
    columns = [as_column(weight_ref[k : k + 1, :]) for k in (0, 1)]
    d_out = dout_ref[...].astype(f32)
    to_slabs(
        COT,
        sum(
            jnp.dot(
                place_ref[k],
                quarters((columns[k] * d_out).astype(bf16)),
                preferred_element_type=f32,
            )
            for k in (0, 1)
        ),
    )
    barrier_with(("ctx", "exp"))
    totals.start(0, ctx)
    totals.start(ctx + 1, ctx_count)
    moves[COT].start()
    spread_lanes(b_ref, brep_ref)
    drive[...] = delta_ref[...] * u_ref[...].astype(f32)

    def end_step(t, tile, line, h):
        return decay_of(line, tile) * h + brep_ref[t] * line[1], None

    done = scan_tokens(seg_rows, channels, (delta_ref, drive), end_step, zero_state(rate_ref))
    for tile, h in zip(tiles_of(channels), done):
        end16[:, tile] = h.astype(bf16)
    ends.start(ctx + 1, ctx_count)
    spread_lanes(c_ref, crep_ref)
    moves[COT].wait()
    take_in(1, COT)

    def out_step(t, tile, line, h):
        new = decay_of(line, tile) * h + brep_ref[t] * line[1]
        return new, jnp.sum(crep_ref[t] * new, axis=0, keepdims=True)

    scan_tokens(seg_rows, channels, (delta_ref, drive), out_step, joined(end_box, True), y)
    gated[...] = (
        (y[...] + skip_ref[...] * u_ref[...].astype(f32)) * silu(z_ref[...].astype(f32))
    ).astype(bf16)
    step = 512
    fetches[0].wait()
    for n in range(width // step):
        tile = slice(n * step, (n + 1) * step)
        value = (
            jnp.dot(gated[...], wout_ref[:, tile], preferred_element_type=f32)
            .astype(bf16)
            .reshape(z_count, 2, my_rows, step)
        )
        for k in (0, 1):
            mixed[k, :, :, tile] = value[:, k]
    pair = remote(mixed.at[1 - core], pair_box, pair_send.at[0], pair_recv.at[0], sibling)
    pair.start()
    spread_out(1)
    pair.wait_recv()

    RIGHT, LEFT = 0, 1
    hops = z_count // 2
    middle = width // 2
    beside = [
        {"exp": ((z + 1) % z_count) * 2 + core},
        {"exp": ((z + z_count - 1) % z_count) * 2 + core},
    ]

    def at_distance(way, far_by):
        return (z + far_by) % z_count if way == RIGHT else (z + z_count - far_by) % z_count

    def side(ref, way, halved):
        return ref.at[:, pl.ds(way * middle, middle)] if halved else ref

    def mix(way, hop):
        return remote(
            side(mixed.at[core, at_distance(way, hops - hop)], way, hop == 0),
            side(mix_box.at[way, hop], way, hop == 0),
            mix_send.at[way, hop],
            mix_recv.at[way, hop],
            beside[way],
        )

    add_into(mixed.at[core, at_distance(RIGHT, hops)], pair_box.at[at_distance(RIGHT, hops)])
    for way in (RIGHT, LEFT):
        mix(way, 0).start()

    def add_pair(d):
        other = (z + d) % z_count
        add_into(mixed.at[core, other], pair_box.at[other])

    each(hops + 1, z_count + hops, add_pair)
    for hop in range(1, hops):
        for way in (RIGHT, LEFT):
            mix(way, hop - 1).wait_recv()
            add_into(
                side(mixed.at[core, at_distance(way, hops - hop)], way, hop == 1),
                side(mix_box.at[way, hop - 1], way, hop == 1),
            )
            mix(way, hop).start()
    for way in (RIGHT, LEFT):
        mix(way, hops - 1).wait_recv()
    stream[...] = (
        resid_ref[...].astype(f32)
        + mixed[core, z].astype(f32)
        + mix_box[RIGHT, hops - 1].astype(f32)
        + mix_box[LEFT, hops - 1].astype(f32)
    )
    flow = stream[...]
    inverse = lax.rsqrt(jnp.mean(flow * flow, axis=-1, keepdims=True) + 1e-05)
    normed = (flow * inverse * gain_ref[...]).astype(bf16)
    spread = place_ref[0] + place_ref[1]
    to_slabs(ROW, jnp.dot(spread, quarters(normed), preferred_element_type=f32))
    moves[ROW].start()
    for g in far_gathers[1]:
        g.before()
        g.after()
    moves[ROW].wait()
    take_in(0, ROW)
    spread_out(0)

    for f in fetches[1:]:
        f.wait()
    both = SIDE * rows

    def group(k, carried):
        @pl.when(k == 0)
        def _():
            for g in far_gathers[1]:
                g.across()

        @pl.when(k == 1)
        def _():
            for g in far_gathers[0]:
                g.before()
                g.after()

        @pl.when(k == 3)
        def _():
            for g in far_gathers[0]:
                g.across()
            for r in reduces(1, 0):
                r.direct()

        shift = jnp.where(k == 0, 0, jnp.where(k == 1, SIDE - 1, jnp.where(k == 2, 1, 2)))
        places = [(second[h].place + shift) % SIDE for h in (0, 1)]

        def taken(array):
            return jnp.concatenate(
                [held[array, h, places[h]].reshape(both, width) for h in (0, 1)], axis=0
            )

        def put(array, tile, value):
            value = value.astype(bf16)
            for h in (0, 1):
                parts[array, h, places[h], :, :, tile] = value[
                    h * both : (h + 1) * both
                ].reshape(SIDE, rows, -1)

        x = taken(0)
        gate = jnp.dot(x, wg_ref[...], preferred_element_type=f32)
        up = jnp.dot(x, wu_ref[...], preferred_element_type=f32)
        hidden_grad = contract_last(taken(1), wd_ref[...])
        sigma = 1.0 / (1.0 + jnp.exp(-gate))
        active = gate * sigma
        hidden = (active * up).astype(bf16)
        gate_grad = (hidden_grad * up * sigma * (1.0 + gate * (1.0 - sigma))).astype(bf16)
        up_grad = (hidden_grad * active).astype(bf16)
        for n in range(width // step):
            tile = slice(n * step, (n + 1) * step)
            put(
                1,
                tile,
                contract_last(gate_grad, wg_ref[tile, :]) + contract_last(up_grad, wu_ref[tile, :]),
            )

        @pl.when(k == 3)
        def _():
            for r in reduces(1, 0):
                r.start()

        for n in range(width // step):
            tile = slice(n * step, (n + 1) * step)
            put(0, tile, jnp.dot(hidden, wd_ref[:, tile], preferred_element_type=f32))
        return carried

    lax.fori_loop(0, SIDE, group, 0)
    grads, outs = reduces(1, 0), reduces(0, 0)
    grads2, outs2 = reduces(1, 1), reduces(0, 1)
    for r in grads:
        r.middle()
    for half in (0, 1):
        own2[1, half] = grads[half].total()
        grads2[half].start()
        grads2[half].direct()
    for r in grads2:
        r.middle()
    for r in outs:
        r.start()
        r.direct()
    sent = [r.total() for r in grads2]
    give_back(GRAD, lambda tile: jnp.concatenate([v[:, tile] for v in sent], axis=0))
    moves[GRAD].start()
    for r in outs:
        r.middle()
    moves[GRAD].wait()

    def combined(kind, matrix):
        flat = boxes[kind].reshape(exp_count * slab_rows, slab_width)
        return whole(jnp.dot(matrix, flat, preferred_element_type=f32))

    scaled = combined(GRAD, placet_ref[0] + placet_ref[1]) * gain_ref[...]
    flow = stream[...]
    inverse = lax.rsqrt(jnp.mean(flow * flow, axis=-1, keepdims=True) + 1e-05)
    project = jnp.mean(scaled * flow, axis=-1, keepdims=True)
    grad_rows = (
        dout_ref[...].astype(f32) + inverse * (scaled - flow * inverse * inverse * project)
    ).astype(bf16)
    gresid_ref[...] = grad_rows
    segment[exp] = grad_rows

    def seg(way, hop, came=False):
        block = segment.at[at_distance(1 - way, hop + (1 if came else 0)) * 2 + core]
        block = side(block, way, hop == hops - 1)
        return remote(block, block, seg_send.at[way, hop], seg_recv.at[way, hop], beside[way])

    def twin(slot):
        return remote(
            segment.at[slot],
            segment.at[slot],
            twin_send.at[slot // 2],
            twin_recv.at[slot // 2],
            sibling,
        )

    for way in (RIGHT, LEFT):
        seg(way, 0).start()
    twin(exp).start()
    for hop in range(1, hops):
        for way in (RIGHT, LEFT):
            seg(way, hop - 1, True).wait_recv()
            seg(way, hop).start()
            twin(at_distance(1 - way, hop) * 2 + core).start()
    for way in (RIGHT, LEFT):
        seg(way, hops - 1, True).wait_recv()
    twin(at_distance(RIGHT, hops) * 2 + core).start()
    for half in (0, 1):
        own2[0, half] = outs[half].total()
        outs2[half].start()
        outs2[half].direct()
    each(0, z_count, lambda i: twin(i * 2 + 1 - core).wait_recv())
    grad = drive
    grad[...] = contract_last(
        segment[...].reshape(seg_rows, width), wout_ref[...]
    ) * silu(z_ref[...].astype(f32))

    for r in outs2:
        r.middle()

    def back_end_step(t, tile, line, h):
        return decay_of(line, tile) * (h + crep_ref[t] * line[1]), None

    done = scan_tokens(
        seg_rows, channels, (delta_ref, grad), back_end_step, zero_state(rate_ref), backward=True
    )
    for tile, h in zip(tiles_of(channels), done):
        back16[:, tile] = h.astype(bf16)
    backs.start(0, ctx)
    sent = [r.total() for r in outs2]
    give_back(OUT, lambda tile: jnp.concatenate([v[:, tile] for v in sent], axis=0))
    moves[OUT].start()

    def back_step(t, tile, line, h):
        new = h + crep_ref[t] * line[1]
        return decay_of(line, tile) * new, jnp.sum(brep_ref[t] * new, axis=0, keepdims=True)

    scan_tokens(
        seg_rows,
        channels,
        (delta_ref, grad),
        back_step,
        joined(back_box, False),
        y,
        backward=True,
    )
    gradu_ref[...] = (delta_ref[...] * y[...] + skip_ref[...] * grad[...]).astype(bf16)
    moves[OUT].wait()
    final_ref[...] = (
        stream[...]
        + columns[0] * combined(OUT, placet_ref[0])
        + columns[1] * combined(OUT, placet_ref[1])
    ).astype(bf16)

    for array in (0, 1):
        for g in near_gathers[array] + far_gathers[array]:
            g.finish()
    for r in grads + outs + grads2 + outs2:
        r.finish()
    for m in moves:
        m.finish()
    pair.wait_send()
    totals.finish(0, ctx)
    totals.finish(ctx + 1, ctx_count)
    ends.finish(ctx + 1, ctx_count)
    backs.finish(0, ctx)
    for way in (RIGHT, LEFT):
        for hop in range(hops):
            mix(way, hop).wait_send()
            seg(way, hop).wait_send()
    each(0, z_count, lambda i: twin(i * 2 + core).wait_send())


def settle_kernel(*refs):
    half = len(refs) // 2
    for source, target in zip(refs[:half], refs[half:]):
        target[...] = source[...]


def settle(values):
    return pl.pallas_call(
        settle_kernel,
        out_shape=[jax.ShapeDtypeStruct(v.shape, v.dtype) for v in values],
        in_specs=[VMEM] * len(values),
        out_specs=[VMEM] * len(values),
    )(*values)


def layer(args, exp_count, ctx_count):
    delta, rate, resid = args[0], args[5], args[8]
    seg_rows, channels = delta.shape
    states = rate.shape[0]
    my_rows, width = resid.shape
    bf16, f32 = jnp.bfloat16, jnp.float32
    slots = 4 * my_rows // exp_count
    half = exp_count * slots // 2
    vm, dma = pltpu.VMEM, pltpu.SemaphoreType.DMA
    full = vm((2, 2, SIDE, SIDE, half, width), bf16)
    plane = vm((seg_rows, channels), f32)
    slab = vm((4, exp_count, 4 * slots, width // 4), bf16)
    state_box = vm((ctx_count, states, channels), bf16)
    shape = jax.ShapeDtypeStruct
    return pl.pallas_call(
        layer_kernel,
        out_shape=[
            shape((my_rows, width), bf16),
            shape((my_rows, width), bf16),
            shape((seg_rows, channels), bf16),
        ],
        in_specs=[
            pl.BlockSpec(memory_space=pl.ANY) if i in (7, 12, 13, 14) else VMEM
            for i in range(len(args))
        ],
        out_specs=[VMEM] * 3,
        scratch_shapes=[
            vm((seg_rows, states, LANES), f32),
            vm((seg_rows, states, LANES), f32),
            vm((states, channels), f32),
            *[vm(args[i].shape, bf16) for i in (7, 12, 13, 14)],
            dma((4,)),
            vm((2, 4 * exp_count * slots, 4 * my_rows), bf16),
            vm((2, 4 * my_rows, 4 * exp_count * slots), bf16),
            plane,
            plane,
            vm((seg_rows, channels), bf16),
            vm((states, channels), bf16),
            vm((states, channels), bf16),
            vm((1, channels), f32),
            state_box,
            vm((ctx_count, 1, channels), f32),
            state_box,
            dma((3, ctx_count)),
            dma((3, ctx_count)),
            vm((2, exp_count // 2, my_rows, width), bf16),
            vm((exp_count // 2, my_rows, width), bf16),
            dma((1,)),
            dma((1,)),
            vm((2, exp_count // 4, my_rows, width), bf16),
            dma((2, exp_count // 4)),
            dma((2, exp_count // 4)),
            slab,
            slab,
            dma((4, exp_count)),
            dma((4, exp_count)),
            vm((my_rows, width), f32),
            vm((exp_count, my_rows, width), bf16),
            dma((2, exp_count // 4)),
            dma((2, exp_count // 4)),
            dma((exp_count // 2,)),
            dma((exp_count // 2,)),
            full,
            full,
            vm((2, 2, 2, SIDE // 2, half, width), bf16),
            vm((2, 2, 2, SIDE, half, width), bf16),
            vm((2, 2, SIDE, half, width), bf16),
            vm((2, 2, 2, half // 2, width), bf16),
            vm((2, 2, 2, half, width), bf16),
            dma((2, 2, 4, 2 + 2 * SIDE)),
            dma((2, 2, 4, 2 + 2 * SIDE)),
        ],
        compiler_params=pltpu.CompilerParams(
            vmem_limit_bytes=60 * 1024 * 1024, collective_id=1, has_side_effects=True
        ),
    )(*args)


def local(
    u_in,
    z_gate,
    delta,
    b_in,
    c_in,
    rate,
    skip,
    w_out,
    resid,
    gain,
    expert_ids,
    route_weights,
    w_gate,
    w_up,
    w_down,
    d_out,
):
    return tuple(
        settle(
            layer(
                (
                    delta,
                    u_in,
                    z_gate,
                    b_in.T,
                    c_in.T,
                    rate,
                    skip[None, :],
                    w_out,
                    resid,
                    gain[None, :],
                    expert_ids.T,
                    route_weights.T,
                    w_gate[0],
                    w_up[0],
                    w_down[0],
                    d_out,
                ),
                lax.axis_size("exp"),
                lax.axis_size("ctx"),
            )
        )
    )


def solution(mesh):
    return jax.shard_map(
        local,
        mesh=mesh,
        in_specs=(
            P("ctx", "exp"),
            P("ctx", "exp"),
            P("ctx", "exp"),
            P("ctx", None),
            P("ctx", None),
            P(None, "exp"),
            P("exp"),
            P("exp", None),
            P(("ctx", "exp"), None),
            P(),
            P(("ctx", "exp"), None),
            P(("ctx", "exp"), None),
            P("exp", None, "ctx"),
            P("exp", None, "ctx"),
            P("exp", "ctx", None),
            P(("ctx", "exp"), None),
        ),
        out_specs=(P(("ctx", "exp"), None), P(("ctx", "exp"), None), P("ctx", "exp")),
        check_vma=False,
    )
```

```python
import functools
import math

import jax
import jax.numpy as jnp
from jax import lax
from jax.experimental import pallas as pl
from jax.experimental.pallas import tpu as pltpu
from jax.sharding import PartitionSpec as P

LANES = 128
VMEM = pl.BlockSpec(memory_space=pltpu.VMEM)


def contract_last(left, right):
    return lax.dot_general(
        left, right, (((1,), (1,)), ((), ())), preferred_element_type=jnp.float32
    )


def silu(v):
    return v * (1.0 / (1.0 + jnp.exp(-v)))


def tiles_of(channels):
    return [slice(i * LANES, (i + 1) * LANES) for i in range(channels // LANES)]


GROUP = 8


def scan_tokens(rows, channels, planes, step, initial, out_ref=None, backward=False):
    tiles = tiles_of(channels)
    row_index = lax.broadcasted_iota(jnp.int32, (GROUP, LANES), 0)

    def group(i, carried):
        base = rows - GROUP - i * GROUP if backward else i * GROUP
        base = pl.multiple_of(base, GROUP)
        blocks = [[plane[pl.ds(base, GROUP), tile] for plane in planes] for tile in tiles]
        made = [jnp.zeros((GROUP, LANES), jnp.float32) for _ in tiles]
        carried = list(carried)
        for j in reversed(range(GROUP)) if backward else range(GROUP):
            for k, tile in enumerate(tiles):
                line = [b[j : j + 1] for b in blocks[k]]
                carried[k], row = step(base + j, tile, line, carried[k])
                if out_ref is not None:
                    made[k] = jnp.where(row_index == j, row, made[k])
        if out_ref is not None:
            for k, tile in enumerate(tiles):
                out_ref[pl.ds(base, GROUP), tile] = made[k]
        return tuple(carried)

    return lax.fori_loop(0, rows // GROUP, group, tuple(initial))


def zero_state(rate_ref):
    states, channels = rate_ref.shape
    return [jnp.zeros((states, LANES), jnp.float32) for _ in tiles_of(channels)]


SIDE = 4
class Ring:
    def __init__(self, along_x):
        c = lax.axis_index("ctx")
        x, y = c // SIDE, c % SIDE
        self.place = x if along_x else y
        up, down = (self.place + 1) % SIDE, (self.place + SIDE - 1) % SIDE
        self.after, self.before, self.across = up, down, (self.place + 2) % SIDE
        self.right = {"ctx": up * SIDE + y if along_x else x * SIDE + up}
        self.left = {"ctx": down * SIDE + y if along_x else x * SIDE + down}


def halves(ref):
    n = ref.shape[0] // 2
    return ref.at[pl.ds(0, n)], ref.at[pl.ds(n, n)]


class Gather:
    def __init__(self, ring, block, pieces, send, recv):
        self.ring, self.block, self.pieces, self.send, self.recv = ring, block, pieces, send, recv

    def copy(self, ref, rightward, sem):
        return pltpu.make_async_remote_copy(
            src_ref=ref,
            dst_ref=ref,
            send_sem=self.send.at[sem],
            recv_sem=self.recv.at[sem],
            device_id=self.ring.right if rightward else self.ring.left,
            device_id_type=pl.DeviceIdType.MESH,
        )

    def piece(self, place, rightward, i):
        ref = self.block(place)
        ref = ref if self.pieces == 1 else ref.at[i]
        return self.copy(ref, rightward, 2 + i if rightward else 2 + self.pieces + i)

    def on(self, place, rightward):
        return self.copy(halves(self.block(place))[0 if rightward else 1], rightward, 0 if rightward else 1)

    def start(self, i=0):
        for rightward in (True, False):
            self.piece(self.ring.place, rightward, i).start()

    def before(self):
        for i in range(self.pieces):
            self.piece(self.ring.before, True, i).wait_recv()
        self.on(self.ring.before, True).start()

    def after(self):
        for i in range(self.pieces):
            self.piece(self.ring.after, False, i).wait_recv()
        self.on(self.ring.after, False).start()

    def across(self):
        for rightward in (True, False):
            self.on(self.ring.across, rightward).wait_recv()

    def finish(self):
        for rightward in (True, False):
            for i in range(self.pieces):
                self.piece(self.ring.place, rightward, i).wait_send()
        self.on(self.ring.before, True).wait_send()
        self.on(self.ring.after, False).wait_send()


def add_into(total, term):
    total[...] = (total[...].astype(jnp.float32) + term[...].astype(jnp.float32)).astype(
        total.dtype
    )


FAR_RIGHT, FAR_LEFT, ON_RIGHT, ON_LEFT, DIRECT_RIGHT, DIRECT_LEFT = range(6)


class Reduce:
    def __init__(self, ring, part, far, near, send, recv):
        self.ring, self.part, self.far, self.near = ring, part, far, near
        self.send, self.recv = send, recv

    def copy(self, way):
        ring = self.ring
        source, target = {
            FAR_RIGHT: lambda: (halves(self.part(ring.across))[0], self.far.at[0]),
            FAR_LEFT: lambda: (halves(self.part(ring.across))[1], self.far.at[1]),
            ON_RIGHT: lambda: (halves(self.part(ring.after))[0], halves(self.near.at[0])[0]),
            ON_LEFT: lambda: (halves(self.part(ring.before))[1], halves(self.near.at[1])[1]),
            DIRECT_RIGHT: lambda: (halves(self.part(ring.after))[1], halves(self.near.at[0])[1]),
            DIRECT_LEFT: lambda: (halves(self.part(ring.before))[0], halves(self.near.at[1])[0]),
        }[way]()
        rightward = way in (FAR_RIGHT, ON_RIGHT, DIRECT_RIGHT)
        return pltpu.make_async_remote_copy(
            src_ref=source,
            dst_ref=target,
            send_sem=self.send.at[way],
            recv_sem=self.recv.at[way],
            device_id=ring.right if rightward else ring.left,
            device_id_type=pl.DeviceIdType.MESH,
        )

    def start(self):
        self.copy(FAR_RIGHT).start()
        self.copy(FAR_LEFT).start()

    def direct(self):
        self.copy(DIRECT_RIGHT).start()
        self.copy(DIRECT_LEFT).start()

    def middle(self):
        self.copy(FAR_RIGHT).wait_recv()
        add_into(halves(self.part(self.ring.after))[0], self.far.at[0])
        self.copy(ON_RIGHT).start()
        self.copy(FAR_LEFT).wait_recv()
        add_into(halves(self.part(self.ring.before))[1], self.far.at[1])
        self.copy(ON_LEFT).start()

    def total(self):
        for way in (ON_RIGHT, ON_LEFT, DIRECT_RIGHT, DIRECT_LEFT):
            self.copy(way).wait_recv()
        f32 = jnp.float32
        own = self.part(self.ring.place)
        return (
            own[...].astype(f32) + self.near[0].astype(f32) + self.near[1].astype(f32)
        ).astype(own.dtype)

    def finish(self):
        for way in range(6):
            self.copy(way).wait_send()


def greet(axes):
    barrier = pltpu.get_barrier_semaphore()
    total = 0
    for axis in axes:
        count = lax.axis_size(axis)
        me = lax.axis_index(axis)

        def signal(d, carried):
            pl.semaphore_signal(
                barrier,
                inc=1,
                device_id={axis: (me + d) % count},
                device_id_type=pl.DeviceIdType.MESH,
            )
            return carried

        lax.fori_loop(1, count, signal, 0)
        total += count - 1
    return lambda: pl.semaphore_wait(barrier, total)


def remote(source, target, send, recv, device):
    return pltpu.make_async_remote_copy(
        src_ref=source,
        dst_ref=target,
        send_sem=send,
        recv_sem=recv,
        device_id=device,
        device_id_type=pl.DeviceIdType.MESH,
    )


def each(low, high, body):
    def step(i, carried):
        body(i)
        return carried

    lax.fori_loop(low, high, step, 0)


class Exchange:
    def __init__(self, source, box, send, recv):
        self.source, self.box, self.send, self.recv = source, box, send, recv
        self.me, self.count = lax.axis_index("exp"), lax.axis_size("exp")

    def copy(self, other, slot):
        return remote(
            self.source.at[other],
            self.box.at[slot],
            self.send.at[other],
            self.recv.at[slot],
            {"exp": other},
        )

    def start(self):
        self.box[self.me] = self.source[self.me]
        each(1, self.count, lambda d: self.copy((self.me + d) % self.count, self.me).start())

    def wait(self):
        def one(d):
            other = (self.me + d) % self.count
            self.copy(other, other).wait_recv()

        each(1, self.count, one)

    def finish(self):
        each(1, self.count, lambda d: self.copy((self.me + d) % self.count, self.me).wait_send())


class Spread:
    def __init__(self, source, box, send, recv):
        self.source, self.box, self.send, self.recv = source, box, send, recv
        self.me = lax.axis_index("ctx")

    def copy(self, other, slot):
        return remote(
            self.source,
            self.box.at[slot],
            self.send.at[other],
            self.recv.at[slot],
            {"ctx": other},
        )

    def start(self, low, high):
        each(low, high, lambda other: self.copy(other, self.me).start())

    def wait_one(self, other):
        self.copy(other, other).wait_recv()

    def finish(self, low, high):
        each(low, high, lambda other: self.copy(other, self.me).wait_send())


def regroup(quarter, rows, slots, transposed):
    size = (rows * 4, rows) if transposed else (rows, rows * 4)
    row = lax.broadcasted_iota(jnp.int32, size, 1 if transposed else 0)
    slab = lax.broadcasted_iota(jnp.int32, size, 0 if transposed else 1)
    place = (row // slots) * (4 * slots) + quarter * slots + row % slots
    return jnp.where(slab == place, 1.0, 0.0).astype(jnp.bfloat16)


def quarters(value):
    step = value.shape[-1] // 4
    return jnp.concatenate([value[:, q * step : (q + 1) * step] for q in range(4)], axis=0)


def whole(value):
    step = value.shape[0] // 4
    return jnp.concatenate([value[q * step : (q + 1) * step] for q in range(4)], axis=1)


def as_column(row):
    count = row.shape[1]
    line = lax.broadcasted_iota(jnp.int32, (count, count), 0)
    column = lax.broadcasted_iota(jnp.int32, (count, count), 1)
    return jnp.sum(jnp.where(line == column, row, 0.0), axis=1, keepdims=True)


def make_places(ids_ref, place_ref, placet_ref, experts, slots, tokens):
    f32, i32 = jnp.float32, jnp.int32
    iota = lax.broadcasted_iota
    ids = [as_column(ids_ref[k : k + 1, :].astype(f32)) for k in (0, 1)]
    names = iota(i32, (tokens, experts), 1).astype(f32)
    onehot = [jnp.where(names == c, 1.0, 0.0) for c in ids]
    earlier = iota(i32, (tokens, tokens), 0) > iota(i32, (tokens, tokens), 1)
    before = jnp.dot(
        jnp.where(earlier, 1.0, 0.0).astype(jnp.bfloat16),
        (onehot[0] + onehot[1]).astype(jnp.bfloat16),
        preferred_element_type=f32,
    )
    slab = 4 * slots

    def codes(size, axis):
        row = iota(i32, size, axis)
        return ((row // slab) * slots + row % slots).astype(f32), (row % slab) // slots

    wide = 4 * experts * slots
    for k in (0, 1):
        target = ids[k] * slots + jnp.sum(before * onehot[k], axis=1, keepdims=True)
        place = iota(i32, (tokens, 4 * tokens), 1) % tokens
        own = place == iota(i32, (tokens, 4 * tokens), 0)
        target_row = jnp.sum(jnp.where(own, target, 0.0), axis=0, keepdims=True)
        code, quarter = codes((wide, 4 * tokens), 0)
        same = quarter == iota(i32, (wide, 4 * tokens), 1) // tokens
        place_ref[k] = jnp.where(
            jnp.logical_and(same, code == target_row), 1.0, 0.0
        ).astype(place_ref.dtype)
        code, quarter = codes((4 * tokens, wide), 1)
        same = quarter == iota(i32, (4 * tokens, wide), 0) // tokens
        target_column = jnp.concatenate([target] * 4, axis=0)
        placet_ref[k] = jnp.where(
            jnp.logical_and(same, code == target_column), 1.0, 0.0
        ).astype(placet_ref.dtype)


def spread_lanes(source_ref, target_ref):
    states, count = source_ref.shape

    def some(i, carried):
        for part in range(count // LANES):
            lanes = source_ref[:, part * LANES : (part + 1) * LANES]
            turned = pltpu.roll(lanes, (LANES - i * GROUP) % LANES, 1)
            for j in range(GROUP):
                target_ref[part * LANES + i * GROUP + j] = jnp.broadcast_to(
                    turned[:, j : j + 1], (states, LANES)
                )
        return carried

    lax.fori_loop(0, LANES // GROUP, some, 0)


def layer_kernel(
    delta_ref,
    u_ref,
    z_ref,
    b_ref,
    c_ref,
    plain_rate_ref,
    skip_ref,
    wout_hbm,
    resid_ref,
    gain_ref,
    ids_ref,
    weight_ref,
    wg_hbm,
    wu_hbm,
    wd_hbm,
    dout_ref,
    final_ref,
    gresid_ref,
    gradu_ref,
    brep_ref,
    crep_ref,
    rate_ref,
    wout_ref,
    wg_ref,
    wu_ref,
    wd_ref,
    weight_sem,
    place_ref,
    placet_ref,
    drive,
    y,
    gated,
    end16,
    back16,
    sums,
    end_box,
    sum_box,
    back_box,
    state_send,
    state_recv,
    mixed,
    pair_box,
    pair_send,
    pair_recv,
    mix_box,
    mix_send,
    mix_recv,
    slabs,
    boxes,
    slab_send,
    slab_recv,
    stream,
    segment,
    seg_send,
    seg_recv,
    twin_send,
    twin_recv,
    held,
    parts,
    far,
    near,
    own2,
    far2,
    near2,
    send,
    recv,
):
    f32 = jnp.float32
    bf16 = jnp.bfloat16
    ring_x, ring_y = Ring(True), Ring(False)
    first = (ring_x, ring_y)
    second = (ring_y, ring_x)
    rows, width = held.shape[-2], held.shape[-1]
    seg_rows, channels = delta_ref.shape
    ctx, ctx_count = lax.axis_index("ctx"), lax.axis_size("ctx")
    exp, exp_count = lax.axis_index("exp"), lax.axis_size("exp")
    z, core = exp // 2, exp % 2
    z_count = exp_count // 2
    sibling = {"exp": z * 2 + 1 - core}
    slots = 2 * rows // exp_count
    my_rows = resid_ref.shape[0]
    slab_rows = slabs.shape[2]
    slab_width = slabs.shape[3]
    COT, ROW, GRAD, OUT = range(4)
    moves = [Exchange(slabs.at[i], boxes.at[i], slab_send.at[i], slab_recv.at[i]) for i in range(4)]
    ends = Spread(end16, end_box, state_send.at[0], state_recv.at[0])
    totals = Spread(sums, sum_box, state_send.at[1], state_recv.at[1])
    backs = Spread(back16, back_box, state_send.at[2], state_recv.at[2])

    def to_slabs(kind, value):
        slabs[kind] = value.astype(bf16).reshape(exp_count, slab_rows, slab_width)

    def dispatched(kind):
        flat = boxes[kind].reshape(exp_count * slab_rows, slab_width)
        return [
            jnp.dot(
                regroup(q, 2 * rows, slots, False), flat, preferred_element_type=f32
            ).astype(bf16)
            for q in range(4)
        ]

    def give_back(kind, read):
        total = None
        for q in range(4):
            tile = slice(q * slab_width, (q + 1) * slab_width)
            term = jnp.dot(
                regroup(q, 2 * rows, slots, True), read(tile), preferred_element_type=f32
            )
            total = term if total is None else total + term
        to_slabs(kind, total)

    def gather(array, half, phase):
        if phase == 0:
            block = lambda i: held.at[array, half, second[half].place, i]
            ring, pieces = first[half], 1
        else:
            block = lambda i: held.at[array, half, i]
            ring, pieces = second[half], SIDE
        return Gather(ring, block, pieces, send.at[array, half, phase], recv.at[array, half, phase])

    near_gathers = [[gather(a, h, 0) for h in (0, 1)] for a in (0, 1)]
    far_gathers = [[gather(a, h, 1) for h in (0, 1)] for a in (0, 1)]

    def take_in(array, kind):
        for q, value in enumerate(dispatched(kind)):
            tile = slice(q * slab_width, (q + 1) * slab_width)
            for half in (0, 1):
                held[array, half, second[half].place, first[half].place, :, tile] = value[
                    half * rows : (half + 1) * rows
                ]
        for g in near_gathers[array]:
            g.start()
        for half in (0, 1):
            far_gathers[array][half].start(first[half].place)

    def spread_out(array):
        pairs = list(zip(near_gathers[array], far_gathers[array]))
        for g, h in pairs:
            g.before()
            g.after()
        for g, h in pairs:
            h.start(g.ring.before)
            h.start(g.ring.after)
        for g, h in pairs:
            g.across()
            h.start(g.ring.across)

    def reduces(array, phase):
        out = []
        for half in (0, 1):
            if phase == 0:
                part = functools.partial(lambda h, i: parts.at[array, h, i], half)
                ring, inbox = second[half], (far.at[array, half], near.at[array, half])
            else:
                part = functools.partial(lambda h, i: own2.at[array, h, i], half)
                ring, inbox = first[half], (far2.at[array, half], near2.at[array, half])
            out.append(
                Reduce(
                    ring,
                    part,
                    *inbox,
                    send.at[array, half, 2 + phase],
                    recv.at[array, half, 2 + phase],
                )
            )
        return out

    def decay_of(line, tile):
        return jnp.exp2(line[0] * rate_ref[:, tile])

    states = rate_ref.shape[0]

    def joined(box, low_first):
        tiles = tiles_of(channels)

        def one(i, carried):
            gap, held_state = carried
            other = ctx - 1 - i if low_first else ctx + 1 + i
            (ends if low_first else backs).wait_one(other)
            totals.wait_one(other)
            made = tuple(
                h
                + jnp.exp2(gap[:, tile] * rate_ref[:, tile]) * box[other, :, tile].astype(f32)
                for tile, h in zip(tiles, held_state)
            )
            return gap + sum_box[other], made

        count = ctx if low_first else ctx_count - 1 - ctx
        zero = tuple(jnp.zeros((states, LANES), f32) for _ in tiles)
        return lax.fori_loop(0, count, one, (jnp.zeros((1, channels), f32), zero))[1]

    fetches = [
        pltpu.make_async_copy(source, target, weight_sem.at[i])
        for i, (source, target) in enumerate(
            ((wout_hbm, wout_ref), (wd_hbm, wd_ref), (wg_hbm, wg_ref), (wu_hbm, wu_ref))
        )
    ]
    arrived = greet(("ctx", "exp"))
    for f in fetches:
        f.start()
    sums[...] = jnp.sum(delta_ref[...], axis=0, keepdims=True)
    rate_ref[...] = plain_rate_ref[...] * (-math.log2(math.e))
    make_places(ids_ref, place_ref, placet_ref, exp_count, slots, my_rows)
    columns = [as_column(weight_ref[k : k + 1, :]) for k in (0, 1)]
    d_out = dout_ref[...].astype(f32)
    to_slabs(
        COT,
        sum(
            jnp.dot(
                place_ref[k],
                quarters((columns[k] * d_out).astype(bf16)),
                preferred_element_type=f32,
            )
            for k in (0, 1)
        ),
    )
    spread_lanes(b_ref, brep_ref)
    drive[...] = delta_ref[...] * u_ref[...].astype(f32)
    arrived()
    totals.start(0, ctx)
    totals.start(ctx + 1, ctx_count)
    moves[COT].start()

    def end_step(t, tile, line, h):
        return decay_of(line, tile) * h + brep_ref[t] * line[1], None

    done = scan_tokens(seg_rows, channels, (delta_ref, drive), end_step, zero_state(rate_ref))
    for tile, h in zip(tiles_of(channels), done):
        end16[:, tile] = h.astype(bf16)
    ends.start(ctx + 1, ctx_count)
    spread_lanes(c_ref, crep_ref)
    moves[COT].wait()
    take_in(1, COT)

    def out_step(t, tile, line, h):
        new = decay_of(line, tile) * h + brep_ref[t] * line[1]
        return new, jnp.sum(crep_ref[t] * new, axis=0, keepdims=True)

    scan_tokens(seg_rows, channels, (delta_ref, drive), out_step, joined(end_box, True), y)
    gated[...] = (
        (y[...] + skip_ref[...] * u_ref[...].astype(f32)) * silu(z_ref[...].astype(f32))
    ).astype(bf16)
    step = 512
    fetches[0].wait()
    for n in range(width // step):
        tile = slice(n * step, (n + 1) * step)
        value = (
            jnp.dot(gated[...], wout_ref[:, tile], preferred_element_type=f32)
            .astype(bf16)
            .reshape(z_count, 2, my_rows, step)
        )
        for k in (0, 1):
            mixed[k, :, :, tile] = value[:, k]
    RIGHT, LEFT = 0, 1
    hops = z_count // 2
    middle = width // 2
    beside = [
        {"exp": ((z + 1) % z_count) * 2 + core},
        {"exp": ((z + z_count - 1) % z_count) * 2 + core},
    ]

    def at_distance(way, far_by):
        return (z + far_by) % z_count if way == RIGHT else (z + z_count - far_by) % z_count

    def side(ref, lane):
        return ref.at[:, pl.ds(lane * middle, middle)]

    def pair(j):
        return remote(
            mixed.at[1 - core, j], pair_box.at[j], pair_send.at[j], pair_recv.at[j], sibling
        )

    order = [(RIGHT, hops)] + [(w, d) for d in range(hops - 1, 0, -1) for w in (RIGHT, LEFT)]
    order = [at_distance(w, d) for w, d in order] + [z]
    for j in order:
        pair(j).start()

    def paired(j):
        pair(j).wait_recv()
        add_into(mixed.at[core, j], pair_box.at[j])

    def mix(way, hop, lane):
        return remote(
            side(mixed.at[core, at_distance(way, hops - hop)], lane),
            side(mix_box.at[way, hop], lane),
            mix_send.at[way, hop, lane],
            mix_recv.at[way, hop, lane],
            beside[way],
        )

    def mix_on(way, hop, lane):
        mix(way, hop - 1, lane).wait_recv()
        add_into(
            side(mixed.at[core, at_distance(way, hops - hop)], lane),
            side(mix_box.at[way, hop - 1], lane),
        )
        mix(way, hop, lane).start()

    paired(order[0])
    for way in (RIGHT, LEFT):
        mix(way, 0, way).start()
    for way in (RIGHT, LEFT):
        paired(order[1 + way])
        mix(way, 1, 1 - way).start()
    for j in order[3:]:
        paired(j)
    for hop in range(1, hops):
        for way in (RIGHT, LEFT):
            mix_on(way, hop, way)
        if hop < hops - 1:
            for way in (RIGHT, LEFT):
                mix_on(way, hop + 1, 1 - way)
        if hop == 1:
            spread_out(1)
    for way in (RIGHT, LEFT):
        for lane in (0, 1):
            mix(way, hops - 1, lane).wait_recv()
    stream[...] = (
        resid_ref[...].astype(f32)
        + mixed[core, z].astype(f32)
        + mix_box[RIGHT, hops - 1].astype(f32)
        + mix_box[LEFT, hops - 1].astype(f32)
    )
    flow = stream[...]
    inverse = lax.rsqrt(jnp.mean(flow * flow, axis=-1, keepdims=True) + 1e-05)
    normed = (flow * inverse * gain_ref[...]).astype(bf16)
    spread = place_ref[0] + place_ref[1]
    to_slabs(ROW, jnp.dot(spread, quarters(normed), preferred_element_type=f32))
    moves[ROW].start()
    for g in far_gathers[1]:
        g.before()
        g.after()
    moves[ROW].wait()
    take_in(0, ROW)
    spread_out(0)

    for f in fetches[1:]:
        f.wait()
    both = SIDE * rows

    def group(k, carried):
        @pl.when(k == 0)
        def _():
            for g in far_gathers[1]:
                g.across()

        @pl.when(k == 1)
        def _():
            for g in far_gathers[0]:
                g.before()
                g.after()

        @pl.when(k == 3)
        def _():
            for g in far_gathers[0]:
                g.across()
            for r in reduces(1, 0):
                r.direct()

        shift = jnp.where(k == 0, 0, jnp.where(k == 1, SIDE - 1, jnp.where(k == 2, 1, 2)))
        places = [(second[h].place + shift) % SIDE for h in (0, 1)]

        def taken(array):
            return jnp.concatenate(
                [held[array, h, places[h]].reshape(both, width) for h in (0, 1)], axis=0
            )

        def put(array, tile, value):
            value = value.astype(bf16)
            for h in (0, 1):
                parts[array, h, places[h], :, :, tile] = value[
                    h * both : (h + 1) * both
                ].reshape(SIDE, rows, -1)

        x = taken(0)
        gate = jnp.dot(x, wg_ref[...], preferred_element_type=f32)
        up = jnp.dot(x, wu_ref[...], preferred_element_type=f32)
        hidden_grad = contract_last(taken(1), wd_ref[...])
        sigma = 1.0 / (1.0 + jnp.exp(-gate))
        active = gate * sigma
        hidden = (active * up).astype(bf16)
        gate_grad = (hidden_grad * up * sigma * (1.0 + gate * (1.0 - sigma))).astype(bf16)
        up_grad = (hidden_grad * active).astype(bf16)
        for n in range(width // step):
            tile = slice(n * step, (n + 1) * step)
            put(
                1,
                tile,
                contract_last(gate_grad, wg_ref[tile, :]) + contract_last(up_grad, wu_ref[tile, :]),
            )

        @pl.when(k == 3)
        def _():
            for r in reduces(1, 0):
                r.start()

        for n in range(width // step):
            tile = slice(n * step, (n + 1) * step)
            put(0, tile, jnp.dot(hidden, wd_ref[:, tile], preferred_element_type=f32))
        return carried

    lax.fori_loop(0, SIDE, group, 0)
    grads, outs = reduces(1, 0), reduces(0, 0)
    grads2, outs2 = reduces(1, 1), reduces(0, 1)
    for r in grads:
        r.middle()
    for half in (0, 1):
        own2[1, half] = grads[half].total()
        grads2[half].start()
        grads2[half].direct()
    for r in grads2:
        r.middle()
    for r in outs:
        r.start()
        r.direct()
    sent = [r.total() for r in grads2]
    give_back(GRAD, lambda tile: jnp.concatenate([v[:, tile] for v in sent], axis=0))
    moves[GRAD].start()
    for r in outs:
        r.middle()
    moves[GRAD].wait()

    def combined(kind, matrix):
        flat = boxes[kind].reshape(exp_count * slab_rows, slab_width)
        return whole(jnp.dot(matrix, flat, preferred_element_type=f32))

    scaled = combined(GRAD, placet_ref[0] + placet_ref[1]) * gain_ref[...]
    flow = stream[...]
    inverse = lax.rsqrt(jnp.mean(flow * flow, axis=-1, keepdims=True) + 1e-05)
    project = jnp.mean(scaled * flow, axis=-1, keepdims=True)
    grad_rows = (
        dout_ref[...].astype(f32) + inverse * (scaled - flow * inverse * inverse * project)
    ).astype(bf16)
    gresid_ref[...] = grad_rows
    segment[exp] = grad_rows

    def seg(way, hop, lane, came=False):
        block = segment.at[at_distance(1 - way, hop + (1 if came else 0)) * 2 + core]
        block = side(block, lane)
        return remote(
            block, block, seg_send.at[way, hop, lane], seg_recv.at[way, hop, lane], beside[way]
        )

    def twin(slot):
        return remote(
            segment.at[slot],
            segment.at[slot],
            twin_send.at[slot // 2],
            twin_recv.at[slot // 2],
            sibling,
        )

    for lane in (0, 1):
        for way in (RIGHT, LEFT):
            seg(way, 0, lane if way == LEFT else 1 - lane).start()
    twin(exp).start()
    for hop in range(1, hops):
        for lane in (0, 1):
            for way in (RIGHT, LEFT):
                now = lane if way == LEFT else 1 - lane
                seg(way, hop - 1, now, True).wait_recv()
                if hop < hops - 1 or now == way:
                    seg(way, hop, now).start()
        for way in (RIGHT, LEFT):
            twin(at_distance(1 - way, hop) * 2 + core).start()
    for half in (0, 1):
        own2[0, half] = outs[half].total()
        outs2[half].start()
        outs2[half].direct()
    for way in (RIGHT, LEFT):
        seg(way, hops - 1, way, True).wait_recv()
    twin(at_distance(RIGHT, hops) * 2 + core).start()
    each(0, z_count, lambda i: twin(i * 2 + 1 - core).wait_recv())
    grad = drive
    grad[...] = contract_last(
        segment[...].reshape(seg_rows, width), wout_ref[...]
    ) * silu(z_ref[...].astype(f32))

    for r in outs2:
        r.middle()

    def back_end_step(t, tile, line, h):
        return decay_of(line, tile) * (h + crep_ref[t] * line[1]), None

    done = scan_tokens(
        seg_rows, channels, (delta_ref, grad), back_end_step, zero_state(rate_ref), backward=True
    )
    for tile, h in zip(tiles_of(channels), done):
        back16[:, tile] = h.astype(bf16)
    backs.start(0, ctx)
    sent = [r.total() for r in outs2]
    give_back(OUT, lambda tile: jnp.concatenate([v[:, tile] for v in sent], axis=0))
    moves[OUT].start()

    def back_step(t, tile, line, h):
        new = h + crep_ref[t] * line[1]
        return decay_of(line, tile) * new, jnp.sum(brep_ref[t] * new, axis=0, keepdims=True)

    scan_tokens(
        seg_rows,
        channels,
        (delta_ref, grad),
        back_step,
        joined(back_box, False),
        y,
        backward=True,
    )
    gradu_ref[...] = (delta_ref[...] * y[...] + skip_ref[...] * grad[...]).astype(bf16)
    moves[OUT].wait()
    final_ref[...] = (
        stream[...]
        + columns[0] * combined(OUT, placet_ref[0])
        + columns[1] * combined(OUT, placet_ref[1])
    ).astype(bf16)

    for array in (0, 1):
        for g in near_gathers[array] + far_gathers[array]:
            g.finish()
    for r in grads + outs + grads2 + outs2:
        r.finish()
    for m in moves:
        m.finish()
    each(0, z_count, lambda j: pair(j).wait_send())
    totals.finish(0, ctx)
    totals.finish(ctx + 1, ctx_count)
    ends.finish(ctx + 1, ctx_count)
    backs.finish(0, ctx)
    for way in (RIGHT, LEFT):
        for hop in range(hops):
            for lane in (0, 1):
                if hop > 0 or lane == way:
                    mix(way, hop, lane).wait_send()
                if hop < hops - 1 or lane == way:
                    seg(way, hop, lane).wait_send()
    each(0, z_count, lambda i: twin(i * 2 + core).wait_send())


def settle_kernel(*refs):
    half = len(refs) // 2
    for source, target in zip(refs[:half], refs[half:]):
        target[...] = source[...]


def settle(values):
    return pl.pallas_call(
        settle_kernel,
        out_shape=[jax.ShapeDtypeStruct(v.shape, v.dtype) for v in values],
        in_specs=[VMEM] * len(values),
        out_specs=[VMEM] * len(values),
    )(*values)


def layer(args, exp_count, ctx_count):
    delta, rate, resid = args[0], args[5], args[8]
    seg_rows, channels = delta.shape
    states = rate.shape[0]
    my_rows, width = resid.shape
    bf16, f32 = jnp.bfloat16, jnp.float32
    slots = 4 * my_rows // exp_count
    half = exp_count * slots // 2
    vm, dma = pltpu.VMEM, pltpu.SemaphoreType.DMA
    full = vm((2, 2, SIDE, SIDE, half, width), bf16)
    plane = vm((seg_rows, channels), f32)
    slab = vm((4, exp_count, 4 * slots, width // 4), bf16)
    state_box = vm((ctx_count, states, channels), bf16)
    shape = jax.ShapeDtypeStruct
    return pl.pallas_call(
        layer_kernel,
        out_shape=[
            shape((my_rows, width), bf16),
            shape((my_rows, width), bf16),
            shape((seg_rows, channels), bf16),
        ],
        in_specs=[
            pl.BlockSpec(memory_space=pl.ANY) if i in (7, 12, 13, 14) else VMEM
            for i in range(len(args))
        ],
        out_specs=[VMEM] * 3,
        scratch_shapes=[
            vm((seg_rows, states, LANES), f32),
            vm((seg_rows, states, LANES), f32),
            vm((states, channels), f32),
            *[vm(args[i].shape, bf16) for i in (7, 12, 13, 14)],
            dma((4,)),
            vm((2, 4 * exp_count * slots, 4 * my_rows), bf16),
            vm((2, 4 * my_rows, 4 * exp_count * slots), bf16),
            plane,
            plane,
            vm((seg_rows, channels), bf16),
            vm((states, channels), bf16),
            vm((states, channels), bf16),
            vm((1, channels), f32),
            state_box,
            vm((ctx_count, 1, channels), f32),
            state_box,
            dma((3, ctx_count)),
            dma((3, ctx_count)),
            vm((2, exp_count // 2, my_rows, width), bf16),
            vm((exp_count // 2, my_rows, width), bf16),
            dma((exp_count // 2,)),
            dma((exp_count // 2,)),
            vm((2, exp_count // 4, my_rows, width), bf16),
            dma((2, exp_count // 4, 2)),
            dma((2, exp_count // 4, 2)),
            slab,
            slab,
            dma((4, exp_count)),
            dma((4, exp_count)),
            vm((my_rows, width), f32),
            vm((exp_count, my_rows, width), bf16),
            dma((2, exp_count // 4, 2)),
            dma((2, exp_count // 4, 2)),
            dma((exp_count // 2,)),
            dma((exp_count // 2,)),
            full,
            full,
            vm((2, 2, 2, SIDE // 2, half, width), bf16),
            vm((2, 2, 2, SIDE, half, width), bf16),
            vm((2, 2, SIDE, half, width), bf16),
            vm((2, 2, 2, half // 2, width), bf16),
            vm((2, 2, 2, half, width), bf16),
            dma((2, 2, 4, 2 + 2 * SIDE)),
            dma((2, 2, 4, 2 + 2 * SIDE)),
        ],
        compiler_params=pltpu.CompilerParams(
            vmem_limit_bytes=60 * 1024 * 1024, collective_id=1, has_side_effects=True
        ),
    )(*args)


def local(
    u_in,
    z_gate,
    delta,
    b_in,
    c_in,
    rate,
    skip,
    w_out,
    resid,
    gain,
    expert_ids,
    route_weights,
    w_gate,
    w_up,
    w_down,
    d_out,
):
    return tuple(
        settle(
            layer(
                (
                    delta,
                    u_in,
                    z_gate,
                    b_in.T,
                    c_in.T,
                    rate,
                    skip[None, :],
                    w_out,
                    resid,
                    gain[None, :],
                    expert_ids.T,
                    route_weights.T,
                    w_gate[0],
                    w_up[0],
                    w_down[0],
                    d_out,
                ),
                lax.axis_size("exp"),
                lax.axis_size("ctx"),
            )
        )
    )


def solution(mesh):
    return jax.shard_map(
        local,
        mesh=mesh,
        in_specs=(
            P("ctx", "exp"),
            P("ctx", "exp"),
            P("ctx", "exp"),
            P("ctx", None),
            P("ctx", None),
            P(None, "exp"),
            P("exp"),
            P("exp", None),
            P(("ctx", "exp"), None),
            P(),
            P(("ctx", "exp"), None),
            P(("ctx", "exp"), None),
            P("exp", None, "ctx"),
            P("exp", None, "ctx"),
            P("exp", "ctx", None),
            P(("ctx", "exp"), None),
        ),
        out_specs=(P(("ctx", "exp"), None), P(("ctx", "exp"), None), P("ctx", "exp")),
        check_vma=False,
    )
```

```python
import functools
import math

import jax
import jax.numpy as jnp
from jax import lax
from jax.experimental import pallas as pl
from jax.experimental.pallas import tpu as pltpu
from jax.sharding import PartitionSpec as P

LANES = 128
VMEM = pl.BlockSpec(memory_space=pltpu.VMEM)


def contract_last(left, right):
    return lax.dot_general(
        left, right, (((1,), (1,)), ((), ())), preferred_element_type=jnp.float32
    )


def silu(v):
    return v * (1.0 / (1.0 + jnp.exp(-v)))


def tiles_of(channels):
    return [slice(i * LANES, (i + 1) * LANES) for i in range(channels // LANES)]


GROUP = 8


def scan_tokens(rows, channels, planes, step, initial, out_ref=None, backward=False):
    tiles = tiles_of(channels)
    row_index = lax.broadcasted_iota(jnp.int32, (GROUP, LANES), 0)

    def group(i, carried):
        base = rows - GROUP - i * GROUP if backward else i * GROUP
        base = pl.multiple_of(base, GROUP)
        blocks = [[plane[pl.ds(base, GROUP), tile] for plane in planes] for tile in tiles]
        made = [jnp.zeros((GROUP, LANES), jnp.float32) for _ in tiles]
        carried = list(carried)
        for j in reversed(range(GROUP)) if backward else range(GROUP):
            for k, tile in enumerate(tiles):
                line = [b[j : j + 1] for b in blocks[k]]
                carried[k], row = step(base + j, tile, line, carried[k])
                if out_ref is not None:
                    made[k] = jnp.where(row_index == j, row, made[k])
        if out_ref is not None:
            for k, tile in enumerate(tiles):
                out_ref[pl.ds(base, GROUP), tile] = made[k]
        return tuple(carried)

    return lax.fori_loop(0, rows // GROUP, group, tuple(initial))


def zero_state(rate_ref):
    states, channels = rate_ref.shape
    return [jnp.zeros((states, LANES), jnp.float32) for _ in tiles_of(channels)]


SIDE = 4
class Ring:
    def __init__(self, along_x):
        c = lax.axis_index("ctx")
        x, y = c // SIDE, c % SIDE
        self.place = x if along_x else y
        up, down = (self.place + 1) % SIDE, (self.place + SIDE - 1) % SIDE
        self.after, self.before, self.across = up, down, (self.place + 2) % SIDE
        self.right = {"ctx": up * SIDE + y if along_x else x * SIDE + up}
        self.left = {"ctx": down * SIDE + y if along_x else x * SIDE + down}


def halves(ref):
    n = ref.shape[0] // 2
    return ref.at[pl.ds(0, n)], ref.at[pl.ds(n, n)]


class Gather:
    def __init__(self, ring, block, pieces, send, recv):
        self.ring, self.block, self.pieces, self.send, self.recv = ring, block, pieces, send, recv

    def copy(self, ref, rightward, sem):
        return pltpu.make_async_remote_copy(
            src_ref=ref,
            dst_ref=ref,
            send_sem=self.send.at[sem],
            recv_sem=self.recv.at[sem],
            device_id=self.ring.right if rightward else self.ring.left,
            device_id_type=pl.DeviceIdType.MESH,
        )

    def piece(self, place, rightward, i):
        ref = self.block(place)
        ref = ref if self.pieces == 1 else ref.at[i]
        return self.copy(ref, rightward, 2 + i if rightward else 2 + self.pieces + i)

    def on(self, place, rightward):
        return self.copy(halves(self.block(place))[0 if rightward else 1], rightward, 0 if rightward else 1)

    def start(self, i=0):
        for rightward in (True, False):
            self.piece(self.ring.place, rightward, i).start()

    def before(self):
        for i in range(self.pieces):
            self.piece(self.ring.before, True, i).wait_recv()
        self.on(self.ring.before, True).start()

    def after(self):
        for i in range(self.pieces):
            self.piece(self.ring.after, False, i).wait_recv()
        self.on(self.ring.after, False).start()

    def across(self):
        for rightward in (True, False):
            self.on(self.ring.across, rightward).wait_recv()

    def finish(self):
        for rightward in (True, False):
            for i in range(self.pieces):
                self.piece(self.ring.place, rightward, i).wait_send()
        self.on(self.ring.before, True).wait_send()
        self.on(self.ring.after, False).wait_send()


def add_into(total, term):
    total[...] = (total[...].astype(jnp.float32) + term[...].astype(jnp.float32)).astype(
        total.dtype
    )


FAR_RIGHT, FAR_LEFT, ON_RIGHT, ON_LEFT, DIRECT_RIGHT, DIRECT_LEFT = range(6)


class Reduce:
    def __init__(self, ring, part, far, near, send, recv):
        self.ring, self.part, self.far, self.near = ring, part, far, near
        self.send, self.recv = send, recv

    def copy(self, way):
        ring = self.ring
        source, target = {
            FAR_RIGHT: lambda: (halves(self.part(ring.across))[0], self.far.at[0]),
            FAR_LEFT: lambda: (halves(self.part(ring.across))[1], self.far.at[1]),
            ON_RIGHT: lambda: (halves(self.part(ring.after))[0], halves(self.near.at[0])[0]),
            ON_LEFT: lambda: (halves(self.part(ring.before))[1], halves(self.near.at[1])[1]),
            DIRECT_RIGHT: lambda: (halves(self.part(ring.after))[1], halves(self.near.at[0])[1]),
            DIRECT_LEFT: lambda: (halves(self.part(ring.before))[0], halves(self.near.at[1])[0]),
        }[way]()
        rightward = way in (FAR_RIGHT, ON_RIGHT, DIRECT_RIGHT)
        return pltpu.make_async_remote_copy(
            src_ref=source,
            dst_ref=target,
            send_sem=self.send.at[way],
            recv_sem=self.recv.at[way],
            device_id=ring.right if rightward else ring.left,
            device_id_type=pl.DeviceIdType.MESH,
        )

    def start(self):
        self.copy(FAR_RIGHT).start()
        self.copy(FAR_LEFT).start()

    def direct(self):
        self.copy(DIRECT_RIGHT).start()
        self.copy(DIRECT_LEFT).start()

    def middle(self):
        self.copy(FAR_RIGHT).wait_recv()
        add_into(halves(self.part(self.ring.after))[0], self.far.at[0])
        self.copy(ON_RIGHT).start()
        self.copy(FAR_LEFT).wait_recv()
        add_into(halves(self.part(self.ring.before))[1], self.far.at[1])
        self.copy(ON_LEFT).start()

    def total(self):
        for way in (ON_RIGHT, ON_LEFT, DIRECT_RIGHT, DIRECT_LEFT):
            self.copy(way).wait_recv()
        f32 = jnp.float32
        own = self.part(self.ring.place)
        return (
            own[...].astype(f32) + self.near[0].astype(f32) + self.near[1].astype(f32)
        ).astype(own.dtype)

    def finish(self):
        for way in range(6):
            self.copy(way).wait_send()


def greet(axes):
    barrier = pltpu.get_barrier_semaphore()
    total = 0
    for axis in axes:
        count = lax.axis_size(axis)
        me = lax.axis_index(axis)

        def signal(d, carried):
            pl.semaphore_signal(
                barrier,
                inc=1,
                device_id={axis: (me + d) % count},
                device_id_type=pl.DeviceIdType.MESH,
            )
            return carried

        lax.fori_loop(1, count, signal, 0)
        total += count - 1
    return lambda: pl.semaphore_wait(barrier, total)


def remote(source, target, send, recv, device):
    return pltpu.make_async_remote_copy(
        src_ref=source,
        dst_ref=target,
        send_sem=send,
        recv_sem=recv,
        device_id=device,
        device_id_type=pl.DeviceIdType.MESH,
    )


def each(low, high, body):
    def step(i, carried):
        body(i)
        return carried

    lax.fori_loop(low, high, step, 0)


class Exchange:
    def __init__(self, source, box, send, recv):
        self.source, self.box, self.send, self.recv = source, box, send, recv
        self.me, self.count = lax.axis_index("exp"), lax.axis_size("exp")

    def copy(self, other, slot):
        return remote(
            self.source.at[other],
            self.box.at[slot],
            self.send.at[other],
            self.recv.at[slot],
            {"exp": other},
        )

    def start(self):
        self.box[self.me] = self.source[self.me]
        half = self.count // 2

        def one(d):
            self.copy((self.me + half + d) % self.count, self.me).start()
            self.copy((self.me + half - d) % self.count, self.me).start()

        self.copy((self.me + half) % self.count, self.me).start()
        each(1, half, one)

    def wait(self):
        def one(d):
            other = (self.me + d) % self.count
            self.copy(other, other).wait_recv()

        each(1, self.count, one)

    def finish(self):
        each(1, self.count, lambda d: self.copy((self.me + d) % self.count, self.me).wait_send())


class Spread:
    def __init__(self, source, box, send, recv):
        self.source, self.box, self.send, self.recv = source, box, send, recv
        self.me = lax.axis_index("ctx")

    def copy(self, other, slot):
        return remote(
            self.source,
            self.box.at[slot],
            self.send.at[other],
            self.recv.at[slot],
            {"ctx": other},
        )

    def start(self, low, high):
        each(low, high, lambda other: self.copy(other, self.me).start())

    def wait_one(self, other):
        self.copy(other, other).wait_recv()

    def finish(self, low, high):
        each(low, high, lambda other: self.copy(other, self.me).wait_send())


def regroup(quarter, rows, slots, transposed):
    size = (rows * 4, rows) if transposed else (rows, rows * 4)
    row = lax.broadcasted_iota(jnp.int32, size, 1 if transposed else 0)
    slab = lax.broadcasted_iota(jnp.int32, size, 0 if transposed else 1)
    place = (row // slots) * (4 * slots) + quarter * slots + row % slots
    return jnp.where(slab == place, 1.0, 0.0).astype(jnp.bfloat16)


def quarters(value):
    step = value.shape[-1] // 4
    return jnp.concatenate([value[:, q * step : (q + 1) * step] for q in range(4)], axis=0)


def whole(value):
    step = value.shape[0] // 4
    return jnp.concatenate([value[q * step : (q + 1) * step] for q in range(4)], axis=1)


def as_column(row):
    count = row.shape[1]
    line = lax.broadcasted_iota(jnp.int32, (count, count), 0)
    column = lax.broadcasted_iota(jnp.int32, (count, count), 1)
    return jnp.sum(jnp.where(line == column, row, 0.0), axis=1, keepdims=True)


def make_places(ids_ref, place_ref, placet_ref, experts, slots, tokens):
    f32, i32 = jnp.float32, jnp.int32
    iota = lax.broadcasted_iota
    ids = [as_column(ids_ref[k : k + 1, :].astype(f32)) for k in (0, 1)]
    names = iota(i32, (tokens, experts), 1).astype(f32)
    onehot = [jnp.where(names == c, 1.0, 0.0) for c in ids]
    earlier = iota(i32, (tokens, tokens), 0) > iota(i32, (tokens, tokens), 1)
    before = jnp.dot(
        jnp.where(earlier, 1.0, 0.0).astype(jnp.bfloat16),
        (onehot[0] + onehot[1]).astype(jnp.bfloat16),
        preferred_element_type=f32,
    )
    slab = 4 * slots

    def codes(size, axis):
        row = iota(i32, size, axis)
        return ((row // slab) * slots + row % slots).astype(f32), (row % slab) // slots

    wide = 4 * experts * slots
    for k in (0, 1):
        target = ids[k] * slots + jnp.sum(before * onehot[k], axis=1, keepdims=True)
        place = iota(i32, (tokens, 4 * tokens), 1) % tokens
        own = place == iota(i32, (tokens, 4 * tokens), 0)
        target_row = jnp.sum(jnp.where(own, target, 0.0), axis=0, keepdims=True)
        code, quarter = codes((wide, 4 * tokens), 0)
        same = quarter == iota(i32, (wide, 4 * tokens), 1) // tokens
        place_ref[k] = jnp.where(
            jnp.logical_and(same, code == target_row), 1.0, 0.0
        ).astype(place_ref.dtype)
        code, quarter = codes((4 * tokens, wide), 1)
        same = quarter == iota(i32, (4 * tokens, wide), 0) // tokens
        target_column = jnp.concatenate([target] * 4, axis=0)
        placet_ref[k] = jnp.where(
            jnp.logical_and(same, code == target_column), 1.0, 0.0
        ).astype(placet_ref.dtype)


def spread_lanes(source_ref, target_ref):
    states, count = source_ref.shape

    def some(i, carried):
        for part in range(count // LANES):
            lanes = source_ref[:, part * LANES : (part + 1) * LANES]
            turned = pltpu.roll(lanes, (LANES - i * GROUP) % LANES, 1)
            for j in range(GROUP):
                target_ref[part * LANES + i * GROUP + j] = jnp.broadcast_to(
                    turned[:, j : j + 1], (states, LANES)
                )
        return carried

    lax.fori_loop(0, LANES // GROUP, some, 0)


def layer_kernel(
    delta_ref,
    u_ref,
    z_ref,
    b_ref,
    c_ref,
    plain_rate_ref,
    skip_ref,
    wout_hbm,
    resid_ref,
    gain_ref,
    ids_ref,
    weight_ref,
    wg_hbm,
    wu_hbm,
    wd_hbm,
    dout_ref,
    final_ref,
    gresid_ref,
    gradu_ref,
    brep_ref,
    crep_ref,
    rate_ref,
    wout_ref,
    wg_ref,
    wu_ref,
    wd_ref,
    weight_sem,
    place_ref,
    placet_ref,
    group_ref,
    groupt_ref,
    drive,
    y,
    gated,
    end16,
    back16,
    sums,
    end_box,
    sum_box,
    back_box,
    state_send,
    state_recv,
    mixed,
    pair_box,
    pair_send,
    pair_recv,
    mix_box,
    mix_send,
    mix_recv,
    slabs,
    boxes,
    slab_send,
    slab_recv,
    stream,
    segment,
    seg_send,
    seg_recv,
    twin_send,
    twin_recv,
    held,
    parts,
    far,
    near,
    own2,
    far2,
    near2,
    send,
    recv,
):
    f32 = jnp.float32
    bf16 = jnp.bfloat16
    ring_x, ring_y = Ring(True), Ring(False)
    first = (ring_x, ring_y)
    second = (ring_y, ring_x)
    rows, width = held.shape[-2], held.shape[-1]
    seg_rows, channels = delta_ref.shape
    ctx, ctx_count = lax.axis_index("ctx"), lax.axis_size("ctx")
    exp, exp_count = lax.axis_index("exp"), lax.axis_size("exp")
    z, core = exp // 2, exp % 2
    z_count = exp_count // 2
    sibling = {"exp": z * 2 + 1 - core}
    slots = 2 * rows // exp_count
    my_rows = resid_ref.shape[0]
    slab_rows = slabs.shape[2]
    slab_width = slabs.shape[3]
    COT, ROW, GRAD, OUT = range(4)
    moves = [Exchange(slabs.at[i], boxes.at[i], slab_send.at[i], slab_recv.at[i]) for i in range(4)]
    ends = Spread(end16, end_box, state_send.at[0], state_recv.at[0])
    totals = Spread(sums, sum_box, state_send.at[1], state_recv.at[1])
    backs = Spread(back16, back_box, state_send.at[2], state_recv.at[2])

    def to_slabs(kind, value):
        slabs[kind] = value.astype(bf16).reshape(exp_count, slab_rows, slab_width)

    def dispatched(kind):
        flat = boxes[kind].reshape(exp_count * slab_rows, slab_width)
        return [
            jnp.dot(
                group_ref[q], flat, preferred_element_type=f32
            ).astype(bf16)
            for q in range(4)
        ]

    def give_back(kind, read):
        total = None
        for q in range(4):
            tile = slice(q * slab_width, (q + 1) * slab_width)
            term = jnp.dot(
                groupt_ref[q], read(tile), preferred_element_type=f32
            )
            total = term if total is None else total + term
        to_slabs(kind, total)

    def gather(array, half, phase):
        if phase == 0:
            block = lambda i: held.at[array, half, second[half].place, i]
            ring, pieces = first[half], 1
        else:
            block = lambda i: held.at[array, half, i]
            ring, pieces = second[half], SIDE
        return Gather(ring, block, pieces, send.at[array, half, phase], recv.at[array, half, phase])

    near_gathers = [[gather(a, h, 0) for h in (0, 1)] for a in (0, 1)]
    far_gathers = [[gather(a, h, 1) for h in (0, 1)] for a in (0, 1)]

    def take_in(array, kind):
        for q, value in enumerate(dispatched(kind)):
            tile = slice(q * slab_width, (q + 1) * slab_width)
            for half in (0, 1):
                held[array, half, second[half].place, first[half].place, :, tile] = value[
                    half * rows : (half + 1) * rows
                ]
        for g in near_gathers[array]:
            g.start()
        for half in (0, 1):
            far_gathers[array][half].start(first[half].place)

    def spread_out(array):
        pairs = list(zip(near_gathers[array], far_gathers[array]))
        for g, h in pairs:
            g.before()
            g.after()
        for g, h in pairs:
            h.start(g.ring.before)
            h.start(g.ring.after)
        for g, h in pairs:
            g.across()
            h.start(g.ring.across)

    def reduces(array, phase):
        out = []
        for half in (0, 1):
            if phase == 0:
                part = functools.partial(lambda h, i: parts.at[array, h, i], half)
                ring, inbox = second[half], (far.at[array, half], near.at[array, half])
            else:
                part = functools.partial(lambda h, i: own2.at[array, h, i], half)
                ring, inbox = first[half], (far2.at[array, half], near2.at[array, half])
            out.append(
                Reduce(
                    ring,
                    part,
                    *inbox,
                    send.at[array, half, 2 + phase],
                    recv.at[array, half, 2 + phase],
                )
            )
        return out

    def decay_of(line, tile):
        return jnp.exp2(line[0] * rate_ref[:, tile])

    states = rate_ref.shape[0]

    def joined(box, low_first):
        tiles = tiles_of(channels)

        def one(i, carried):
            gap, held_state = carried
            other = ctx - 1 - i if low_first else ctx + 1 + i
            (ends if low_first else backs).wait_one(other)
            totals.wait_one(other)
            made = tuple(
                h
                + jnp.exp2(gap[:, tile] * rate_ref[:, tile]) * box[other, :, tile].astype(f32)
                for tile, h in zip(tiles, held_state)
            )
            return gap + sum_box[other], made

        count = ctx if low_first else ctx_count - 1 - ctx
        zero = tuple(jnp.zeros((states, LANES), f32) for _ in tiles)
        return lax.fori_loop(0, count, one, (jnp.zeros((1, channels), f32), zero))[1]

    fetches = [
        pltpu.make_async_copy(source, target, weight_sem.at[i])
        for i, (source, target) in enumerate(
            ((wout_hbm, wout_ref), (wd_hbm, wd_ref), (wg_hbm, wg_ref), (wu_hbm, wu_ref))
        )
    ]
    arrived = greet(("ctx", "exp"))
    for f in fetches:
        f.start()
    sums[...] = jnp.sum(delta_ref[...], axis=0, keepdims=True)
    rate_ref[...] = plain_rate_ref[...] * (-math.log2(math.e))
    make_places(ids_ref, place_ref, placet_ref, exp_count, slots, my_rows)
    columns = [as_column(weight_ref[k : k + 1, :]) for k in (0, 1)]
    d_out = dout_ref[...].astype(f32)
    to_slabs(
        COT,
        sum(
            jnp.dot(
                place_ref[k],
                quarters((columns[k] * d_out).astype(bf16)),
                preferred_element_type=f32,
            )
            for k in (0, 1)
        ),
    )
    spread_lanes(b_ref, brep_ref)
    drive[...] = delta_ref[...] * u_ref[...].astype(f32)
    arrived()
    totals.start(0, ctx)
    totals.start(ctx + 1, ctx_count)
    moves[COT].start()

    def end_step(t, tile, line, h):
        return decay_of(line, tile) * h + brep_ref[t] * line[1], None

    done = scan_tokens(seg_rows, channels, (delta_ref, drive), end_step, zero_state(rate_ref))
    for tile, h in zip(tiles_of(channels), done):
        end16[:, tile] = h.astype(bf16)
    ends.start(ctx + 1, ctx_count)
    spread_lanes(c_ref, crep_ref)
    for q in range(4):
        group_ref[q] = regroup(q, 2 * rows, slots, False)
    moves[COT].wait()
    take_in(1, COT)

    def out_step(t, tile, line, h):
        new = decay_of(line, tile) * h + brep_ref[t] * line[1]
        return new, jnp.sum(crep_ref[t] * new, axis=0, keepdims=True)

    scan_tokens(seg_rows, channels, (delta_ref, drive), out_step, joined(end_box, True), y)
    gated[...] = (
        (y[...] + skip_ref[...] * u_ref[...].astype(f32)) * silu(z_ref[...].astype(f32))
    ).astype(bf16)
    step = 512
    fetches[0].wait()
    for n in range(width // step):
        tile = slice(n * step, (n + 1) * step)
        value = (
            jnp.dot(gated[...], wout_ref[:, tile], preferred_element_type=f32)
            .astype(bf16)
            .reshape(z_count, 2, my_rows, step)
        )
        for k in (0, 1):
            mixed[k, :, :, tile] = value[:, k]
    RIGHT, LEFT = 0, 1
    hops = z_count // 2
    middle = width // 2
    beside = [
        {"exp": ((z + 1) % z_count) * 2 + core},
        {"exp": ((z + z_count - 1) % z_count) * 2 + core},
    ]

    def at_distance(way, far_by):
        return (z + far_by) % z_count if way == RIGHT else (z + z_count - far_by) % z_count

    def side(ref, lane):
        return ref.at[:, pl.ds(lane * middle, middle)]

    def pair(j):
        return remote(
            mixed.at[1 - core, j], pair_box.at[j], pair_send.at[j], pair_recv.at[j], sibling
        )

    order = [(RIGHT, hops)] + [(w, d) for d in range(hops - 1, 0, -1) for w in (RIGHT, LEFT)]
    order = [at_distance(w, d) for w, d in order] + [z]
    for j in order:
        pair(j).start()

    def paired(j):
        pair(j).wait_recv()
        add_into(mixed.at[core, j], pair_box.at[j])

    def mix(way, hop, lane):
        return remote(
            side(mixed.at[core, at_distance(way, hops - hop)], lane),
            side(mix_box.at[way, hop], lane),
            mix_send.at[way, hop, lane],
            mix_recv.at[way, hop, lane],
            beside[way],
        )

    def mix_on(way, hop, lane):
        mix(way, hop - 1, lane).wait_recv()
        add_into(
            side(mixed.at[core, at_distance(way, hops - hop)], lane),
            side(mix_box.at[way, hop - 1], lane),
        )
        mix(way, hop, lane).start()

    paired(order[0])
    for way in (RIGHT, LEFT):
        mix(way, 0, way).start()
    for way in (RIGHT, LEFT):
        paired(order[1 + way])
        mix(way, 1, 1 - way).start()
    for j in order[3:]:
        paired(j)
    for hop in range(1, hops):
        for way in (RIGHT, LEFT):
            mix_on(way, hop, way)
        if hop < hops - 1:
            for way in (RIGHT, LEFT):
                mix_on(way, hop + 1, 1 - way)
        if hop == 1:
            spread_out(1)
    for way in (RIGHT, LEFT):
        for lane in (0, 1):
            mix(way, hops - 1, lane).wait_recv()
    stream[...] = (
        resid_ref[...].astype(f32)
        + mixed[core, z].astype(f32)
        + mix_box[RIGHT, hops - 1].astype(f32)
        + mix_box[LEFT, hops - 1].astype(f32)
    )
    flow = stream[...]
    inverse = lax.rsqrt(jnp.mean(flow * flow, axis=-1, keepdims=True) + 1e-05)
    normed = (flow * inverse * gain_ref[...]).astype(bf16)
    spread = place_ref[0] + place_ref[1]
    to_slabs(ROW, jnp.dot(spread, quarters(normed), preferred_element_type=f32))
    moves[ROW].start()
    for q in range(4):
        groupt_ref[q] = regroup(q, 2 * rows, slots, True)
    for g in far_gathers[1]:
        g.before()
        g.after()
    moves[ROW].wait()
    take_in(0, ROW)
    spread_out(0)

    for f in fetches[1:]:
        f.wait()
    both = SIDE * rows

    def group(k, carried):
        @pl.when(k == 0)
        def _():
            for g in far_gathers[1]:
                g.across()

        @pl.when(k == 1)
        def _():
            for g in far_gathers[0]:
                g.before()
                g.after()

        @pl.when(k == 3)
        def _():
            for g in far_gathers[0]:
                g.across()
            for r in reduces(1, 0):
                r.direct()

        shift = jnp.where(k == 0, 0, jnp.where(k == 1, SIDE - 1, jnp.where(k == 2, 1, 2)))
        places = [(second[h].place + shift) % SIDE for h in (0, 1)]

        def taken(array):
            return jnp.concatenate(
                [held[array, h, places[h]].reshape(both, width) for h in (0, 1)], axis=0
            )

        def put(array, tile, value):
            value = value.astype(bf16)
            for h in (0, 1):
                parts[array, h, places[h], :, :, tile] = value[
                    h * both : (h + 1) * both
                ].reshape(SIDE, rows, -1)

        x = taken(0)
        gate = jnp.dot(x, wg_ref[...], preferred_element_type=f32)
        up = jnp.dot(x, wu_ref[...], preferred_element_type=f32)
        hidden_grad = contract_last(taken(1), wd_ref[...])
        sigma = 1.0 / (1.0 + jnp.exp(-gate))
        active = gate * sigma
        hidden = (active * up).astype(bf16)
        gate_grad = (hidden_grad * up * sigma * (1.0 + gate * (1.0 - sigma))).astype(bf16)
        up_grad = (hidden_grad * active).astype(bf16)
        for n in range(width // step):
            tile = slice(n * step, (n + 1) * step)
            put(
                1,
                tile,
                contract_last(gate_grad, wg_ref[tile, :]) + contract_last(up_grad, wu_ref[tile, :]),
            )

        @pl.when(k == 3)
        def _():
            for r in reduces(1, 0):
                r.start()

        for n in range(width // step):
            tile = slice(n * step, (n + 1) * step)
            put(0, tile, jnp.dot(hidden, wd_ref[:, tile], preferred_element_type=f32))
        return carried

    lax.fori_loop(0, SIDE, group, 0)
    grads, outs = reduces(1, 0), reduces(0, 0)
    grads2, outs2 = reduces(1, 1), reduces(0, 1)
    for r in grads:
        r.middle()
    for half in (0, 1):
        own2[1, half] = grads[half].total()
        grads2[half].start()
        grads2[half].direct()
    for r in grads2:
        r.middle()
    for r in outs:
        r.start()
        r.direct()
    sent = [r.total() for r in grads2]
    give_back(GRAD, lambda tile: jnp.concatenate([v[:, tile] for v in sent], axis=0))
    moves[GRAD].start()
    for r in outs:
        r.middle()
    moves[GRAD].wait()

    def combined(kind, matrix):
        flat = boxes[kind].reshape(exp_count * slab_rows, slab_width)
        return whole(jnp.dot(matrix, flat, preferred_element_type=f32))

    scaled = combined(GRAD, placet_ref[0] + placet_ref[1]) * gain_ref[...]
    flow = stream[...]
    inverse = lax.rsqrt(jnp.mean(flow * flow, axis=-1, keepdims=True) + 1e-05)
    project = jnp.mean(scaled * flow, axis=-1, keepdims=True)
    grad_rows = (
        dout_ref[...].astype(f32) + inverse * (scaled - flow * inverse * inverse * project)
    ).astype(bf16)
    gresid_ref[...] = grad_rows
    segment[exp] = grad_rows

    def seg(way, hop, lane, came=False):
        block = segment.at[at_distance(1 - way, hop + (1 if came else 0)) * 2 + core]
        block = side(block, lane)
        return remote(
            block, block, seg_send.at[way, hop, lane], seg_recv.at[way, hop, lane], beside[way]
        )

    def twin(slot):
        return remote(
            segment.at[slot],
            segment.at[slot],
            twin_send.at[slot // 2],
            twin_recv.at[slot // 2],
            sibling,
        )

    for lane in (0, 1):
        for way in (RIGHT, LEFT):
            seg(way, 0, lane if way == LEFT else 1 - lane).start()
    twin(exp).start()
    for hop in range(1, hops):
        for lane in (0, 1):
            for way in (RIGHT, LEFT):
                now = lane if way == LEFT else 1 - lane
                seg(way, hop - 1, now, True).wait_recv()
                if hop < hops - 1 or now == way:
                    seg(way, hop, now).start()
        for way in (RIGHT, LEFT):
            twin(at_distance(1 - way, hop) * 2 + core).start()
    for half in (0, 1):
        own2[0, half] = outs[half].total()
        outs2[half].start()
        outs2[half].direct()
    for way in (RIGHT, LEFT):
        seg(way, hops - 1, way, True).wait_recv()
    twin(at_distance(RIGHT, hops) * 2 + core).start()
    each(0, z_count, lambda i: twin(i * 2 + 1 - core).wait_recv())
    grad = drive
    grad[...] = contract_last(
        segment[...].reshape(seg_rows, width), wout_ref[...]
    ) * silu(z_ref[...].astype(f32))

    for r in outs2:
        r.middle()

    def back_end_step(t, tile, line, h):
        return decay_of(line, tile) * (h + crep_ref[t] * line[1]), None

    done = scan_tokens(
        seg_rows, channels, (delta_ref, grad), back_end_step, zero_state(rate_ref), backward=True
    )
    for tile, h in zip(tiles_of(channels), done):
        back16[:, tile] = h.astype(bf16)
    backs.start(0, ctx)
    sent = [r.total() for r in outs2]
    give_back(OUT, lambda tile: jnp.concatenate([v[:, tile] for v in sent], axis=0))
    moves[OUT].start()

    def back_step(t, tile, line, h):
        new = h + crep_ref[t] * line[1]
        return decay_of(line, tile) * new, jnp.sum(brep_ref[t] * new, axis=0, keepdims=True)

    scan_tokens(
        seg_rows,
        channels,
        (delta_ref, grad),
        back_step,
        joined(back_box, False),
        y,
        backward=True,
    )
    gradu_ref[...] = (delta_ref[...] * y[...] + skip_ref[...] * grad[...]).astype(bf16)
    moves[OUT].wait()
    final_ref[...] = (
        stream[...]
        + columns[0] * combined(OUT, placet_ref[0])
        + columns[1] * combined(OUT, placet_ref[1])
    ).astype(bf16)

    for array in (0, 1):
        for g in near_gathers[array] + far_gathers[array]:
            g.finish()
    for r in grads + outs + grads2 + outs2:
        r.finish()
    for m in moves:
        m.finish()
    each(0, z_count, lambda j: pair(j).wait_send())
    totals.finish(0, ctx)
    totals.finish(ctx + 1, ctx_count)
    ends.finish(ctx + 1, ctx_count)
    backs.finish(0, ctx)
    for way in (RIGHT, LEFT):
        for hop in range(hops):
            for lane in (0, 1):
                if hop > 0 or lane == way:
                    mix(way, hop, lane).wait_send()
                if hop < hops - 1 or lane == way:
                    seg(way, hop, lane).wait_send()
    each(0, z_count, lambda i: twin(i * 2 + core).wait_send())


def settle_kernel(*refs):
    half = len(refs) // 2
    for source, target in zip(refs[:half], refs[half:]):
        target[...] = source[...]


def settle(values):
    return pl.pallas_call(
        settle_kernel,
        out_shape=[jax.ShapeDtypeStruct(v.shape, v.dtype) for v in values],
        in_specs=[VMEM] * len(values),
        out_specs=[VMEM] * len(values),
    )(*values)


def layer(args, exp_count, ctx_count):
    delta, rate, resid = args[0], args[5], args[8]
    seg_rows, channels = delta.shape
    states = rate.shape[0]
    my_rows, width = resid.shape
    bf16, f32 = jnp.bfloat16, jnp.float32
    slots = 4 * my_rows // exp_count
    half = exp_count * slots // 2
    vm, dma = pltpu.VMEM, pltpu.SemaphoreType.DMA
    full = vm((2, 2, SIDE, SIDE, half, width), bf16)
    plane = vm((seg_rows, channels), f32)
    slab = vm((4, exp_count, 4 * slots, width // 4), bf16)
    state_box = vm((ctx_count, states, channels), bf16)
    shape = jax.ShapeDtypeStruct
    return pl.pallas_call(
        layer_kernel,
        out_shape=[
            shape((my_rows, width), bf16),
            shape((my_rows, width), bf16),
            shape((seg_rows, channels), bf16),
        ],
        in_specs=[
            pl.BlockSpec(memory_space=pl.ANY) if i in (7, 12, 13, 14) else VMEM
            for i in range(len(args))
        ],
        out_specs=[VMEM] * 3,
        scratch_shapes=[
            vm((seg_rows, states, LANES), f32),
            vm((seg_rows, states, LANES), f32),
            vm((states, channels), f32),
            *[vm(args[i].shape, bf16) for i in (7, 12, 13, 14)],
            dma((4,)),
            vm((2, 4 * exp_count * slots, 4 * my_rows), bf16),
            vm((2, 4 * my_rows, 4 * exp_count * slots), bf16),
            vm((4, exp_count * slots, 4 * exp_count * slots), bf16),
            vm((4, 4 * exp_count * slots, exp_count * slots), bf16),
            plane,
            plane,
            vm((seg_rows, channels), bf16),
            vm((states, channels), bf16),
            vm((states, channels), bf16),
            vm((1, channels), f32),
            state_box,
            vm((ctx_count, 1, channels), f32),
            state_box,
            dma((3, ctx_count)),
            dma((3, ctx_count)),
            vm((2, exp_count // 2, my_rows, width), bf16),
            vm((exp_count // 2, my_rows, width), bf16),
            dma((exp_count // 2,)),
            dma((exp_count // 2,)),
            vm((2, exp_count // 4, my_rows, width), bf16),
            dma((2, exp_count // 4, 2)),
            dma((2, exp_count // 4, 2)),
            slab,
            slab,
            dma((4, exp_count)),
            dma((4, exp_count)),
            vm((my_rows, width), f32),
            vm((exp_count, my_rows, width), bf16),
            dma((2, exp_count // 4, 2)),
            dma((2, exp_count // 4, 2)),
            dma((exp_count // 2,)),
            dma((exp_count // 2,)),
            full,
            full,
            vm((2, 2, 2, SIDE // 2, half, width), bf16),
            vm((2, 2, 2, SIDE, half, width), bf16),
            vm((2, 2, SIDE, half, width), bf16),
            vm((2, 2, 2, half // 2, width), bf16),
            vm((2, 2, 2, half, width), bf16),
            dma((2, 2, 4, 2 + 2 * SIDE)),
            dma((2, 2, 4, 2 + 2 * SIDE)),
        ],
        compiler_params=pltpu.CompilerParams(
            vmem_limit_bytes=60 * 1024 * 1024, collective_id=1, has_side_effects=True
        ),
    )(*args)


def local(
    u_in,
    z_gate,
    delta,
    b_in,
    c_in,
    rate,
    skip,
    w_out,
    resid,
    gain,
    expert_ids,
    route_weights,
    w_gate,
    w_up,
    w_down,
    d_out,
):
    return tuple(
        settle(
            layer(
                (
                    delta,
                    u_in,
                    z_gate,
                    b_in.T,
                    c_in.T,
                    rate,
                    skip[None, :],
                    w_out,
                    resid,
                    gain[None, :],
                    expert_ids.T,
                    route_weights.T,
                    w_gate[0],
                    w_up[0],
                    w_down[0],
                    d_out,
                ),
                lax.axis_size("exp"),
                lax.axis_size("ctx"),
            )
        )
    )


def solution(mesh):
    return jax.shard_map(
        local,
        mesh=mesh,
        in_specs=(
            P("ctx", "exp"),
            P("ctx", "exp"),
            P("ctx", "exp"),
            P("ctx", None),
            P("ctx", None),
            P(None, "exp"),
            P("exp"),
            P("exp", None),
            P(("ctx", "exp"), None),
            P(),
            P(("ctx", "exp"), None),
            P(("ctx", "exp"), None),
            P("exp", None, "ctx"),
            P("exp", None, "ctx"),
            P("exp", "ctx", None),
            P(("ctx", "exp"), None),
        ),
        out_specs=(P(("ctx", "exp"), None), P(("ctx", "exp"), None), P("ctx", "exp")),
        check_vma=False,
    )
```
